32 devices in a mesh: conv: 2 (over x), seq: 8 (over z, y), head: 2 (over core).
Axes of the slice: x: 2, y: 2, z: 4, core: 2. Of those that a mesh axis runs over, the one named last changes fastest.
Arguments:
- queries: bfloat16 [3072, 2048], P(('conv', 'seq'), 'head'), parts along dimension 0, may hold values from -10 to 10, as said below
- key_states: bfloat16 [3072, 512], P(('conv', 'seq'), 'head'), parts along dimension 0, may hold values from -5 to 5, as said below
- value_states: bfloat16 [3072, 512], P(('conv', 'seq'), 'head'), parts along dimension 0, may hold values from -16 to 16
- out_weight: bfloat16 [2048, 4096], P('head'), may hold values from -0.125 to 0.125
- turn_lengths: int32 [32], P('conv'), parts along dimension 0, may hold values from 1 to 959, as said below
- block_flags: int32 [16, 8], P(('conv', 'seq')), parts along dimension 0, may hold values 0 or 1
Outputs:
- pooled: float32 [32, 4096], P(('conv', 'seq'), 'head'), parts along dimension 0
The draws below stay inside these ranges and needn't reach their ends.
There are 2 independent parts, one for each index of `conv`. The reference program is written for one: setup_inputs(seed, part) draws one part's arguments, and reference() takes and returns one part's arrays. A program takes and returns all parts, laid end to end along the dimension named above; an argument that names none is the same for every part. Nothing has to cross between parts.
Inputs may be any that keep to these rules, and one draw needn't show every extreme that they name: `queries`: every entry lies within the stated bounds. `key_states`: every entry lies within the stated bounds. `turn_lengths`: the lengths sum to 1536; turn 0 has one token and turn 1, the longest, has exactly 959 tokens.
All inputs are finite; a program needn't handle non-finite values. No bound on the sum of `block_flags` on one device may be relied on, other than what follows from the above.
Results may differ from the reference program's by a relative error of at most 0.0035.
Values may be sent and summed in bfloat16 or wider, within the bound.
No kernel may reach another device: no remote copies, remote signals or barrier semaphores. Data moves between devices by JAX's collectives and lax.ppermute only.
A program may use at most 128 MiB of HBM per device.

```python
import math
import jax
import jax.numpy as jnp
from jax import lax

D = 4096
HEADS = 16
KV_HEADS = 4
HD = 128
TOK_DEV = 192
TURN_DEV = 2
TOKENS = 1536
TURNS = 16
TURN_MOST = 959
NBLK = 8


def draw_queries(key, part):
    values_drawn = 2.5 * jax.random.normal(jax.random.fold_in(key, 1), (TOKENS, HEADS * HD), jnp.float32)
    return jnp.clip(values_drawn, -10.0, 10.0).astype(jnp.bfloat16)


def draw_key_states(key, part):
    values_drawn = jax.random.normal(jax.random.fold_in(key, 2), (TOKENS, KV_HEADS * HD), jnp.float32)
    return jnp.clip(values_drawn, -5.0, 5.0).astype(jnp.bfloat16)


def draw_turn_lengths(key, part):
    remain_tokens = TOKENS - TURN_MOST - (TURN_DEV - 1)
    remain_turns = TURNS - TURN_DEV
    picked = jax.random.permutation(jax.random.fold_in(key, 21), remain_tokens - 1)[:remain_turns - 1] + 1
    cuts = jnp.sort(picked.astype(jnp.int32))
    bounds = jnp.concatenate([jnp.zeros((1,), jnp.int32), cuts, jnp.full((1,), remain_tokens, jnp.int32)])
    rest = (bounds[1:] - bounds[:-1]).astype(jnp.int32)
    leading = jnp.concatenate([jnp.ones((TURN_DEV - 1,), jnp.int32), jnp.full((1,), TURN_MOST, jnp.int32)])
    return jnp.concatenate([leading, rest]).astype(jnp.int32)


def set_ends(values, own_key, smallest, largest):
    extent = values.shape
    spot = [jax.random.randint(jax.random.fold_in(own_key, axis), (), 0, extent[axis]) for axis in range(len(extent))]
    values = values.at[tuple(spot)].set(smallest)
    longest = extent.index(max(extent))
    spot[longest] = (spot[longest] + 1) % extent[longest]
    return values.at[tuple(spot)].set(largest)


def level_of(stream_key, shape, shards, least, largest):
    def one(position, parts):
        heights = jax.random.uniform(jax.random.fold_in(jax.random.fold_in(stream_key, 6), position), (parts,), jnp.float32, least / len(shards), largest / len(shards))
        return jnp.repeat(jnp.exp(heights), shape[position] // parts).reshape((-1,) + (1,) * (len(shape) - position - 1))

    gain = one(*shards[0])
    for cut in shards[1:]:
        gain = gain * one(*cut)
    return gain


def normal_values(own_key, shape, scale, reach, cuts=(), held_as=jnp.bfloat16):
    values = scale * jax.random.normal(own_key, shape, jnp.float32)
    if cuts:
        values = values * level_of(own_key, shape, cuts, -0.22, 0.18)
    return jnp.clip(values, -reach, reach).astype(held_as)


def setup_inputs(seed: int = 0, part: int = 0) -> dict:
    streams_of = jax.random.split(jax.random.key(seed), 7)
    part_keys = jax.random.split(jax.random.fold_in(streams_of[6], part), 7)
    queries = draw_queries(jax.random.fold_in(jax.random.fold_in(streams_of[6], part), 71), part)
    key_states = draw_key_states(jax.random.fold_in(jax.random.fold_in(streams_of[6], part), 71), part)
    value_states = normal_values(part_keys[2], (TOKENS, KV_HEADS * HD), 4.0, 16.0, ((0, 8), (1, 2)))
    out_weight = normal_values(streams_of[3], (HEADS * HD, D), (HEADS * HD) ** -0.5, 0.125, ((0, 2),))
    turn_lengths = draw_turn_lengths(jax.random.fold_in(jax.random.fold_in(streams_of[6], part), 71), part)
    block_flags = set_ends((jax.random.randint(part_keys[5], (NBLK, NBLK), 0, 4) < 3).astype(jnp.int32), jax.random.fold_in(part_keys[5], 1), 0, 1)
    return dict(queries=queries, key_states=key_states, value_states=value_states, out_weight=out_weight, turn_lengths=turn_lengths, block_flags=block_flags)


big_negative = -1e+30
log_two_e = 1.4426950408889634

def reference(queries, key_states, value_states, out_weight, turn_lengths, block_flags):
    repeat = HEADS // KV_HEADS
    factor = log_two_e / math.sqrt(HD)
    key_all = key_states.reshape(TOKENS, KV_HEADS, HD).astype(jnp.float32)
    value_all = value_states.reshape(TOKENS, KV_HEADS, HD).astype(jnp.float32)
    key_pos = jnp.arange(TOKENS, dtype=jnp.int32)
    key_block = key_pos // TOK_DEV
    q_block = math.gcd(TOKENS, 512)
    block_total = TOKENS // q_block

    def one_block(number):
        start = (number * q_block).astype(jnp.int32)
        query_rows = lax.dynamic_slice_in_dim(queries, start, q_block, 0)
        query_rows = query_rows.reshape(q_block, KV_HEADS, repeat, HD).astype(jnp.float32)
        query_pos = start + jnp.arange(q_block, dtype=jnp.int32)
        query_block = query_pos // TOK_DEV
        flag_table = block_flags[query_block][:, key_block]
        visible = (key_pos[None, :] <= query_pos[:, None]) & ((key_block[None, :] == query_block[:, None]) | (flag_table == 1))
        logit = jnp.einsum('qgrd,kgd->grqk', query_rows, key_all) * factor
        logit = jnp.where(visible[None, None], logit, big_negative)
        row_top = jnp.ceil(lax.optimization_barrier(jnp.max(logit, axis=-1)))
        weights = jnp.where(visible[None, None], jnp.exp2(logit - row_top[..., None]), 0.0)
        weight_sum = lax.optimization_barrier(jnp.sum(weights, axis=-1))
        rounded = lax.optimization_barrier(weights.astype(jnp.bfloat16)).astype(jnp.float32)
        output = jnp.einsum('grqk,kgd->grqd', rounded, value_all) / weight_sum[..., None]
        return output.transpose(2, 0, 1, 3).reshape(q_block, HEADS * HD).astype(jnp.bfloat16)
    blocks = lax.map(one_block, jnp.arange(block_total, dtype=jnp.int32))
    attended = blocks.reshape(TOKENS, HEADS * HD)
    projected = jnp.dot(attended, out_weight, preferred_element_type=jnp.float32)
    turn_ends = jnp.cumsum(turn_lengths).astype(jnp.int32)
    starts = turn_ends - turn_lengths
    member = (starts[:, None] <= key_pos[None, :]) & (key_pos[None, :] < turn_ends[:, None])
    turn_share = jnp.where(member, 1.0, 0.0).astype(jnp.float32) / turn_lengths[:, None].astype(jnp.float32)
    return jnp.dot(turn_share, projected, precision=lax.Precision.HIGHEST)
```

```python
import functools
import math

import jax
import jax.numpy as jnp
from jax import lax
from jax.experimental import pallas as pl
from jax.experimental.pallas import tpu as pltpu
from jax.sharding import PartitionSpec as P

HD = 128

big_negative = -1e30
log_two_e = 1.4426950408889634


def block_update(q_ref, k_ref, v_ref, top, total_sum, totals, groups, repeat, diagonal):
    q_rows = q_ref.shape[0]
    factor = log_two_e / math.sqrt(HD)
    for g in range(groups):
        grouped = jnp.concatenate(
            [q_ref[:, (g * repeat + r) * HD : (g * repeat + r + 1) * HD] for r in range(repeat)], axis=0
        )
        keys = k_ref[:, g * HD : (g + 1) * HD]
        values = v_ref[:, g * HD : (g + 1) * HD]
        logit = (
            lax.dot_general(
                keys, grouped, (((1,), (1,)), ((), ())), preferred_element_type=jnp.float32
            )
            * factor
        )
        if diagonal:
            key_pos = lax.broadcasted_iota(jnp.int32, logit.shape, 0)
            q_pos = lax.rem(lax.broadcasted_iota(jnp.int32, logit.shape, 1), q_rows)
            logit = jnp.where(key_pos <= q_pos, logit, big_negative)
        old_top = top[g]
        new_top = jnp.maximum(old_top, jnp.ceil(jnp.max(logit, axis=0, keepdims=True)))
        weights = jnp.exp2(logit - new_top)
        rescale = jnp.exp2(old_top - new_top)
        update = lax.dot_general(
            values,
            weights.astype(jnp.bfloat16),
            (((0,), (0,)), ((), ())),
            preferred_element_type=jnp.float32,
        )
        top[g] = new_top
        total_sum[g] = total_sum[g] * rescale + jnp.sum(weights, axis=0, keepdims=True)
        totals[g] = totals[g] * rescale + update


def attend_kernel(blocks, groups, repeat, first, last, *refs):
    on_ref, q_ref = refs[:2]
    refs = refs[2:]
    keys, values = refs[:blocks], refs[blocks : 2 * blocks]
    refs = refs[2 * blocks :]
    if not first:
        before, refs = refs[:3], refs[3:]
    if last:
        member_ref, inverse_ref = refs[:2]
        refs = refs[2:]
        outs, state = refs[:-3], refs[-3:]
    else:
        state = refs
    if first:
        state[0][...] = jnp.full(state[0].shape, big_negative, jnp.float32)
        state[1][...] = jnp.zeros(state[1].shape, jnp.float32)
        state[2][...] = jnp.zeros(state[2].shape, jnp.float32)
    else:
        for mine, given in zip(state, before):
            mine[...] = given[...]
    for b in range(blocks):
        update = functools.partial(
            block_update, q_ref, keys[b], values[b], *state, groups, repeat, first and b == 0
        )
        if first and b == 0:
            update()
        else:
            pl.when(on_ref[b] == 1)(update)
    if last:
        chunks = len(outs)
        turns_here = outs[0].shape[0]
        for g in range(groups):
            attended = (state[2][g] / state[1][g]).astype(jnp.bfloat16)
            pooled = lax.dot_general(
                member_ref[...],
                attended,
                (((1,), (1,)), ((), ())),
                preferred_element_type=jnp.float32,
            )
            pooled = pooled * inverse_ref[...]
            for r in range(repeat):
                for c in range(chunks):
                    start = (r * chunks + c) * turns_here
                    outs[c][:, (g * repeat + r) * HD : (g * repeat + r + 1) * HD] = pooled[
                        start : start + turns_here
                    ]


def attend(on, queries, keys, values, state, pool, groups, chunks, turns_here):
    q_rows, width = queries.shape
    repeat = width // HD // groups
    blocks = len(keys)
    first, last = state is None, pool is not None
    columns = repeat * q_rows
    state_shapes = [(groups, 1, columns), (groups, 1, columns), (groups, HD, columns)]
    in_vmem = pl.BlockSpec(memory_space=pltpu.VMEM)
    args = [on, queries, *keys, *values]
    if not first:
        args += list(state)
    if last:
        args += list(pool)
        out_shape = [jax.ShapeDtypeStruct((turns_here, width), jnp.float32)] * chunks
        scratch = [pltpu.VMEM(shape, jnp.float32) for shape in state_shapes]
    else:
        out_shape = [jax.ShapeDtypeStruct(shape, jnp.float32) for shape in state_shapes]
        scratch = []
    return pl.pallas_call(
        functools.partial(attend_kernel, blocks, groups, repeat, first, last),
        out_shape=out_shape,
        in_specs=[pl.BlockSpec(memory_space=pltpu.SMEM)] + [in_vmem] * (len(args) - 1),
        out_specs=[in_vmem] * len(out_shape),
        scratch_shapes=scratch,
        compiler_params=pltpu.CompilerParams(vmem_limit_bytes=40 * 1024 * 1024),
        cost_estimate=pl.CostEstimate(
            flops=4 * blocks * q_rows * q_rows * width,
            bytes_accessed=blocks * q_rows * width,
            transcendentals=blocks * q_rows * q_rows * width // HD,
        ),
    )(*args)


def project_kernel(parts, *refs):
    rows, weight_ref, out_ref = refs[:parts], refs[parts], refs[parts + 1]
    total = rows[0][...]
    for other in rows[1:]:
        total = total + other[...]
    count = total.shape[0]
    high = total.astype(jnp.bfloat16)
    low = (total - high.astype(jnp.float32)).astype(jnp.bfloat16)
    both = jnp.concatenate([high, low], axis=0)
    product = jnp.dot(both, weight_ref[...], preferred_element_type=jnp.float32)
    out_ref[...] = product[:count] + product[count:]


def project(rows, weight):
    depth, columns = weight.shape
    count = rows[0].shape[0]
    step = math.gcd(columns, 512)
    return pl.pallas_call(
        functools.partial(project_kernel, len(rows)),
        out_shape=jax.ShapeDtypeStruct((count, columns), jnp.float32),
        grid=(columns // step,),
        in_specs=[pl.BlockSpec((count, depth), lambda c: (0, 0))] * len(rows)
        + [pl.BlockSpec((depth, step), lambda c: (0, c))],
        out_specs=pl.BlockSpec((count, step), lambda c: (0, c)),
        compiler_params=pltpu.CompilerParams(vmem_limit_bytes=40 * 1024 * 1024),
        cost_estimate=pl.CostEstimate(
            flops=2 * count * depth * columns, bytes_accessed=2 * depth * columns, transcendentals=0
        ),
    )(*rows, weight)


def on_device(count, queries, key_states, value_states, out_weight, turn_lengths, block_flags):
    across = 2 ** (int(math.log2(count)) // 2)
    down = count // across
    q_rows, width = queries.shape
    groups = key_states.shape[1] // HD
    repeat = width // HD // groups
    turns = turn_lengths.shape[0]
    turns_here = turns // count
    me = lax.axis_index("seq")
    my_z, my_y = me // across, me % across

    def up(rows):
        return lax.ppermute(rows, "seq", [(i, i + across) for i in range(count - across)])

    def over(rows, shift, later_only):
        pairs = []
        for z in range(down):
            for y in range(across):
                if later_only and y + shift >= across:
                    continue
                pairs.append((z * across + y, z * across + (y + shift) % across))
        return lax.ppermute(rows, "seq", pairs)

    def flag_of(owner, allowed):
        found = lax.dynamic_index_in_dim(
            block_flags[0], jnp.clip(owner, 0, count - 1), 0, keepdims=False
        )
        return jnp.where(allowed & (found == 1), 1, 0).astype(jnp.int32)

    chunk = (me + jnp.arange(count, dtype=jnp.int32)) % count
    turn_ends = jnp.cumsum(turn_lengths)
    starts = turn_ends - turn_lengths
    order = (chunk[:, None] * turns_here + jnp.arange(turns_here, dtype=jnp.int32)[None]).reshape(-1)
    own_pos = me * q_rows + jnp.arange(q_rows, dtype=jnp.int32)
    member = (starts[order][:, None] <= own_pos[None]) & (own_pos[None] < turn_ends[order][:, None])
    same = jnp.arange(repeat)[:, None] == jnp.arange(repeat)[None]
    member = (same[:, None, :, None] & member[None, :, None, :]).reshape(
        repeat * turns, repeat * q_rows
    )
    member = member.astype(jnp.bfloat16)
    inverse = 1.0 / turn_lengths[order].astype(jnp.float32)
    inverse = jnp.tile(inverse, repeat)[:, None]

    state = None
    keys, values = key_states, value_states
    for distance in range(down):
        if distance:
            keys, values = up(keys), up(values)
        all_keys, all_values = [keys], [values]
        on = [flag_of(me - distance * across, my_z >= distance)]
        for shift in range(1, across):
            all_keys.append(over(keys, shift, distance == 0))
            all_values.append(over(values, shift, distance == 0))
            from_y = (my_y - shift) % across
            owner = (my_z - distance) * across + from_y
            on.append(flag_of(owner, (owner >= 0) & (owner < me) & (my_z >= distance)))
        on = jnp.stack(on)
        pool = (member, inverse) if distance == down - 1 else None
        state = attend(on, queries, all_keys, all_values, state, pool, groups, count, turns_here)

    rows = [state[0]]
    for shift in range(1, count):
        pairs = [(i, (i + shift) % count) for i in range(count)]
        rows.append(lax.ppermute(state[shift], "seq", pairs))
    projected = project(rows, out_weight)
    half = projected.shape[1] // 2
    my_head = lax.axis_index("head")
    mine = lax.dynamic_slice_in_dim(projected, my_head * half, half, 1)
    other = lax.dynamic_slice_in_dim(projected, (1 - my_head) * half, half, 1)
    return mine + lax.ppermute(other, "head", [(0, 1), (1, 0)])


def solution(mesh):
    in_specs = (
        P(("conv", "seq"), "head"),
        P(("conv", "seq"), "head"),
        P(("conv", "seq"), "head"),
        P("head", None),
        P("conv"),
        P(("conv", "seq"), None),
    )
    out_specs = P(("conv", "seq"), "head")
    return jax.shard_map(
        functools.partial(on_device, mesh.shape["seq"]),
        mesh=mesh,
        in_specs=in_specs,
        out_specs=out_specs,
        check_vma=False,
    )
```

```python
import functools
import math

import jax
import jax.numpy as jnp
from jax import lax
from jax.experimental import pallas as pl
from jax.experimental.pallas import tpu as pltpu
from jax.sharding import PartitionSpec as P

HD = 128

big_negative = -1e30
log_two_e = 1.4426950408889634


def block_update(q_ref, kv_ref, state, groups, repeat, first):
    top, total_sum, totals = state
    q_rows = q_ref.shape[0]
    columns = repeat * q_rows
    chunk = math.gcd(columns, 256)
    factor = log_two_e / math.sqrt(HD)
    for g in range(groups):
        grouped = jnp.concatenate(
            [q_ref[:, (g * repeat + r) * HD : (g * repeat + r + 1) * HD] for r in range(repeat)], axis=0
        )
        keys = kv_ref[:, g * HD : (g + 1) * HD]
        values = kv_ref[:, (groups + g) * HD : (groups + g + 1) * HD]
        for c in range(columns // chunk):
            span = slice(c * chunk, (c + 1) * chunk)
            logit = lax.dot_general(
                keys, grouped[span], (((1,), (1,)), ((), ())), preferred_element_type=jnp.float32
            )
            if first:
                key_pos = lax.broadcasted_iota(jnp.int32, (q_rows, 1), 0)
                column = c * chunk + lax.broadcasted_iota(jnp.int32, (1, chunk), 1)
                logit = jnp.where(key_pos <= lax.rem(column, q_rows), logit, big_negative)
            block_top = jnp.ceil(jnp.max(logit, axis=0, keepdims=True) * factor)
            new_top = block_top if first else jnp.maximum(top[g, :, span], block_top)
            weights = jnp.exp2(logit * factor - new_top)
            block_sum = jnp.sum(weights, axis=0, keepdims=True)
            update = lax.dot_general(
                values,
                weights.astype(jnp.bfloat16),
                (((0,), (0,)), ((), ())),
                preferred_element_type=jnp.float32,
            )
            if first:
                total_sum[g, :, span] = block_sum
                totals[g, :, span] = update
            else:
                rescale = jnp.exp2(top[g, :, span] - new_top)
                total_sum[g, :, span] = total_sum[g, :, span] * rescale + block_sum
                totals[g, :, span] = totals[g, :, span] * rescale + update
            top[g, :, span] = new_top


def attend_kernel(owners_of, groups, repeat, first, last, me_ref, flags_ref, q_ref, *refs):
    count = flags_ref.shape[1]
    me = me_ref[0]
    owners = owners_of(me)
    blocks, refs = refs[: len(owners)], refs[len(owners) :]
    if not first:
        before, refs = refs[:3], refs[3:]
    if last:
        low_ref, high_ref, inverse_ref, weight_ref, out_ref = refs[:5]
        state = refs[5:]
    else:
        state = refs
    if not first:
        for mine, given in zip(state, before):
            mine[...] = given[...]
    for kv_ref, owner in zip(blocks, owners):
        update = functools.partial(block_update, q_ref, kv_ref, state, groups, repeat, first)
        if first:
            update()
        else:
            flag = flags_ref[0, jnp.clip(owner, 0, count - 1)]
            pl.when((owner >= 0) & (owner < me) & (flag == 1))(update)
    if last:
        turns = inverse_ref.shape[0] // repeat
        columns = low_ref.shape[0] // turns * q_ref.shape[0]
        column = lax.broadcasted_iota(jnp.int32, (repeat * turns, columns), 1)
        member = (column >= low_ref[...]) & (column < high_ref[...])
        member = jnp.where(member, 1.0, 0.0).astype(jnp.bfloat16)
        heads = []
        for g in range(groups):
            attended = (state[2][g] / state[1][g]).astype(jnp.bfloat16)
            pooled = lax.dot_general(
                member, attended, (((1,), (1,)), ((), ())), preferred_element_type=jnp.float32
            )
            pooled = pooled * inverse_ref[...]
            heads += [pooled[r * turns : (r + 1) * turns] for r in range(repeat)]
        pooled = jnp.concatenate(heads, axis=1)
        high = pooled.astype(jnp.bfloat16)
        low = (pooled - high.astype(jnp.float32)).astype(jnp.bfloat16)
        both = jnp.concatenate([high, low], axis=0)
        pieces, rows, half = out_ref.shape
        sides = weight_ref.shape[1] // half
        step = math.gcd(half, 512)
        for side in range(sides):
            for c in range(half // step):
                start = side * half + c * step
                product = jnp.dot(
                    both, weight_ref[:, start : start + step], preferred_element_type=jnp.float32
                )
                product = product[:turns] + product[turns:]
                for s in range(pieces // sides):
                    out_ref[s * sides + side, :, c * step : (c + 1) * step] = product[
                        s * rows : (s + 1) * rows
                    ]


def attend(owners_of, me, flags, queries, blocks, state, pool, groups, out_piece):
    q_rows, width = queries.shape
    repeat = width // HD // groups
    first, last = state is None, pool is not None
    columns = repeat * q_rows
    state_shapes = [(groups, 1, columns), (groups, 1, columns), (groups, HD, columns)]
    in_vmem = pl.BlockSpec(memory_space=pltpu.VMEM)
    in_smem = pl.BlockSpec(memory_space=pltpu.SMEM)
    args = [me, flags, queries, *blocks]
    if not first:
        args += list(state)
    if last:
        args += list(pool)
        out_shape = [jax.ShapeDtypeStruct(out_piece, jnp.float32)]
        scratch = [pltpu.VMEM(shape, jnp.float32) for shape in state_shapes]
    else:
        out_shape = [jax.ShapeDtypeStruct(shape, jnp.float32) for shape in state_shapes]
        scratch = []
    return pl.pallas_call(
        functools.partial(attend_kernel, owners_of, groups, repeat, first, last),
        out_shape=out_shape,
        in_specs=[in_smem] * 2 + [in_vmem] * (len(args) - 2),
        out_specs=[in_vmem] * len(out_shape),
        scratch_shapes=scratch,
        compiler_params=pltpu.CompilerParams(vmem_limit_bytes=(32 if last else 16) * 1024 * 1024),
        cost_estimate=pl.CostEstimate(
            flops=4 * len(blocks) * q_rows * q_rows * width,
            bytes_accessed=len(blocks) * q_rows * width,
            transcendentals=len(blocks) * q_rows * q_rows * width // HD,
        ),
    )(*args)


def on_device(count, queries, key_states, value_states, out_weight, turn_lengths, block_flags):
    across = 2 ** (int(math.log2(count)) // 2)
    down = count // across
    q_rows, width = queries.shape
    groups = key_states.shape[1] // HD
    repeat = width // HD // groups
    turns = turn_lengths.shape[0]
    me = lax.axis_index("seq")
    heads = lax.axis_size("head")

    def up(rows):
        return lax.ppermute(rows, "seq", [(i, i + across) for i in range(count - across)])

    def over(rows, shift, later_only):
        pairs = []
        for z in range(down):
            for y in range(across):
                if later_only and y + shift >= across:
                    continue
                pairs.append((z * across + y, z * across + (y + shift) % across))
        return lax.ppermute(rows, "seq", pairs)

    def owners_at(stage, index):
        z, y = index // across, lax.rem(index, across)
        owners = []
        if stage:
            row = (z - (stage - 1)) * across
            owners += [row + lax.rem(y - shift + across, across) for shift in range(1, across)]
        if stage < down:
            owners.append(index - stage * across)
        return owners

    turn_ends = jnp.cumsum(turn_lengths)
    starts = turn_ends - turn_lengths
    offset = (jnp.arange(repeat, dtype=jnp.int32) * q_rows)[:, None]
    low = (jnp.clip(starts - me * q_rows, 0, q_rows)[None] + offset).reshape(-1, 1)
    high = (jnp.clip(turn_ends - me * q_rows, 0, q_rows)[None] + offset).reshape(-1, 1)
    inverse = jnp.tile(1.0 / turn_lengths.astype(jnp.float32), repeat)[:, None]
    pool = (low, high, inverse, out_weight)
    out_piece = (count * heads, turns // count, out_weight.shape[1] // heads)

    me_array = me.astype(jnp.int32).reshape(1)
    state = None
    rows = jnp.concatenate([key_states, value_states], axis=1)
    shifted = []
    for stage in range(down + 1):
        blocks = list(shifted)
        if stage < down:
            blocks.append(rows)
        new_state = attend(
            functools.partial(owners_at, stage),
            me_array,
            block_flags,
            queries,
            blocks,
            state,
            pool if stage == down else None,
            groups,
            out_piece,
        )
        if stage < down:
            if stage < down - 1:
                following = up(rows)
            shifted = [over(rows, shift, stage == 0) for shift in range(1, across)]
            if stage < down - 1:
                following, *new_state = lax.optimization_barrier((following, *new_state))
                rows = following
            else:
                shifted[0], *new_state = lax.optimization_barrier((shifted[0], *new_state))
        state = new_state
    parts = lax.all_to_all(state[0], ("seq", "head"), split_axis=0, concat_axis=0, tiled=True)
    return jnp.sum(parts, axis=0)


def solution(mesh):
    in_specs = (
        P(("conv", "seq"), "head"),
        P(("conv", "seq"), "head"),
        P(("conv", "seq"), "head"),
        P("head", None),
        P("conv"),
        P(("conv", "seq"), None),
    )
    out_specs = P(("conv", "seq"), "head")
    return jax.shard_map(
        functools.partial(on_device, mesh.shape["seq"]),
        mesh=mesh,
        in_specs=in_specs,
        out_specs=out_specs,
        check_vma=False,
    )
```

```python
import functools
import math

import jax
import jax.numpy as jnp
from jax import lax
from jax.experimental import pallas as pl
from jax.experimental.pallas import tpu as pltpu
from jax.sharding import PartitionSpec as P

HD = 128

big_negative = -1e30
log_two_e = 1.4426950408889634

small_cost = pl.CostEstimate(flops=1024, bytes_accessed=1024, transcendentals=0)

in_vmem = pl.BlockSpec(memory_space=pltpu.VMEM)
in_smem = pl.BlockSpec(memory_space=pltpu.SMEM)
anywhere = pl.BlockSpec(memory_space=pl.ANY)


def pack_kernel(key_ref, value_ref, out_ref):
    width = key_ref.shape[1]
    out_ref[:, :width] = key_ref[...]
    out_ref[:, width:] = value_ref[...]


def pack(keys, values):
    rows, width = keys.shape
    return pl.pallas_call(
        pack_kernel,
        out_shape=jax.ShapeDtypeStruct((rows, 2 * width), keys.dtype),
        in_specs=[in_vmem] * 2,
        out_specs=in_vmem,
    )(keys, values)


def block_update(turned_ref, kv_ref, state, q_rows, first):
    top, total_sum, totals = state
    groups, _, columns = turned_ref.shape
    chunk = math.gcd(columns, 256)
    factor = log_two_e / math.sqrt(HD)
    for g in range(groups):
        keys = kv_ref[:, g * HD : (g + 1) * HD]
        values = kv_ref[:, (groups + g) * HD : (groups + g + 1) * HD].T
        for c in range(columns // chunk):
            span = slice(c * chunk, (c + 1) * chunk)
            logit = jnp.dot(keys, turned_ref[g, :, span], preferred_element_type=jnp.float32)
            if first:
                key_pos = lax.broadcasted_iota(jnp.int32, (q_rows, 1), 0)
                column = c * chunk + lax.broadcasted_iota(jnp.int32, (1, chunk), 1)
                logit = jnp.where(key_pos <= lax.rem(column, q_rows), logit, big_negative)
            block_top = jnp.ceil(jnp.max(logit, axis=0, keepdims=True) * factor)
            new_top = block_top if first else jnp.maximum(top[g, :, span], block_top)
            weights = jnp.exp2(logit * factor - new_top)
            block_sum = jnp.sum(weights, axis=0, keepdims=True)
            update = jnp.dot(
                values, weights.astype(jnp.bfloat16), preferred_element_type=jnp.float32
            )
            if first:
                total_sum[g, :, span] = block_sum
                totals[g, :, span] = update
            else:
                rescale = jnp.exp2(top[g, :, span] - new_top)
                total_sum[g, :, span] = total_sum[g, :, span] * rescale + block_sum
                totals[g, :, span] = totals[g, :, span] * rescale + update
            top[g, :, span] = new_top


def first_kernel(
    repeat, meta_ref, lengths_ref, q_ref, kv_ref, weight_ref, *outs_and_scratch
):
    turned_ref, member_ref, inverse_ref, weight_out, *state = outs_and_scratch[:-2]
    rows_ref, copied = outs_and_scratch[-2:]
    weight_copy = pltpu.make_async_copy(weight_ref, weight_out, copied)
    weight_copy.start()
    q_rows = q_ref.shape[0]
    groups = turned_ref.shape[0]
    for g in range(groups):
        for r in range(repeat):
            head = g * repeat + r
            turned_ref[g, :, r * q_rows : (r + 1) * q_rows] = q_ref[:, head * HD : (head + 1) * HD].T
    block_update(turned_ref, kv_ref, state, q_rows, True)

    turns = lengths_ref.shape[0]
    columns = repeat * q_rows
    column = lax.broadcasted_iota(jnp.int32, (1, columns), 1)
    position = lax.rem(column, q_rows) + meta_ref[0] * q_rows
    start = jnp.int32(0)
    for t in range(turns):
        length = lengths_ref[t]
        inside = (position >= start) & (position < start + length)
        rows_ref[t : t + 1, :] = jnp.where(inside, 1.0, 0.0)
        inverse_ref[t : t + 1, :] = 1.0 / jnp.full((1, HD), length, jnp.int32).astype(jnp.float32)
        start = start + length
    for r in range(repeat):
        mine = (column >= r * q_rows) & (column < (r + 1) * q_rows)
        member_ref[r * turns : (r + 1) * turns, :] = jnp.where(mine, rows_ref[...], 0.0).astype(
            jnp.bfloat16
        )
    weight_copy.wait()


def attend_first(meta, lengths, queries, rows, weight):
    q_rows, width = queries.shape
    groups = rows.shape[1] // 2 // HD
    repeat = width // HD // groups
    columns = repeat * q_rows
    turns = lengths.shape[0]
    f32, b16 = jnp.float32, jnp.bfloat16
    return pl.pallas_call(
        functools.partial(first_kernel, repeat),
        out_shape=[
            jax.ShapeDtypeStruct((groups, HD, columns), b16),
            jax.ShapeDtypeStruct((repeat * turns, columns), b16),
            jax.ShapeDtypeStruct((turns, HD), f32),
            jax.ShapeDtypeStruct(weight.shape, weight.dtype),
            jax.ShapeDtypeStruct((groups, 1, columns), f32),
            jax.ShapeDtypeStruct((groups, 1, columns), f32),
            jax.ShapeDtypeStruct((groups, HD, columns), f32),
        ],
        in_specs=[in_smem, in_smem, in_vmem, in_vmem, anywhere],
        out_specs=[in_vmem] * 7,
        scratch_shapes=[pltpu.VMEM((turns, columns), f32), pltpu.SemaphoreType.DMA(())],
        compiler_params=pltpu.CompilerParams(vmem_limit_bytes=44 * 1024 * 1024),
        cost_estimate=small_cost,
    )(meta, lengths, queries, rows, weight)


def next_kernel(owners_of, q_rows, last, meta_ref, turned_ref, *refs):
    count = meta_ref.shape[0] - 1
    me = meta_ref[0]
    owners = owners_of(me)
    blocks, refs = refs[: len(owners)], refs[len(owners) :]
    before, refs = refs[:3], refs[3:]
    if last:
        member_ref, inverse_ref, weight_ref, out_ref = refs[:4]
        state = refs[4:]
    else:
        state = refs
    for mine, given in zip(state, before):
        mine[...] = given[...]
    for kv_ref, owner in zip(blocks, owners):
        flag = meta_ref[1 + jnp.clip(owner, 0, count - 1)]
        update = functools.partial(block_update, turned_ref, kv_ref, state, q_rows, False)
        pl.when((owner >= 0) & (owner < me) & (flag == 1))(update)
    if last:
        turns = inverse_ref.shape[0]
        groups, _, columns = turned_ref.shape
        heads = []
        for g in range(groups):
            attended = (state[2][g] / state[1][g]).astype(jnp.bfloat16)
            pooled = lax.dot_general(
                member_ref[...],
                attended,
                (((1,), (1,)), ((), ())),
                preferred_element_type=jnp.float32,
            )
            for r in range(columns // q_rows):
                heads.append(pooled[r * turns : (r + 1) * turns] * inverse_ref[...])
        pooled = jnp.concatenate(heads, axis=1)
        high = pooled.astype(jnp.bfloat16)
        low = (pooled - high.astype(jnp.float32)).astype(jnp.bfloat16)
        both = jnp.concatenate([high, low], axis=0)
        pieces, rows, half = out_ref.shape
        sides = weight_ref.shape[1] // half
        step = math.gcd(half, 512)
        for side in range(sides):
            for c in range(half // step):
                start = side * half + c * step
                product = jnp.dot(
                    both, weight_ref[:, start : start + step], preferred_element_type=jnp.float32
                )
                product = (product[:turns] + product[turns:]).astype(out_ref.dtype)
                for s in range(pieces // sides):
                    out_ref[s * sides + side, :, c * step : (c + 1) * step] = product[
                        s * rows : (s + 1) * rows
                    ]


def attend_next(owners_of, q_rows, meta, turned, blocks, state, pool, out_piece):
    last = pool is not None
    groups, _, columns = turned.shape
    state_shapes = [(groups, 1, columns), (groups, 1, columns), (groups, HD, columns)]
    args = [meta, turned, *blocks, *state]
    if last:
        args += list(pool)
        out_shape = [jax.ShapeDtypeStruct(out_piece, jnp.bfloat16)]
        scratch = [pltpu.VMEM(shape, jnp.float32) for shape in state_shapes]
    else:
        out_shape = [jax.ShapeDtypeStruct(shape, jnp.float32) for shape in state_shapes]
        scratch = []
    return pl.pallas_call(
        functools.partial(next_kernel, owners_of, q_rows, last),
        out_shape=out_shape,
        in_specs=[in_smem] + [in_vmem] * (len(args) - 1),
        out_specs=[in_vmem] * len(out_shape),
        scratch_shapes=scratch,
        compiler_params=pltpu.CompilerParams(vmem_limit_bytes=(24 if last else 16) * 1024 * 1024),
        cost_estimate=small_cost,
    )(*args)


def on_device(count, queries, key_states, value_states, out_weight, turn_lengths, block_flags):
    across = 2 ** (int(math.log2(count)) // 2)
    down = count // across
    q_rows = queries.shape[0]
    turns = turn_lengths.shape[0]
    me = lax.axis_index("seq")
    heads = lax.axis_size("head")

    def up(rows, distance):
        step = distance * across
        return lax.ppermute(rows, "seq", [(i, i + step) for i in range(count - step)])

    def over(rows, shift, distance):
        pairs = []
        for z in range(distance, down):
            for y in range(across):
                if distance == 0 and y + shift >= across:
                    continue
                pairs.append((z * across + y, z * across + (y + shift) % across))
        return lax.ppermute(rows, "seq", pairs)

    def owners_at(stage, index):
        z, y = index // across, lax.rem(index, across)
        row = (z - (stage - 1)) * across
        owners = [row + lax.rem(y - shift + across, across) for shift in range(1, across)]
        if stage < down:
            owners.append(index - stage * across)
        return owners

    meta = jnp.concatenate([me.astype(jnp.int32)[None], block_flags[0]])
    rows = pack(key_states, value_states)
    below = [rows] + [up(rows, distance) for distance in range(1, down)]
    shifted = [over(rows, shift, 0) for shift in range(1, across)]
    turned, member, inverse, weight, *state = attend_first(
        meta, turn_lengths, queries, rows, out_weight
    )
    pool = (member, inverse, weight)
    out_piece = (count * heads, turns // count, out_weight.shape[1] // heads)
    for stage in range(1, down + 1):
        blocks = list(shifted)
        if stage < down:
            blocks.append(below[stage])
            ready, *state = lax.optimization_barrier((below[stage], *state))
            shifted = [over(ready, shift, stage) for shift in range(1, across)]
        state = attend_next(
            functools.partial(owners_at, stage),
            q_rows,
            meta,
            turned,
            blocks,
            state,
            pool if stage == down else None,
            out_piece,
        )
    parts = lax.all_to_all(state[0], ("seq", "head"), split_axis=0, concat_axis=0, tiled=True)
    return jnp.sum(parts.astype(jnp.float32), axis=0)


def solution(mesh):
    in_specs = (
        P(("conv", "seq"), "head"),
        P(("conv", "seq"), "head"),
        P(("conv", "seq"), "head"),
        P("head", None),
        P("conv"),
        P(("conv", "seq"), None),
    )
    out_specs = P(("conv", "seq"), "head")
    return jax.shard_map(
        functools.partial(on_device, mesh.shape["seq"]),
        mesh=mesh,
        in_specs=in_specs,
        out_specs=out_specs,
        check_vma=False,
    )
```

```python
import functools
import math

import jax
import jax.numpy as jnp
from jax import lax
from jax.experimental import pallas as pl
from jax.experimental.pallas import tpu as pltpu
from jax.sharding import PartitionSpec as P

HD = 128

big_negative = -1e30
log_two_e = 1.4426950408889634

big_limit = 44 * 1024 * 1024
small_cost = pl.CostEstimate(flops=1024, bytes_accessed=1024, transcendentals=0)

in_vmem = pl.BlockSpec(memory_space=pltpu.VMEM)
in_smem = pl.BlockSpec(memory_space=pltpu.SMEM)
anywhere = pl.BlockSpec(memory_space=pl.ANY)


def pack_kernel(key_ref, value_ref, out_ref):
    width = key_ref.shape[1]
    out_ref[:, :width] = key_ref[...]
    out_ref[:, width:] = value_ref[...]


def pack(keys, values):
    rows, width = keys.shape
    return pl.pallas_call(
        pack_kernel,
        out_shape=jax.ShapeDtypeStruct((rows, 2 * width), keys.dtype),
        in_specs=[in_vmem] * 2,
        out_specs=in_vmem,
    )(keys, values)


def stage_update(turned_ref, blocks, switches, state, q_rows, first):
    top, total_sum, totals = state
    groups, _, columns = turned_ref.shape
    factor = log_two_e / math.sqrt(HD)
    logits = [
        [
            jnp.dot(
                kv_ref[:, g * HD : (g + 1) * HD], turned_ref[g], preferred_element_type=jnp.float32
            )
            for kv_ref in blocks
        ]
        for g in range(groups)
    ]
    if first:
        key_pos = lax.broadcasted_iota(jnp.int32, (q_rows, 1), 0)
        column = lax.broadcasted_iota(jnp.int32, (1, columns), 1)
        visible = key_pos <= lax.rem(column, q_rows)
        logits = [[jnp.where(visible, logit, big_negative) for logit in mine] for mine in logits]
    for g in range(groups):
        new_top = None if first else top[g]
        for logit, switch in zip(logits[g], switches):
            block_top = jnp.ceil(jnp.max(logit, axis=0, keepdims=True) * factor)
            if first:
                new_top = block_top
            else:
                new_top = jnp.maximum(new_top, jnp.where(switch, block_top, big_negative))
        update, block_sum = None, None
        for kv_ref, logit, switch in zip(blocks, logits[g], switches):
            against = new_top if first else jnp.where(switch, new_top, -big_negative)
            weights = jnp.exp2(logit * factor - against)
            values = kv_ref[:, (groups + g) * HD : (groups + g + 1) * HD].T
            part = jnp.dot(values, weights.astype(jnp.bfloat16), preferred_element_type=jnp.float32)
            part_sum = jnp.sum(weights, axis=0, keepdims=True)
            update = part if update is None else update + part
            block_sum = part_sum if block_sum is None else block_sum + part_sum
        if not first:
            rescale = jnp.exp2(top[g] - new_top)
            block_sum = total_sum[g] * rescale + block_sum
            update = totals[g] * rescale + update
        top[g] = new_top
        total_sum[g] = block_sum
        totals[g] = update


def first_kernel(repeat, turns, meta_ref, q_ref, kv_ref, turned_ref, member_ref, inverse_ref, *rest):
    state, rows_ref = rest[:-1], rest[-1]
    q_rows = q_ref.shape[0]
    groups = turned_ref.shape[0]
    for g in range(groups):
        for r in range(repeat):
            head = g * repeat + r
            turned_ref[g, :, r * q_rows : (r + 1) * q_rows] = q_ref[:, head * HD : (head + 1) * HD].T
    stage_update(turned_ref, [kv_ref], [None], state, q_rows, True)

    columns = repeat * q_rows
    column = lax.broadcasted_iota(jnp.int32, (1, columns), 1)
    position = lax.rem(column, q_rows) + meta_ref[0] * q_rows
    start = jnp.int32(0)
    for t in range(turns):
        length = meta_ref[2 + t]
        inside = (position >= start) & (position < start + length)
        rows_ref[t : t + 1, :] = jnp.where(inside, 1.0, 0.0)
        inverse_ref[t : t + 1, :] = 1.0 / jnp.full((1, HD), length, jnp.int32).astype(jnp.float32)
        start = start + length
    for r in range(repeat):
        mine = (column >= r * q_rows) & (column < (r + 1) * q_rows)
        member_ref[r * turns : (r + 1) * turns, :] = jnp.where(mine, rows_ref[...], 0.0).astype(
            jnp.bfloat16
        )


def attend_first(meta, turns, queries, rows):
    q_rows, width = queries.shape
    groups = rows.shape[1] // 2 // HD
    repeat = width // HD // groups
    columns = repeat * q_rows
    f32, b16 = jnp.float32, jnp.bfloat16
    return pl.pallas_call(
        functools.partial(first_kernel, repeat, turns),
        out_shape=[
            jax.ShapeDtypeStruct((groups, HD, columns), b16),
            jax.ShapeDtypeStruct((repeat * turns, columns), b16),
            jax.ShapeDtypeStruct((turns, HD), f32),
            jax.ShapeDtypeStruct((groups, 1, columns), f32),
            jax.ShapeDtypeStruct((groups, 1, columns), f32),
            jax.ShapeDtypeStruct((groups, HD, columns), f32),
        ],
        in_specs=[in_smem, in_vmem, in_vmem],
        out_specs=[in_vmem] * 6,
        scratch_shapes=[pltpu.VMEM((turns, columns), f32)],
        compiler_params=pltpu.CompilerParams(vmem_limit_bytes=big_limit),
        cost_estimate=small_cost,
    )(meta, queries, rows)


def next_kernel(owners_of, turns, q_rows, held, with_weight, last, meta_ref, turned_ref, *refs):
    flags_at = 2 + turns
    count = meta_ref.shape[0] - flags_at
    me = meta_ref[0]
    owners = owners_of(me)
    blocks, refs = refs[: len(owners)], refs[len(owners) :]
    state, refs = refs[:3], refs[3 + held :]
    if with_weight:
        weight_ref, *outs, weight_out, token_ref, copied = refs
        weight_copy = pltpu.make_async_copy(weight_ref, weight_out, copied)
        weight_copy.start()
    elif last:
        member_ref, inverse_ref, out_ref = refs
    else:
        token_ref = refs[-1]
    if not last:
        token_ref[...] = jnp.zeros(token_ref.shape, jnp.float32)
    switches = [
        (owner >= 0) & (owner < me) & (meta_ref[flags_at + jnp.clip(owner, 0, count - 1)] == 1)
        for owner in owners
    ]

    @pl.when(functools.reduce(jnp.logical_or, switches))
    def _():
        stage_update(turned_ref, blocks, switches, state, q_rows, False)

    if with_weight:
        weight_copy.wait()
    if last:
        groups, _, columns = turned_ref.shape
        rows = out_ref.shape[1]
        for g in range(groups):
            attended = (state[2][g] / state[1][g]).astype(jnp.bfloat16)
            pooled = lax.dot_general(
                member_ref[...],
                attended,
                (((1,), (1,)), ((), ())),
                preferred_element_type=jnp.float32,
            )
            repeat = columns // q_rows
            for r in range(repeat):
                mean = pooled[r * turns : (r + 1) * turns] * inverse_ref[...]
                head = g * repeat + r
                for s in range(out_ref.shape[0]):
                    out_ref[s, :, head * HD : (head + 1) * HD] = mean[s * rows : (s + 1) * rows]


def attend_next(owners_of, turns, q_rows, meta, turned, blocks, state, weight, pool, held, out_piece):
    with_weight, last = weight is not None, pool is not None
    args = [meta, turned, *blocks, *state]
    state_at = 2 + len(blocks)
    scratch, aliases = [], {}
    args += held
    in_specs = [in_smem] + [in_vmem] * (state_at + 2) + [anywhere] * len(held)
    if last:
        args += list(pool)
        in_specs += [in_vmem] * len(pool)
        out_shape = [jax.ShapeDtypeStruct(out_piece, jnp.float32)]
    else:
        out_shape = [jax.ShapeDtypeStruct(part.shape, part.dtype) for part in state]
        aliases = {state_at + i: i for i in range(len(state))}
        if with_weight:
            args.append(weight)
            in_specs.append(anywhere)
            out_shape.append(jax.ShapeDtypeStruct(weight.shape, weight.dtype))
            scratch = [pltpu.SemaphoreType.DMA(())]
        out_shape.append(jax.ShapeDtypeStruct((8, HD), jnp.float32))
    return pl.pallas_call(
        functools.partial(next_kernel, owners_of, turns, q_rows, len(held), with_weight, last),
        out_shape=out_shape,
        in_specs=in_specs,
        out_specs=[in_vmem] * len(out_shape),
        scratch_shapes=scratch,
        input_output_aliases=aliases,
        compiler_params=pltpu.CompilerParams(vmem_limit_bytes=big_limit),
        cost_estimate=small_cost,
    )(*args)


def project_kernel(meta_ref, parts_ref, weight_ref, keep_ref, send_ref):
    my_head = meta_ref[1]
    total = parts_ref[0]
    for s in range(1, parts_ref.shape[0]):
        total = total + parts_ref[s]
    rows = total.shape[0]
    high = total.astype(jnp.bfloat16)
    low = (total - high.astype(jnp.float32)).astype(jnp.bfloat16)
    both = jnp.concatenate([high, low], axis=0)
    half = keep_ref.shape[1]
    step = math.gcd(half, 512)
    for out_ref, side in ((send_ref, 1 - my_head), (keep_ref, my_head)):
        for c in range(half // step):
            start = pl.multiple_of(side * half + c * step, step)
            product = jnp.dot(
                both, weight_ref[:, pl.ds(start, step)], preferred_element_type=jnp.float32
            )
            out_ref[:, c * step : (c + 1) * step] = product[:rows] + product[rows:]


def project(meta, parts, weight):
    shape = jax.ShapeDtypeStruct((parts.shape[1], weight.shape[1] // 2), jnp.float32)
    return pl.pallas_call(
        project_kernel,
        out_shape=[shape] * 2,
        in_specs=[in_smem, in_vmem, in_vmem],
        out_specs=[in_vmem] * 2,
        compiler_params=pltpu.CompilerParams(vmem_limit_bytes=16 * 1024 * 1024),
        cost_estimate=small_cost,
    )(meta, parts, weight)


def on_device(count, queries, key_states, value_states, out_weight, turn_lengths, block_flags):
    across = 2 ** (int(math.log2(count)) // 2)
    down = count // across
    q_rows = queries.shape[0]
    turns = turn_lengths.shape[0]
    me = lax.axis_index("seq")

    def up(rows, distance):
        step = distance * across
        return lax.ppermute(rows, "seq", [(i, i + step) for i in range(count - step)])

    def over(rows, shift, distance):
        pairs = []
        for z in range(distance, down):
            for y in range(across):
                if distance == 0 and y + shift >= across:
                    continue
                pairs.append((z * across + y, z * across + (y + shift) % across))
        return lax.ppermute(rows, "seq", pairs)

    def owners_at(stage, index):
        z, y = index // across, lax.rem(index, across)
        row = (z - (stage - 1)) * across
        owners = [row + lax.rem(y - shift + across, across) for shift in range(1, across)]
        if stage < down:
            owners.append(index - stage * across)
        return owners

    my_head = lax.axis_index("head")
    meta = jnp.concatenate(
        [me.astype(jnp.int32)[None], my_head.astype(jnp.int32)[None], turn_lengths, block_flags[0]]
    )
    rows = pack(key_states, value_states)
    below = [rows] + [up(rows, distance) for distance in range(1, down)]
    shifted = [over(rows, shift, 0) for shift in range(1, across)]
    turned, member, inverse, *state = attend_first(meta, turns, queries, rows)
    out_piece = (count, turns // count, queries.shape[1])
    weight, tokens = None, [inverse]
    for stage in range(1, down + 1):
        blocks = list(shifted)
        if stage < down:
            ready = below[stage]
            held = []
            if stage > 1:
                ready, *held = lax.optimization_barrier((ready, tokens[stage - 2]))
            blocks.append(ready)
            shifted = [over(ready, shift, stage) for shift in range(1, across)]
        *state, token = attend_next(
            functools.partial(owners_at, stage),
            turns,
            q_rows,
            meta,
            turned,
            blocks,
            state,
            out_weight if stage == down - 1 else None,
            (member, inverse) if stage == down else None,
            held if stage < down else [],
            out_piece,
        )
        tokens.append(token)
        if stage == down - 1:
            weight = state.pop()
    parts = lax.all_to_all(token, "seq", split_axis=0, concat_axis=0, tiled=True)
    keep, send = project(meta, parts, weight)
    return keep + lax.ppermute(send, "head", [(0, 1), (1, 0)])


def solution(mesh):
    in_specs = (
        P(("conv", "seq"), "head"),
        P(("conv", "seq"), "head"),
        P(("conv", "seq"), "head"),
        P("head", None),
        P("conv"),
        P(("conv", "seq"), None),
    )
    out_specs = P(("conv", "seq"), "head")
    return jax.shard_map(
        functools.partial(on_device, mesh.shape["seq"]),
        mesh=mesh,
        in_specs=in_specs,
        out_specs=out_specs,
        check_vma=False,
    )
```

```python
import functools
import math

import jax
import jax.numpy as jnp
from jax import lax
from jax.experimental import pallas as pl
from jax.experimental.pallas import tpu as pltpu
from jax.sharding import PartitionSpec as P

HD = 128

big_negative = -1e30
log_two_e = 1.4426950408889634

big_limit = 40 * 1024 * 1024
small_cost = pl.CostEstimate(flops=1024, bytes_accessed=1024, transcendentals=0)

in_vmem = pl.BlockSpec(memory_space=pltpu.VMEM)
in_smem = pl.BlockSpec(memory_space=pltpu.SMEM)
anywhere = pl.BlockSpec(memory_space=pl.ANY)


def place(across):
    index = lax.axis_index("seq")
    return index // across, lax.rem(index, across)


def block_at(z, y, e, across):
    return z * across + lax.rem(y - e + across, across)


def call(kernel, out_shape, **settings):
    limit = settings.pop("limit", 16 * 1024 * 1024)
    return pl.pallas_call(
        kernel,
        out_shape=out_shape,
        out_specs=jax.tree.map(lambda _: in_vmem, out_shape),
        compiler_params=pltpu.CompilerParams(vmem_limit_bytes=limit),
        cost_estimate=small_cost,
        **settings,
    )


def pack_keys_kernel(across, key_ref, value_ref, *outs_and_sem):
    outs, done = outs_and_sem[:-1], outs_and_sem[-1]
    _, y = place(across)
    copies = []
    for e, out_ref in enumerate(outs):
        start = pl.multiple_of(lax.rem(y + e, across) * HD, HD)
        for i, ref in enumerate((key_ref, value_ref)):
            copies.append(
                pltpu.make_async_copy(
                    ref.at[:, pl.ds(start, HD)], out_ref.at[:, i * HD : (i + 1) * HD], done.at[2 * e + i]
                )
            )
    for copy in copies:
        copy.start()
    for copy in copies:
        copy.wait()


def pack_keys(across, keys, values):
    shape = jax.ShapeDtypeStruct((keys.shape[0], 2 * HD), keys.dtype)
    return call(
        functools.partial(pack_keys_kernel, across),
        [shape] * across,
        in_specs=[anywhere] * 2,
        scratch_shapes=[pltpu.SemaphoreType.DMA((2 * across,))],
    )(keys, values)


def pack_queries_kernel(across, flags_at, meta_ref, query_ref, after_ref, *outs_and_sem):
    del after_ref
    outs, done = outs_and_sem[:-1], outs_and_sem[-1]
    _, y = place(across)
    q_rows, width = query_ref.shape
    mine = width // across
    copies = []
    for e, out_ref in enumerate(outs):
        start = pl.multiple_of(lax.rem(y + e, across) * mine, mine)
        copies.append(
            pltpu.make_async_copy(
                query_ref.at[:, pl.ds(start, mine)], out_ref.at[0:q_rows, :], done.at[e]
            )
        )
    for copy in copies:
        copy.start()
    count = meta_ref.shape[0] - flags_at
    padded = outs[0].shape[0] - q_rows
    number = lax.broadcasted_iota(jnp.int32, (padded, mine), 0)
    flags = jnp.zeros((padded, mine), jnp.float32)
    for j in range(count):
        flags = jnp.where((number == j) & (meta_ref[flags_at + j] == 1), 1.0, flags)
    for out_ref in outs:
        out_ref[q_rows:, :] = flags.astype(out_ref.dtype)
    for copy in copies:
        copy.wait()


def pack_queries(across, flags_at, meta, queries, after):
    q_rows, width = queries.shape
    padded = -(-(meta.shape[0] - flags_at) // 16) * 16
    shape = jax.ShapeDtypeStruct((q_rows + padded, width // across), queries.dtype)
    return call(
        functools.partial(pack_queries_kernel, across, flags_at),
        [shape] * across,
        in_specs=[in_smem, anywhere, anywhere],
        scratch_shapes=[pltpu.SemaphoreType.DMA((across,))],
    )(meta, queries, after)


def join_kernel(*refs):
    *parts, out_ref = refs
    rows = parts[0].shape[0]
    for e, part in enumerate(parts):
        out_ref[e * rows : (e + 1) * rows, :] = part[...]


def join(parts):
    rows, width = parts[0].shape
    shape = jax.ShapeDtypeStruct((rows * len(parts), width), parts[0].dtype)
    return call(join_kernel, shape, in_specs=[in_vmem] * len(parts))(*parts)


def row_update(turned_ref, kv_ref, switches, state, first):
    top, total_sum, totals = state
    across, _, columns = turned_ref.shape
    rows = kv_ref.shape[0] // across
    factor = log_two_e / math.sqrt(HD)
    keys = kv_ref[:, :HD]
    values = kv_ref[:, HD:].T
    logits = [
        jnp.dot(keys, turned_ref[e], preferred_element_type=jnp.float32) for e in range(across)
    ]
    if first:
        key_pos = lax.broadcasted_iota(jnp.int32, (rows, 1), 0)
        column = lax.broadcasted_iota(jnp.int32, (1, columns), 1)
        causal = key_pos <= lax.rem(column, rows)
    for e in range(across):
        blocks = [logits[e][b * rows : (b + 1) * rows] for b in range(across)]
        if first:
            blocks[e] = jnp.where(causal, blocks[e], big_negative)
        new_top = None if first else top[e]
        for b in range(across):
            block_top = jnp.ceil(jnp.max(blocks[b], axis=0, keepdims=True) * factor)
            if switches[e][b] is not None:
                block_top = jnp.where(switches[e][b], block_top, big_negative)
            new_top = block_top if new_top is None else jnp.maximum(new_top, block_top)
        weights, block_sum = [], None
        for b in range(across):
            against = new_top
            if switches[e][b] is not None:
                against = jnp.where(switches[e][b], new_top, -big_negative)
            weights.append(jnp.exp2(blocks[b] * factor - against))
            part = jnp.sum(weights[b], axis=0, keepdims=True)
            block_sum = part if block_sum is None else block_sum + part
        weights = jnp.concatenate([w.astype(jnp.bfloat16) for w in weights], axis=0)
        update = jnp.dot(values, weights, preferred_element_type=jnp.float32)
        if not first:
            rescale = jnp.exp2(top[e] - new_top)
            block_sum = total_sum[e] * rescale + block_sum
            update = totals[e] * rescale + update
        top[e] = new_top
        total_sum[e] = block_sum
        totals[e] = update


def switch_of(flags_ref, e, owner, columns, allowed=None):
    padded = flags_ref.shape[0] // 2
    flag = flags_ref[pl.ds(e * padded + jnp.maximum(owner, 0), 1), :]
    if allowed is not None:
        flag = flag * jnp.where(allowed, 1.0, 0.0)
    return jnp.concatenate([flag] * (columns // HD), axis=1) > 0.5


def first_kernel(across, turns, meta_ref, *refs):
    queries, refs = refs[:across], refs[across:]
    kv_ref, weight_ref, turned_ref, flags_ref, member_ref, inverse_ref, weight_out = refs[:7]
    state, rows_ref, copied = refs[7:10], refs[10], refs[11]
    weight_copy = pltpu.make_async_copy(weight_ref, weight_out, copied)
    weight_copy.start()
    z, y = place(across)
    q_rows = kv_ref.shape[0] // across
    repeat = queries[0].shape[1] // HD
    columns = repeat * q_rows
    padded = queries[0].shape[0] - q_rows
    for e in range(across):
        for r in range(repeat):
            turned_ref[e, :, r * q_rows : (r + 1) * q_rows] = queries[e][
                0:q_rows, r * HD : (r + 1) * HD
            ].T
        flags_ref[e * padded : (e + 1) * padded, :] = queries[e][q_rows:, 0:HD].astype(jnp.float32)
    owners = [block_at(z, y, e, across) for e in range(across)]
    switches = [
        [
            None if e == b else switch_of(flags_ref, e, owners[b], columns, owners[b] < owners[e])
            for b in range(across)
        ]
        for e in range(across)
    ]
    row_update(turned_ref, kv_ref, switches, state, True)

    column = lax.broadcasted_iota(jnp.int32, (1, columns), 1)
    for e in range(across):
        position = lax.rem(column, q_rows) + owners[e] * q_rows
        start = jnp.int32(0)
        for t in range(turns):
            length = meta_ref[1 + t]
            inside = (position >= start) & (position < start + length)
            rows_ref[t : t + 1, :] = jnp.where(inside, 1.0, 0.0)
            if e == 0:
                count = jnp.full((1, HD), length, jnp.int32).astype(jnp.float32)
                inverse_ref[t : t + 1, :] = 1.0 / count
            start = start + length
        for r in range(repeat):
            mine = (column >= r * q_rows) & (column < (r + 1) * q_rows)
            member_ref[e, r * turns : (r + 1) * turns, :] = jnp.where(
                mine, rows_ref[...], 0.0
            ).astype(jnp.bfloat16)
    weight_copy.wait()


def attend_first(across, turns, meta, queries, rows, weight):
    q_rows = rows.shape[0] // across
    padded = queries[0].shape[0] - q_rows
    repeat = queries[0].shape[1] // HD
    columns = repeat * q_rows
    f32, b16 = jnp.float32, jnp.bfloat16
    return call(
        functools.partial(first_kernel, across, turns),
        [
            jax.ShapeDtypeStruct((across, HD, columns), b16),
            jax.ShapeDtypeStruct((across * padded, HD), f32),
            jax.ShapeDtypeStruct((across, repeat * turns, columns), b16),
            jax.ShapeDtypeStruct((turns, HD), f32),
            jax.ShapeDtypeStruct(weight.shape, weight.dtype),
            jax.ShapeDtypeStruct((across, 1, columns), f32),
            jax.ShapeDtypeStruct((across, 1, columns), f32),
            jax.ShapeDtypeStruct((across, HD, columns), f32),
        ],
        in_specs=[in_smem] + [in_vmem] * (across + 1) + [anywhere],
        scratch_shapes=[pltpu.VMEM((turns, columns), f32), pltpu.SemaphoreType.DMA(())],
        limit=big_limit,
    )(meta, *queries, rows, weight)


def next_kernel(across, distance, turns, last, turned_ref, flags_ref, kv_ref, *refs):
    state, refs = refs[:3], refs[3:]
    z, y = place(across)
    columns = turned_ref.shape[2]

    @pl.when(z >= distance)
    def _():
        owners = [block_at(z - distance, y, b, across) for b in range(across)]
        switches = [
            [switch_of(flags_ref, e, owners[b], columns) for b in range(across)]
            for e in range(across)
        ]
        row_update(turned_ref, kv_ref, switches, state, False)

    if last:
        member_ref, inverse_ref, out_ref = refs
        rows = out_ref.shape[1]
        pooled = None
        for e in range(across):
            attended = (state[2][e] / state[1][e]).astype(jnp.bfloat16)
            part = lax.dot_general(
                member_ref[e],
                attended,
                (((1,), (1,)), ((), ())),
                preferred_element_type=jnp.float32,
            )
            pooled = part if pooled is None else pooled + part
        for r in range(pooled.shape[0] // turns):
            mean = pooled[r * turns : (r + 1) * turns] * inverse_ref[...]
            for s in range(out_ref.shape[0]):
                out_ref[s, :, r * HD : (r + 1) * HD] = mean[s * rows : (s + 1) * rows]


def attend_next(across, distance, turns, turned, flags, rows, state, pool, out_piece):
    last = pool is not None
    args = [turned, flags, rows, *state]
    if last:
        args += list(pool)
        out_shape, aliases = [jax.ShapeDtypeStruct(out_piece, jnp.float32)], {}
    else:
        out_shape = [jax.ShapeDtypeStruct(part.shape, part.dtype) for part in state]
        aliases = {3 + i: i for i in range(len(state))}
    return call(
        functools.partial(next_kernel, across, distance, turns, last),
        out_shape,
        in_specs=[in_vmem] * len(args),
        input_output_aliases=aliases,
    )(*args)


def project_kernel(across, meta_ref, parts_ref, weight_ref, keep_ref, send_ref):
    my_head = meta_ref[0]
    groups = []
    for y in range(across):
        total = parts_ref[y]
        for s in range(y + across, parts_ref.shape[0], across):
            total = total + parts_ref[s]
        groups.append(total)
    total = jnp.concatenate(groups, axis=1)
    rows = total.shape[0]
    high = total.astype(jnp.bfloat16)
    low = (total - high.astype(jnp.float32)).astype(jnp.bfloat16)
    both = jnp.concatenate([high, low], axis=0)
    half = keep_ref.shape[1]
    step = math.gcd(half, 512)
    for out_ref, side in ((send_ref, 1 - my_head), (keep_ref, my_head)):
        for c in range(half // step):
            start = pl.multiple_of(side * half + c * step, step)
            product = jnp.dot(
                both, weight_ref[:, pl.ds(start, step)], preferred_element_type=jnp.float32
            )
            out_ref[:, c * step : (c + 1) * step] = product[:rows] + product[rows:]


def project(across, meta, parts, weight):
    shape = jax.ShapeDtypeStruct((parts.shape[1], weight.shape[1] // 2), jnp.float32)
    return call(
        functools.partial(project_kernel, across),
        [shape] * 2,
        in_specs=[in_smem, in_vmem, in_vmem],
    )(meta, parts, weight)


def on_device(count, queries, key_states, value_states, out_weight, turn_lengths, block_flags):
    across = key_states.shape[1] // HD
    down = count // across
    turns = turn_lengths.shape[0]

    def over(rows, shift):
        pairs = [(i, i - i % across + (i + shift) % across) for i in range(count)]
        return lax.ppermute(rows, "seq", pairs)

    def up(rows, distance):
        step = distance * across
        return lax.ppermute(rows, "seq", [(i, i + step) for i in range(count - step)])

    my_head = lax.axis_index("head").astype(jnp.int32)
    meta = jnp.concatenate([my_head[None], turn_lengths, block_flags[0]])
    mine, *others = pack_keys(across, key_states, value_states)
    rows = join([mine] + [over(other, shift + 1) for shift, other in enumerate(others)])
    below = [rows] + [up(rows, distance) for distance in range(1, down)]
    mine, *others = pack_queries(across, 1 + turns, meta, queries, mine)
    queries = [mine] + [over(other, shift + 1) for shift, other in enumerate(others)]
    turned, flags, member, inverse, weight, *state = attend_first(
        across, turns, meta, queries, rows, out_weight
    )
    out_piece = (count, turns // count, queries[0].shape[1])
    for distance in range(1, down):
        last = distance == down - 1
        state = attend_next(
            across,
            distance,
            turns,
            turned,
            flags,
            below[distance],
            state,
            (member, inverse) if last else None,
            out_piece,
        )
    parts = lax.all_to_all(state[0], "seq", split_axis=0, concat_axis=0, tiled=True)
    keep, send = project(across, meta, parts, weight)
    return keep + lax.ppermute(send, "head", [(0, 1), (1, 0)])


def solution(mesh):
    in_specs = (
        P(("conv", "seq"), "head"),
        P(("conv", "seq"), "head"),
        P(("conv", "seq"), "head"),
        P("head", None),
        P("conv"),
        P(("conv", "seq"), None),
    )
    out_specs = P(("conv", "seq"), "head")
    return jax.shard_map(
        functools.partial(on_device, mesh.shape["seq"]),
        mesh=mesh,
        in_specs=in_specs,
        out_specs=out_specs,
        check_vma=False,
    )
```

```python
import functools
import math

import jax
import jax.numpy as jnp
from jax import lax
from jax.experimental import pallas as pl
from jax.experimental.pallas import tpu as pltpu
from jax.sharding import PartitionSpec as P

HD = 128

big_negative = -1e30
log_two_e = 1.4426950408889634

big_limit = 40 * 1024 * 1024
small_cost = pl.CostEstimate(flops=1024, bytes_accessed=1024, transcendentals=0)

in_vmem = pl.BlockSpec(memory_space=pltpu.VMEM)
in_smem = pl.BlockSpec(memory_space=pltpu.SMEM)
anywhere = pl.BlockSpec(memory_space=pl.ANY)


def place(across):
    index = lax.axis_index("seq")
    return index // across, lax.rem(index, across)


def block_at(z, y, e, across):
    return z * across + lax.rem(y - e + across, across)


def call(kernel, out_shape, **settings):
    limit = settings.pop("limit", 16 * 1024 * 1024)
    return pl.pallas_call(
        kernel,
        out_shape=out_shape,
        out_specs=jax.tree.map(lambda _: in_vmem, out_shape),
        compiler_params=pltpu.CompilerParams(vmem_limit_bytes=limit),
        cost_estimate=small_cost,
        **settings,
    )


def pack_kernel(across, key_ref, value_ref, query_ref, flags_ref, *refs):
    heads, rows = refs[:across], refs[across : 2 * across]
    flags_read, flags_rows, done, read = refs[2 * across :]
    _, y = place(across)
    q_rows, width = query_ref.shape
    mine = width // across
    sources = []
    for e in range(across):
        at = lax.rem(y + e, across)
        head = pl.ds(pl.multiple_of(at * HD, HD), HD)
        for i, ref in enumerate((key_ref, value_ref)):
            sources.append((ref.at[:, head], heads[e].at[:, i * HD : (i + 1) * HD]))
            sources.append((ref.at[:, head], rows[e].at[0:q_rows, i * HD : (i + 1) * HD]))
        group = pl.ds(pl.multiple_of(at * mine, mine), mine)
        sources.append((query_ref.at[:, group], rows[e].at[0:q_rows, 2 * HD : 2 * HD + mine]))
    flags_copy = pltpu.make_async_copy(flags_ref, flags_read, read)
    flags_copy.start()
    copies = [
        pltpu.make_async_copy(source, target, done.at[i])
        for i, (source, target) in enumerate(sources)
    ]
    for copy in copies:
        copy.start()
    flags_copy.wait()
    number = lax.broadcasted_iota(jnp.int32, flags_rows.shape, 0)
    flags = jnp.zeros(number.shape, jnp.float32)
    for j in range(flags_read.shape[1]):
        flags = jnp.where((number == j) & (flags_read[0, j] == 1), 1.0, flags)
    flags_rows[...] = flags.astype(flags_rows.dtype)
    for e in range(across):
        copy = pltpu.make_async_copy(flags_rows, rows[e].at[q_rows:, :], done.at[len(sources) + e])
        copy.start()
        copies.append(copy)
    for copy in copies:
        copy.wait()


def pack(across, keys, values, queries, flags):
    q_rows, width = queries.shape
    padded = -(-flags.shape[1] // 16) * 16
    wide = 2 * HD + width // across
    head = jax.ShapeDtypeStruct((q_rows, 2 * HD), keys.dtype)
    row = jax.ShapeDtypeStruct((q_rows + padded, wide), keys.dtype)
    outs = pl.pallas_call(
        functools.partial(pack_kernel, across),
        out_shape=[head] * across + [row] * across,
        in_specs=[anywhere] * 4,
        out_specs=[anywhere] * (2 * across),
        scratch_shapes=[
            pltpu.SMEM(flags.shape, jnp.int32),
            pltpu.VMEM((padded, wide), keys.dtype),
            pltpu.SemaphoreType.DMA((6 * across,)),
            pltpu.SemaphoreType.DMA(()),
        ],
        cost_estimate=small_cost,
    )(keys, values, queries, flags)
    return outs[:across], outs[across:]


def row_update(turned_ref, blocks_of_row, switches, state, first):
    top, total_sum, totals = state
    across, _, columns = turned_ref.shape
    rows = blocks_of_row[0].shape[0]
    factor = log_two_e / math.sqrt(HD)
    keys = jnp.concatenate([kv_ref[0:rows, :HD] for kv_ref in blocks_of_row], axis=0)
    values = jnp.concatenate([kv_ref[0:rows, HD : 2 * HD] for kv_ref in blocks_of_row], axis=0).T
    logits = [
        jnp.dot(keys, turned_ref[e], preferred_element_type=jnp.float32) for e in range(across)
    ]
    if first:
        key_pos = lax.broadcasted_iota(jnp.int32, (rows, 1), 0)
        column = lax.broadcasted_iota(jnp.int32, (1, columns), 1)
        causal = key_pos <= lax.rem(column, rows)
    for e in range(across):
        blocks = [logits[e][b * rows : (b + 1) * rows] for b in range(across)]
        if first:
            blocks[e] = jnp.where(causal, blocks[e], big_negative)
        new_top = None if first else top[e]
        for b in range(across):
            block_top = jnp.ceil(jnp.max(blocks[b], axis=0, keepdims=True) * factor)
            if switches[e][b] is not None:
                block_top = jnp.where(switches[e][b], block_top, big_negative)
            new_top = block_top if new_top is None else jnp.maximum(new_top, block_top)
        weights, block_sum = [], None
        for b in range(across):
            against = new_top
            if switches[e][b] is not None:
                against = jnp.where(switches[e][b], new_top, -big_negative)
            weights.append(jnp.exp2(blocks[b] * factor - against))
            part = jnp.sum(weights[b], axis=0, keepdims=True)
            block_sum = part if block_sum is None else block_sum + part
        weights = jnp.concatenate([w.astype(jnp.bfloat16) for w in weights], axis=0)
        update = jnp.dot(values, weights, preferred_element_type=jnp.float32)
        if not first:
            rescale = jnp.exp2(top[e] - new_top)
            block_sum = total_sum[e] * rescale + block_sum
            update = totals[e] * rescale + update
        top[e] = new_top
        total_sum[e] = block_sum
        totals[e] = update


def switch_of(flags_ref, e, owner, columns, allowed=None):
    padded = flags_ref.shape[0] // 2
    flag = flags_ref[pl.ds(e * padded + jnp.maximum(owner, 0), 1), :]
    if allowed is not None:
        flag = flag * jnp.where(allowed, 1.0, 0.0)
    return jnp.concatenate([flag] * (columns // HD), axis=1) > 0.5


def first_kernel(across, turns, q_rows, after, meta_ref, *refs):
    row, refs = refs[:across], refs[across + after :]
    weight_ref, turned_ref, flags_ref, member_ref, inverse_ref, weight_out = refs[:6]
    state, rows_ref, copied = refs[6:9], refs[9], refs[10]
    pieces = copied.shape[0]
    depth = weight_ref.shape[0] // pieces
    weight_copies = [
        pltpu.make_async_copy(
            weight_ref.at[i * depth : (i + 1) * depth],
            weight_out.at[i * depth : (i + 1) * depth],
            copied.at[i],
        )
        for i in range(pieces)
    ]
    for copy in weight_copies:
        copy.start()
    z, y = place(across)
    repeat = row[0].shape[1] // HD - 2
    columns = repeat * q_rows
    padded = row[0].shape[0] - q_rows
    for e in range(across):
        for r in range(repeat):
            turned_ref[e, :, r * q_rows : (r + 1) * q_rows] = row[e][
                0:q_rows, (2 + r) * HD : (3 + r) * HD
            ].T
        flags_ref[e * padded : (e + 1) * padded, :] = row[e][q_rows:, 0:HD].astype(jnp.float32)
    owners = [block_at(z, y, e, across) for e in range(across)]
    switches = [
        [
            None if e == b else switch_of(flags_ref, e, owners[b], columns, owners[b] < owners[e])
            for b in range(across)
        ]
        for e in range(across)
    ]
    row_update(turned_ref, [ref.at[0:q_rows, 0 : 2 * HD] for ref in row], switches, state, True)

    column = lax.broadcasted_iota(jnp.int32, (1, columns), 1)
    for e in range(across):
        position = lax.rem(column, q_rows) + owners[e] * q_rows
        start = jnp.int32(0)
        for t in range(turns):
            length = meta_ref[1 + t]
            inside = (position >= start) & (position < start + length)
            rows_ref[t : t + 1, :] = jnp.where(inside, 1.0, 0.0)
            if e == 0:
                count = jnp.full((1, HD), length, jnp.int32).astype(jnp.float32)
                inverse_ref[t : t + 1, :] = 1.0 / count
            start = start + length
        for r in range(repeat):
            mine = (column >= r * q_rows) & (column < (r + 1) * q_rows)
            member_ref[e, r * turns : (r + 1) * turns, :] = jnp.where(
                mine, rows_ref[...], 0.0
            ).astype(jnp.bfloat16)
    for copy in weight_copies:
        copy.wait()


def attend_first(across, turns, q_rows, meta, row, weight, after):
    padded = row[0].shape[0] - q_rows
    repeat = row[0].shape[1] // HD - 2
    columns = repeat * q_rows
    f32, b16 = jnp.float32, jnp.bfloat16
    return call(
        functools.partial(first_kernel, across, turns, q_rows, len(after)),
        [
            jax.ShapeDtypeStruct((across, HD, columns), b16),
            jax.ShapeDtypeStruct((across * padded, HD), f32),
            jax.ShapeDtypeStruct((across, repeat * turns, columns), b16),
            jax.ShapeDtypeStruct((turns, HD), f32),
            jax.ShapeDtypeStruct(weight.shape, weight.dtype),
            jax.ShapeDtypeStruct((across, 1, columns), f32),
            jax.ShapeDtypeStruct((across, 1, columns), f32),
            jax.ShapeDtypeStruct((across, HD, columns), f32),
        ],
        in_specs=[in_smem] + [in_vmem] * across + [anywhere] * (len(after) + 1),
        scratch_shapes=[pltpu.VMEM((turns, columns), f32), pltpu.SemaphoreType.DMA((8,))],
        limit=big_limit,
    )(meta, *row, *after, weight)


def next_kernel(across, distance, turns, last, turned_ref, flags_ref, *refs):
    row, state, refs = refs[:across], refs[across : across + 3], refs[across + 3 :]
    z, y = place(across)
    columns = turned_ref.shape[2]

    @pl.when(z >= distance)
    def _():
        owners = [block_at(z - distance, y, b, across) for b in range(across)]
        switches = [
            [switch_of(flags_ref, e, owners[b], columns) for b in range(across)]
            for e in range(across)
        ]
        row_update(turned_ref, row, switches, state, False)

    if last:
        member_ref, inverse_ref, out_ref = refs
        rows = out_ref.shape[1]
        pooled = None
        for e in range(across):
            attended = (state[2][e] / state[1][e]).astype(jnp.bfloat16)
            part = lax.dot_general(
                member_ref[e],
                attended,
                (((1,), (1,)), ((), ())),
                preferred_element_type=jnp.float32,
            )
            pooled = part if pooled is None else pooled + part
        for r in range(pooled.shape[0] // turns):
            mean = pooled[r * turns : (r + 1) * turns] * inverse_ref[...]
            for s in range(out_ref.shape[0]):
                out_ref[s, :, r * HD : (r + 1) * HD] = mean[s * rows : (s + 1) * rows]


def attend_next(across, distance, turns, turned, flags, row, state, pool, out_piece):
    last = pool is not None
    args = [turned, flags, *row, *state]
    if last:
        args += list(pool)
        out_shape, aliases = [jax.ShapeDtypeStruct(out_piece, jnp.float32)], {}
    else:
        out_shape = [jax.ShapeDtypeStruct(part.shape, part.dtype) for part in state]
        aliases = {2 + across + i: i for i in range(len(state))}
    return call(
        functools.partial(next_kernel, across, distance, turns, last),
        out_shape,
        in_specs=[in_vmem] * len(args),
        input_output_aliases=aliases,
    )(*args)


def project_kernel(across, other, meta_ref, parts_ref, weight_ref, out_ref):
    side = 1 - meta_ref[0] if other else meta_ref[0]
    groups = []
    for y in range(across):
        total = parts_ref[y]
        for s in range(y + across, parts_ref.shape[0], across):
            total = total + parts_ref[s]
        groups.append(total)
    total = jnp.concatenate(groups, axis=1)
    rows = total.shape[0]
    high = total.astype(jnp.bfloat16)
    low = (total - high.astype(jnp.float32)).astype(jnp.bfloat16)
    both = jnp.concatenate([high, low], axis=0)
    half = out_ref.shape[1]
    step = math.gcd(half, 512)
    for c in range(half // step):
        start = pl.multiple_of(side * half + c * step, step)
        product = jnp.dot(
            both, weight_ref[:, pl.ds(start, step)], preferred_element_type=jnp.float32
        )
        out_ref[:, c * step : (c + 1) * step] = product[:rows] + product[rows:]


def project(across, other, meta, parts, weight):
    return call(
        functools.partial(project_kernel, across, other),
        jax.ShapeDtypeStruct((parts.shape[1], weight.shape[1] // 2), jnp.float32),
        in_specs=[in_smem, in_vmem, in_vmem],
    )(meta, parts, weight)


def on_device(count, queries, key_states, value_states, out_weight, turn_lengths, block_flags):
    across = key_states.shape[1] // HD
    down = count // across
    turns = turn_lengths.shape[0]

    def send(rows, distance, shift):
        pairs = []
        for i in range(count - distance * across):
            z, y = i // across + distance, (i + shift) % across
            pairs.append((i, z * across + y))
        return lax.ppermute(rows, "seq", pairs)

    my_head = lax.axis_index("head").astype(jnp.int32)
    meta = jnp.concatenate([my_head[None], turn_lengths])
    parts, row = pack(across, key_states, value_states, queries, block_flags)
    below = [
        [send(parts[shift], distance, shift) for shift in range(across)]
        for distance in range(1, down)
    ]
    row = [row[0]] + [send(row[shift], 0, shift) for shift in range(1, across)]
    turned, flags, member, inverse, weight, *state = attend_first(
        across, turns, queries.shape[0], meta, row, out_weight, below[-1]
    )
    out_piece = (count, turns // count, queries.shape[1] // across)
    for distance in range(down - 1, 0, -1):
        last = distance == 1
        state = attend_next(
            across,
            distance,
            turns,
            turned,
            flags,
            below[distance - 1],
            state,
            (member, inverse) if last else None,
            out_piece,
        )
    parts = lax.all_to_all(state[0], "seq", split_axis=0, concat_axis=0, tiled=True)
    others = project(across, True, meta, parts, weight)
    others = lax.ppermute(others, "head", [(0, 1), (1, 0)])
    return project(across, False, meta, parts, weight) + others


def solution(mesh):
    in_specs = (
        P(("conv", "seq"), "head"),
        P(("conv", "seq"), "head"),
        P(("conv", "seq"), "head"),
        P("head", None),
        P("conv"),
        P(("conv", "seq"), None),
    )
    out_specs = P(("conv", "seq"), "head")
    return jax.shard_map(
        functools.partial(on_device, mesh.shape["seq"]),
        mesh=mesh,
        in_specs=in_specs,
        out_specs=out_specs,
        check_vma=False,
    )
```

```python
import functools
import math

import jax
import jax.numpy as jnp
from jax import lax
from jax.experimental import pallas as pl
from jax.experimental.pallas import tpu as pltpu
from jax.sharding import PartitionSpec as P

HD = 128

big_negative = -1e30
log_two_e = 1.4426950408889634

big_limit = 40 * 1024 * 1024
small_cost = pl.CostEstimate(flops=1024, bytes_accessed=1024, transcendentals=0)

in_vmem = pl.BlockSpec(memory_space=pltpu.VMEM)
in_smem = pl.BlockSpec(memory_space=pltpu.SMEM)
anywhere = pl.BlockSpec(memory_space=pl.ANY)


def place(across):
    index = lax.axis_index("seq")
    return index // across, lax.rem(index, across)


def block_at(z, y, e, across):
    return z * across + lax.rem(y - e + across, across)


def call(kernel, out_shape, **settings):
    limit = settings.pop("limit", 16 * 1024 * 1024)
    return pl.pallas_call(
        kernel,
        out_shape=out_shape,
        out_specs=jax.tree.map(lambda _: in_vmem, out_shape),
        compiler_params=pltpu.CompilerParams(vmem_limit_bytes=limit),
        cost_estimate=small_cost,
        **settings,
    )


def pick(rows, number, parts):
    width = rows.shape[1] // parts
    picked = rows[:, :width]
    for part in range(1, parts):
        picked = jnp.where(number == part, rows[:, part * width : (part + 1) * width], picked)
    return picked


def pair(keys, values):
    which = lax.broadcasted_iota(jnp.int32, (2,) + keys.shape, 0)
    return jnp.where(which == 0, keys[None], values[None])


def join_kernel(*refs):
    *parts, out_ref = refs
    for e, part in enumerate(parts):
        out_ref[e] = part[...]


def join(parts):
    shape = jax.ShapeDtypeStruct((len(parts),) + parts[0].shape, parts[0].dtype)
    return call(join_kernel, shape, in_specs=[in_vmem] * len(parts))(*parts)


def row_update(turned_ref, kv_ref, switches, state, first):
    top, total_sum, totals = state
    across, _, columns = turned_ref.shape
    rows = kv_ref.shape[2]
    factor = log_two_e / math.sqrt(HD)
    keys = kv_ref[:, 0].reshape(across * rows, HD)
    values = kv_ref[:, 1].reshape(across * rows, HD).T
    logits = [
        jnp.dot(keys, turned_ref[e], preferred_element_type=jnp.float32) for e in range(across)
    ]
    if first:
        key_pos = lax.broadcasted_iota(jnp.int32, (rows, 1), 0)
        column = lax.broadcasted_iota(jnp.int32, (1, columns), 1)
        causal = key_pos <= lax.rem(column, rows)
    for e in range(across):
        blocks = [logits[e][b * rows : (b + 1) * rows] for b in range(across)]
        if first:
            blocks[e] = jnp.where(causal, blocks[e], big_negative)
        new_top = None if first else top[e]
        for b in range(across):
            block_top = jnp.ceil(jnp.max(blocks[b], axis=0, keepdims=True) * factor)
            if switches[e][b] is not None:
                block_top = jnp.where(switches[e][b], block_top, big_negative)
            new_top = block_top if new_top is None else jnp.maximum(new_top, block_top)
        weights, block_sum = [], None
        for b in range(across):
            against = new_top
            if switches[e][b] is not None:
                against = jnp.where(switches[e][b], new_top, -big_negative)
            weights.append(jnp.exp2(blocks[b] * factor - against))
            part = jnp.sum(weights[b], axis=0, keepdims=True)
            block_sum = part if block_sum is None else block_sum + part
        weights = jnp.concatenate([w.astype(jnp.bfloat16) for w in weights], axis=0)
        update = jnp.dot(values, weights, preferred_element_type=jnp.float32)
        if not first:
            rescale = jnp.exp2(top[e] - new_top)
            block_sum = total_sum[e] * rescale + block_sum
            update = totals[e] * rescale + update
        top[e] = new_top
        total_sum[e] = block_sum
        totals[e] = update


def switch_of(flags_ref, e, owner, columns, allowed=None):
    flag = flags_ref[e, jnp.maximum(owner, 0)] == 1
    if allowed is not None:
        flag = flag & allowed
    return jnp.full((1, columns), jnp.where(flag, 1, 0), jnp.int32) == 1


def first_kernel(across, turns, meta_ref, flags_ref, own_ref, *refs):
    queries, refs = refs[: across - 1], refs[across - 1 :]
    kv_ref, weight_ref, turned_ref, member_ref, inverse_ref, weight_out = refs[:6]
    state, rows_ref, copied = refs[6:9], refs[9], refs[10]
    weight_copy = pltpu.make_async_copy(weight_ref, weight_out, copied)
    weight_copy.start()
    z, y = place(across)
    q_rows = kv_ref.shape[2]
    repeat = own_ref.shape[1] // HD // across
    columns = repeat * q_rows
    for r in range(repeat):
        span = slice(r * q_rows, (r + 1) * q_rows)
        head = pl.multiple_of((y * repeat + r) * HD, HD)
        turned_ref[0, :, span] = own_ref[:, pl.ds(head, HD)].T
        for e in range(1, across):
            turned_ref[e, :, span] = queries[e - 1][:, r * HD : (r + 1) * HD].T
    owners = [block_at(z, y, e, across) for e in range(across)]
    switches = [
        [
            None if e == b else switch_of(flags_ref, e, owners[b], columns, owners[b] < owners[e])
            for b in range(across)
        ]
        for e in range(across)
    ]
    row_update(turned_ref, kv_ref, switches, state, True)

    column = lax.broadcasted_iota(jnp.int32, (1, columns), 1)
    for e in range(across):
        position = lax.rem(column, q_rows) + owners[e] * q_rows
        start = jnp.int32(0)
        for t in range(turns):
            length = meta_ref[1 + t]
            inside = (position >= start) & (position < start + length)
            rows_ref[t : t + 1, :] = jnp.where(inside, 1.0, 0.0)
            if e == 0:
                count = jnp.full((1, HD), length, jnp.int32).astype(jnp.float32)
                inverse_ref[t : t + 1, :] = 1.0 / count
            start = start + length
        for r in range(repeat):
            mine = (column >= r * q_rows) & (column < (r + 1) * q_rows)
            member_ref[e, r * turns : (r + 1) * turns, :] = jnp.where(
                mine, rows_ref[...], 0.0
            ).astype(jnp.bfloat16)
    weight_copy.wait()


def attend_first(across, turns, meta, flags, own, queries, rows, weight):
    q_rows = rows.shape[2]
    repeat = own.shape[1] // HD // across
    columns = repeat * q_rows
    f32, b16 = jnp.float32, jnp.bfloat16
    return call(
        functools.partial(first_kernel, across, turns),
        [
            jax.ShapeDtypeStruct((across, HD, columns), b16),
            jax.ShapeDtypeStruct((across, repeat * turns, columns), b16),
            jax.ShapeDtypeStruct((turns, HD), f32),
            jax.ShapeDtypeStruct(weight.shape, weight.dtype),
            jax.ShapeDtypeStruct((across, 1, columns), f32),
            jax.ShapeDtypeStruct((across, 1, columns), f32),
            jax.ShapeDtypeStruct((across, HD, columns), f32),
        ],
        in_specs=[in_smem] * 2 + [in_vmem] * (across + 1) + [anywhere],
        scratch_shapes=[pltpu.VMEM((turns, columns), f32), pltpu.SemaphoreType.DMA(())],
        limit=big_limit,
    )(meta, flags, own, *queries, rows, weight)


def next_kernel(across, distance, turns, last, flags_ref, turned_ref, kv_ref, *refs):
    state, refs = refs[:3], refs[3:]
    z, y = place(across)
    columns = turned_ref.shape[2]

    @pl.when(z >= distance)
    def _():
        owners = [block_at(z - distance, y, b, across) for b in range(across)]
        switches = [
            [switch_of(flags_ref, e, owners[b], columns) for b in range(across)]
            for e in range(across)
        ]
        row_update(turned_ref, kv_ref, switches, state, False)

    if last:
        member_ref, inverse_ref, out_ref = refs
        rows = out_ref.shape[1]
        pooled = None
        for e in range(across):
            attended = (state[2][e] / state[1][e]).astype(jnp.bfloat16)
            part = lax.dot_general(
                member_ref[e],
                attended,
                (((1,), (1,)), ((), ())),
                preferred_element_type=jnp.float32,
            )
            pooled = part if pooled is None else pooled + part
        for r in range(pooled.shape[0] // turns):
            mean = pooled[r * turns : (r + 1) * turns] * inverse_ref[...]
            for s in range(out_ref.shape[0]):
                out_ref[s, :, r * HD : (r + 1) * HD] = mean[s * rows : (s + 1) * rows]


def attend_next(across, distance, turns, turned, flags, rows, state, pool, out_piece):
    last = pool is not None
    args = [flags, turned, rows, *state]
    if last:
        args += list(pool)
        out_shape, aliases = [jax.ShapeDtypeStruct(out_piece, jnp.float32)], {}
    else:
        out_shape = [jax.ShapeDtypeStruct(part.shape, part.dtype) for part in state]
        aliases = {3 + i: i for i in range(len(state))}
    return call(
        functools.partial(next_kernel, across, distance, turns, last),
        out_shape,
        in_specs=[in_smem] + [in_vmem] * (len(args) - 1),
        input_output_aliases=aliases,
    )(*args)


def project_kernel(across, other, meta_ref, parts_ref, weight_ref, out_ref):
    side = 1 - meta_ref[0] if other else meta_ref[0]
    groups = []
    for y in range(across):
        total = parts_ref[y]
        for s in range(y + across, parts_ref.shape[0], across):
            total = total + parts_ref[s]
        groups.append(total)
    total = jnp.concatenate(groups, axis=1)
    rows = total.shape[0]
    high = total.astype(jnp.bfloat16)
    low = (total - high.astype(jnp.float32)).astype(jnp.bfloat16)
    both = jnp.concatenate([high, low], axis=0)
    half = out_ref.shape[1]
    step = math.gcd(half, 512)
    for c in range(half // step):
        start = pl.multiple_of(side * half + c * step, step)
        product = jnp.dot(
            both, weight_ref[:, pl.ds(start, step)], preferred_element_type=jnp.float32
        )
        out_ref[:, c * step : (c + 1) * step] = product[:rows] + product[rows:]


def project(across, other, meta, parts, weight):
    return call(
        functools.partial(project_kernel, across, other),
        jax.ShapeDtypeStruct((parts.shape[1], weight.shape[1] // 2), jnp.float32),
        in_specs=[in_smem, in_vmem, in_vmem],
    )(meta, parts, weight)


def on_device(count, queries, key_states, value_states, out_weight, turn_lengths, block_flags):
    across = key_states.shape[1] // HD
    down = count // across
    turns = turn_lengths.shape[0]

    def over(rows, shift):
        pairs = [(i, i - i % across + (i + shift) % across) for i in range(count)]
        return lax.ppermute(rows, "seq", pairs)

    def up(rows, distance):
        step = distance * across
        return lax.ppermute(rows, "seq", [(i, i + step) for i in range(count - step)])

    _, y = place(across)
    my_head = lax.axis_index("head").astype(jnp.int32)
    meta = jnp.concatenate([my_head[None], turn_lengths])
    heads = []
    for shift in range(across):
        at = lax.rem(y + shift, across)
        heads.append(pair(pick(key_states, at, across), pick(value_states, at, across)))
    others = [
        over(pick(queries, lax.rem(y + shift, across), across), shift) for shift in range(1, across)
    ]
    rows = join([heads[0]] + [over(heads[shift], shift) for shift in range(1, across)])
    below = [rows] + [up(rows, distance) for distance in range(1, down)]
    flags, below[-1] = lax.optimization_barrier((block_flags, below[-1]))
    flags = jnp.concatenate([flags] + [over(flags, shift) for shift in range(1, across)], axis=0)
    turned, member, inverse, weight, *state = attend_first(
        across, turns, meta, flags, queries, others, rows, out_weight
    )
    out_piece = (count, turns // count, queries.shape[1] // across)
    for distance in range(down - 1, 0, -1):
        last = distance == 1
        state = attend_next(
            across,
            distance,
            turns,
            turned,
            flags,
            below[distance],
            state,
            (member, inverse) if last else None,
            out_piece,
        )
    parts = lax.all_to_all(state[0], "seq", split_axis=0, concat_axis=0, tiled=True)
    others = project(across, True, meta, parts, weight)
    others = lax.ppermute(others, "head", [(0, 1), (1, 0)])
    return project(across, False, meta, parts, weight) + others


def solution(mesh):
    in_specs = (
        P(("conv", "seq"), "head"),
        P(("conv", "seq"), "head"),
        P(("conv", "seq"), "head"),
        P("head", None),
        P("conv"),
        P(("conv", "seq"), None),
    )
    out_specs = P(("conv", "seq"), "head")
    return jax.shard_map(
        functools.partial(on_device, mesh.shape["seq"]),
        mesh=mesh,
        in_specs=in_specs,
        out_specs=out_specs,
        check_vma=False,
    )
```

```python
import functools
import math

import jax
import jax.numpy as jnp
from jax import lax
from jax.experimental import pallas as pl
from jax.experimental.pallas import tpu as pltpu
from jax.sharding import PartitionSpec as P

HD = 128

big_negative = -1e30
log_two_e = 1.4426950408889634

big_limit = 40 * 1024 * 1024
small_cost = pl.CostEstimate(flops=1024, bytes_accessed=1024, transcendentals=0)

in_vmem = pl.BlockSpec(memory_space=pltpu.VMEM)
in_smem = pl.BlockSpec(memory_space=pltpu.SMEM)
anywhere = pl.BlockSpec(memory_space=pl.ANY)


def place(across):
    index = lax.axis_index("seq")
    return index // across, lax.rem(index, across)


def block_at(z, y, e, across):
    return z * across + lax.rem(y - e + across, across)


def call(kernel, out_shape, **settings):
    limit = settings.pop("limit", 16 * 1024 * 1024)
    return pl.pallas_call(
        kernel,
        out_shape=out_shape,
        out_specs=jax.tree.map(lambda _: in_vmem, out_shape),
        compiler_params=pltpu.CompilerParams(vmem_limit_bytes=limit),
        cost_estimate=small_cost,
        **settings,
    )


def pick(rows, number, parts):
    width = rows.shape[1] // parts
    picked = rows[:, :width]
    for part in range(1, parts):
        picked = jnp.where(number == part, rows[:, part * width : (part + 1) * width], picked)
    return picked


def pair(keys, values):
    which = lax.broadcasted_iota(jnp.int32, (2,) + keys.shape, 0)
    return jnp.where(which == 0, keys[None], values[None])


def join_kernel(*refs):
    *parts, _, out_ref = refs
    for e, part in enumerate(parts):
        out_ref[e] = part[...]


def join(parts, after):
    shape = jax.ShapeDtypeStruct((len(parts),) + parts[0].shape, parts[0].dtype)
    return call(join_kernel, shape, in_specs=[in_vmem] * len(parts) + [anywhere])(*parts, after)


def rows_update(turned_ref, rows_refs, switches, state, first):
    top, total_sum, totals = state
    across, _, columns = turned_ref.shape
    rows = rows_refs[0].shape[2]
    count = across * len(rows_refs)
    factor = log_two_e / math.sqrt(HD)
    keys = [kv_ref[:, 0].reshape(across * rows, HD) for kv_ref in rows_refs]
    values = [kv_ref[:, 1].reshape(across * rows, HD).T for kv_ref in rows_refs]
    logits = [
        [jnp.dot(part, turned_ref[e], preferred_element_type=jnp.float32) for part in keys]
        for e in range(across)
    ]
    if first:
        key_pos = lax.broadcasted_iota(jnp.int32, (rows, 1), 0)
        column = lax.broadcasted_iota(jnp.int32, (1, columns), 1)
        causal = key_pos <= lax.rem(column, rows)
    for e in range(across):
        blocks = [
            logits[e][b // across][b % across * rows : (b % across + 1) * rows] for b in range(count)
        ]
        if first:
            blocks[e] = jnp.where(causal, blocks[e], big_negative)
        new_top = None if first else top[e]
        for b in range(count):
            block_top = jnp.ceil(jnp.max(blocks[b], axis=0, keepdims=True) * factor)
            if switches[e][b] is not None:
                block_top = jnp.where(switches[e][b], block_top, big_negative)
            new_top = block_top if new_top is None else jnp.maximum(new_top, block_top)
        weights, block_sum = [], None
        for b in range(count):
            against = new_top
            if switches[e][b] is not None:
                against = jnp.where(switches[e][b], new_top, -big_negative)
            weights.append(jnp.exp2(blocks[b] * factor - against))
            part = jnp.sum(weights[b], axis=0, keepdims=True)
            block_sum = part if block_sum is None else block_sum + part
        update = None
        for i, part in enumerate(values):
            mine = weights[i * across : (i + 1) * across]
            mine = jnp.concatenate([w.astype(jnp.bfloat16) for w in mine], axis=0)
            part = jnp.dot(part, mine, preferred_element_type=jnp.float32)
            update = part if update is None else update + part
        if not first:
            rescale = jnp.exp2(top[e] - new_top)
            block_sum = total_sum[e] * rescale + block_sum
            update = totals[e] * rescale + update
        top[e] = new_top
        total_sum[e] = block_sum
        totals[e] = update


def switch_of(flags_ref, e, owner, columns, allowed=None):
    flag = flags_ref[e, pl.ds(jnp.maximum(owner, 0), 1), :]
    if allowed is not None:
        flag = flag * jnp.where(allowed, 1.0, 0.0)
    return jnp.concatenate([flag] * (columns // HD), axis=1) > 0.5


def first_kernel(across, turns, meta_ref, own_flags_ref, own_ref, *refs):
    queries, refs = refs[: across - 1], refs[across - 1 :]
    kv_ref, weight_ref, turned_ref, flags_ref, member_ref, inverse_ref, weight_out = refs[:7]
    state, rows_ref, copied = refs[7:10], refs[10], refs[11]
    weight_copy = pltpu.make_async_copy(weight_ref, weight_out, copied)
    weight_copy.start()
    z, y = place(across)
    q_rows = kv_ref.shape[2]
    repeat = own_ref.shape[1] // HD // across
    columns = repeat * q_rows
    for r in range(repeat):
        span = slice(r * q_rows, (r + 1) * q_rows)
        head = pl.multiple_of((y * repeat + r) * HD, HD)
        turned_ref[0, :, span] = own_ref[:, pl.ds(head, HD)].T
        for e in range(1, across):
            turned_ref[e, :, span] = queries[e - 1][0:q_rows, r * HD : (r + 1) * HD].T
    flags_ref[0] = own_flags_ref[...]
    for e in range(1, across):
        flags_ref[e] = queries[e - 1][q_rows:, 0:HD].astype(jnp.float32)
    owners = [block_at(z, y, e, across) for e in range(across)]
    switches = [
        [
            None if e == b else switch_of(flags_ref, e, owners[b], columns, owners[b] < owners[e])
            for b in range(across)
        ]
        for e in range(across)
    ]
    rows_update(turned_ref, [kv_ref], switches, state, True)

    column = lax.broadcasted_iota(jnp.int32, (1, columns), 1)
    for e in range(across):
        position = lax.rem(column, q_rows) + owners[e] * q_rows
        start = jnp.int32(0)
        for t in range(turns):
            length = meta_ref[1 + t]
            inside = (position >= start) & (position < start + length)
            rows_ref[t : t + 1, :] = jnp.where(inside, 1.0, 0.0)
            if e == 0:
                count = jnp.full((1, HD), length, jnp.int32).astype(jnp.float32)
                inverse_ref[t : t + 1, :] = 1.0 / count
            start = start + length
        for r in range(repeat):
            mine = (column >= r * q_rows) & (column < (r + 1) * q_rows)
            member_ref[e, r * turns : (r + 1) * turns, :] = jnp.where(
                mine, rows_ref[...], 0.0
            ).astype(jnp.bfloat16)
    weight_copy.wait()


def attend_first(across, turns, meta, flags, own, queries, rows, weight):
    q_rows = rows.shape[2]
    repeat = own.shape[1] // HD // across
    columns = repeat * q_rows
    f32, b16 = jnp.float32, jnp.bfloat16
    return call(
        functools.partial(first_kernel, across, turns),
        [
            jax.ShapeDtypeStruct((across, HD, columns), b16),
            jax.ShapeDtypeStruct((across,) + flags.shape, f32),
            jax.ShapeDtypeStruct((across, repeat * turns, columns), b16),
            jax.ShapeDtypeStruct((turns, HD), f32),
            jax.ShapeDtypeStruct(weight.shape, weight.dtype),
            jax.ShapeDtypeStruct((across, 1, columns), f32),
            jax.ShapeDtypeStruct((across, 1, columns), f32),
            jax.ShapeDtypeStruct((across, HD, columns), f32),
        ],
        in_specs=[in_smem] + [in_vmem] * (across + 2) + [anywhere],
        scratch_shapes=[pltpu.VMEM((turns, columns), f32), pltpu.SemaphoreType.DMA(())],
        limit=big_limit,
    )(meta, flags, own, *queries, rows, weight)


def next_kernel(across, distances, turns, last, flags_ref, turned_ref, *refs):
    below, refs = refs[: len(distances)], refs[len(distances) :]
    state, refs = refs[:3], refs[3:]
    z, y = place(across)
    columns = turned_ref.shape[2]

    def update(number):
        switches = [
            [
                switch_of(flags_ref, e, block_at(z - distance, y, b, across), columns)
                for distance in distances[:number]
                for b in range(across)
            ]
            for e in range(across)
        ]
        rows_update(turned_ref, below[:number], switches, state, False)

    for number, distance in enumerate(distances):
        if number + 1 == len(distances):
            pl.when(z >= distance)(functools.partial(update, number + 1))
        else:
            pl.when(z == distance)(functools.partial(update, number + 1))

    if last:
        member_ref, inverse_ref, out_ref = refs
        rows = out_ref.shape[1]
        pooled = None
        for e in range(across):
            attended = (state[2][e] / state[1][e]).astype(jnp.bfloat16)
            part = lax.dot_general(
                member_ref[e],
                attended,
                (((1,), (1,)), ((), ())),
                preferred_element_type=jnp.float32,
            )
            pooled = part if pooled is None else pooled + part
        for r in range(pooled.shape[0] // turns):
            mean = pooled[r * turns : (r + 1) * turns] * inverse_ref[...]
            for s in range(out_ref.shape[0]):
                out_ref[s, :, r * HD : (r + 1) * HD] = mean[s * rows : (s + 1) * rows]


def attend_next(across, distances, turns, turned, flags, below, state, pool, out_piece):
    last = pool is not None
    args = [flags, turned, *below, *state]
    if last:
        args += list(pool)
        out_shape, aliases = [jax.ShapeDtypeStruct(out_piece, jnp.float32)], {}
    else:
        out_shape = [jax.ShapeDtypeStruct(part.shape, part.dtype) for part in state]
        aliases = {2 + len(below) + i: i for i in range(len(state))}
    return call(
        functools.partial(next_kernel, across, distances, turns, last),
        out_shape,
        in_specs=[in_vmem] * len(args),
        input_output_aliases=aliases,
    )(*args)


def project_kernel(across, other, meta_ref, parts_ref, weight_ref, out_ref):
    side = 1 - meta_ref[0] if other else meta_ref[0]
    groups = []
    for y in range(across):
        total = parts_ref[y]
        for s in range(y + across, parts_ref.shape[0], across):
            total = total + parts_ref[s]
        groups.append(total)
    total = jnp.concatenate(groups, axis=1)
    rows = total.shape[0]
    high = total.astype(jnp.bfloat16)
    low = (total - high.astype(jnp.float32)).astype(jnp.bfloat16)
    both = jnp.concatenate([high, low], axis=0)
    half = out_ref.shape[1]
    step = math.gcd(half, 512)
    for c in range(half // step):
        start = pl.multiple_of(side * half + c * step, step)
        product = jnp.dot(
            both, weight_ref[:, pl.ds(start, step)], preferred_element_type=jnp.float32
        )
        out_ref[:, c * step : (c + 1) * step] = product[:rows] + product[rows:]


def project(across, other, meta, parts, weight):
    return call(
        functools.partial(project_kernel, across, other),
        jax.ShapeDtypeStruct((parts.shape[1], weight.shape[1] // 2), jnp.float32),
        in_specs=[in_smem, in_vmem, in_vmem],
    )(meta, parts, weight)


def on_device(count, queries, key_states, value_states, out_weight, turn_lengths, block_flags):
    across = key_states.shape[1] // HD
    down = count // across
    turns = turn_lengths.shape[0]

    def over(rows, shift):
        pairs = [(i, i - i % across + (i + shift) % across) for i in range(count)]
        return lax.ppermute(rows, "seq", pairs)

    def up(rows, distance):
        step = distance * across
        return lax.ppermute(rows, "seq", [(i, i + step) for i in range(count - step)])

    _, y = place(across)
    my_head = lax.axis_index("head").astype(jnp.int32)
    meta = jnp.concatenate([my_head[None], turn_lengths])
    heads = []
    for shift in range(across):
        at = lax.rem(y + shift, across)
        heads.append(pair(pick(key_states, at, across), pick(value_states, at, across)))
    padded = -(-count // 16) * 16
    flags = jnp.pad(block_flags[0], (0, padded - count))[:, None]
    sent = []
    for shift in range(1, across):
        group = pick(queries, lax.rem(y + shift, across), across)
        below = jnp.broadcast_to(flags, (padded, group.shape[1])).astype(group.dtype)
        sent.append(jnp.concatenate([group, below], axis=0))
    flags = jnp.broadcast_to(flags, (padded, HD)).astype(jnp.float32)
    others = [over(group, shift) for shift, group in enumerate(sent, 1)]
    rows = join([heads[0]] + [over(heads[shift], shift) for shift in range(1, across)], sent[0])
    below = [rows] + [up(rows, distance) for distance in range(1, down)]
    turned, flags, member, inverse, weight, *state = attend_first(
        across, turns, meta, flags, queries, others, rows, out_weight
    )
    out_piece = (count, turns // count, queries.shape[1] // across)
    stages = [[1]] + [list(range(d, min(d + 2, down))) for d in range(2, down, 2)]
    for distances in stages:
        last = distances == stages[-1]
        state = attend_next(
            across,
            distances,
            turns,
            turned,
            flags,
            [below[distance] for distance in distances],
            state,
            (member, inverse) if last else None,
            out_piece,
        )
    parts = lax.all_to_all(state[0], "seq", split_axis=0, concat_axis=0, tiled=True)
    others = project(across, True, meta, parts, weight)
    others = lax.ppermute(others, "head", [(0, 1), (1, 0)])
    return project(across, False, meta, parts, weight) + others


def solution(mesh):
    in_specs = (
        P(("conv", "seq"), "head"),
        P(("conv", "seq"), "head"),
        P(("conv", "seq"), "head"),
        P("head", None),
        P("conv"),
        P(("conv", "seq"), None),
    )
    out_specs = P(("conv", "seq"), "head")
    return jax.shard_map(
        functools.partial(on_device, mesh.shape["seq"]),
        mesh=mesh,
        in_specs=in_specs,
        out_specs=out_specs,
        check_vma=False,
    )
```

```python
import functools
import math

import jax
import jax.numpy as jnp
from jax import lax
from jax.experimental import pallas as pl
from jax.experimental.pallas import tpu as pltpu
from jax.sharding import PartitionSpec as P

HD = 128

big_negative = -1e30
log_two_e = 1.4426950408889634

big_limit = 40 * 1024 * 1024
small_cost = pl.CostEstimate(flops=1024, bytes_accessed=1024, transcendentals=0)

in_vmem = pl.BlockSpec(memory_space=pltpu.VMEM)
in_smem = pl.BlockSpec(memory_space=pltpu.SMEM)
anywhere = pl.BlockSpec(memory_space=pl.ANY)


def place(across):
    index = lax.axis_index("seq")
    return index // across, lax.rem(index, across)


def block_at(z, y, e, across):
    return z * across + lax.rem(y - e + across, across)


def call(kernel, out_shape, **settings):
    limit = settings.pop("limit", 16 * 1024 * 1024)
    return pl.pallas_call(
        kernel,
        out_shape=out_shape,
        out_specs=jax.tree.map(lambda _: in_vmem, out_shape),
        compiler_params=pltpu.CompilerParams(vmem_limit_bytes=limit),
        cost_estimate=small_cost,
        **settings,
    )


def pick(rows, number, parts):
    width = rows.shape[1] // parts
    picked = rows[:, :width]
    for part in range(1, parts):
        picked = jnp.where(number == part, rows[:, part * width : (part + 1) * width], picked)
    return picked


def pair(keys, values):
    which = lax.broadcasted_iota(jnp.int32, (2,) + keys.shape, 0)
    return jnp.where(which == 0, keys[None], values[None])


def join_kernel(*refs):
    *parts, _, out_ref = refs
    for e, part in enumerate(parts):
        out_ref[e] = part[...]


def join(parts, after):
    shape = jax.ShapeDtypeStruct((len(parts),) + parts[0].shape, parts[0].dtype)
    return call(join_kernel, shape, in_specs=[in_vmem] * len(parts) + [anywhere])(*parts, after)


def rows_update(turned_ref, rows_refs, switches, state, first):
    top, total_sum, totals = state
    across, _, columns = turned_ref.shape
    rows = rows_refs[0].shape[2]
    count = across * len(rows_refs)
    factor = log_two_e / math.sqrt(HD)
    keys = [kv_ref[:, 0].reshape(across * rows, HD) for kv_ref in rows_refs]
    values = [kv_ref[:, 1].reshape(across * rows, HD).T for kv_ref in rows_refs]
    logits = [
        [jnp.dot(part, turned_ref[e], preferred_element_type=jnp.float32) for part in keys]
        for e in range(across)
    ]
    if first:
        key_pos = lax.broadcasted_iota(jnp.int32, (rows, 1), 0)
        column = lax.broadcasted_iota(jnp.int32, (1, columns), 1)
        causal = key_pos <= lax.rem(column, rows)
    for e in range(across):
        blocks = [
            logits[e][b // across][b % across * rows : (b % across + 1) * rows] for b in range(count)
        ]
        if first:
            blocks[e] = jnp.where(causal, blocks[e], big_negative)
        new_top = None if first else top[e]
        for b in range(count):
            block_top = jnp.ceil(jnp.max(blocks[b], axis=0, keepdims=True) * factor)
            if switches[e][b] is not None:
                block_top = jnp.where(switches[e][b], block_top, big_negative)
            new_top = block_top if new_top is None else jnp.maximum(new_top, block_top)
        weights, block_sum = [], None
        for b in range(count):
            against = new_top
            if switches[e][b] is not None:
                against = jnp.where(switches[e][b], new_top, -big_negative)
            weights.append(jnp.exp2(blocks[b] * factor - against))
            part = jnp.sum(weights[b], axis=0, keepdims=True)
            block_sum = part if block_sum is None else block_sum + part
        update = None
        for i, part in enumerate(values):
            mine = weights[i * across : (i + 1) * across]
            mine = jnp.concatenate([w.astype(jnp.bfloat16) for w in mine], axis=0)
            part = jnp.dot(part, mine, preferred_element_type=jnp.float32)
            update = part if update is None else update + part
        if not first:
            rescale = jnp.exp2(top[e] - new_top)
            block_sum = total_sum[e] * rescale + block_sum
            update = totals[e] * rescale + update
        top[e] = new_top
        total_sum[e] = block_sum
        totals[e] = update


def switch_of(flags_ref, e, owner, columns, allowed=None):
    flag = flags_ref[e, pl.ds(jnp.maximum(owner, 0), 1), :]
    if allowed is not None:
        flag = flag * jnp.where(allowed, 1.0, 0.0)
    return jnp.concatenate([flag] * (columns // HD), axis=1) > 0.5


def first_kernel(across, turns, meta_ref, own_flags_ref, own_ref, *refs):
    queries, refs = refs[: across - 1], refs[across - 1 :]
    kv_ref, weight_ref, turned_ref, flags_ref, member_ref, inverse_ref, weight_out = refs[:7]
    state, rows_ref, copied = refs[7:10], refs[10], refs[11]
    weight_copy = pltpu.make_async_copy(weight_ref, weight_out, copied)
    weight_copy.start()
    z, y = place(across)
    q_rows = kv_ref.shape[2]
    repeat = own_ref.shape[1] // HD // across
    columns = repeat * q_rows
    for r in range(repeat):
        span = slice(r * q_rows, (r + 1) * q_rows)
        head = pl.multiple_of((y * repeat + r) * HD, HD)
        turned_ref[0, :, span] = own_ref[:, pl.ds(head, HD)].T
        for e in range(1, across):
            turned_ref[e, :, span] = queries[e - 1][0:q_rows, r * HD : (r + 1) * HD].T
    flags_ref[0] = own_flags_ref[...]
    for e in range(1, across):
        flags_ref[e] = queries[e - 1][q_rows:, 0:HD].astype(jnp.float32)
    owners = [block_at(z, y, e, across) for e in range(across)]
    switches = [
        [
            None if e == b else switch_of(flags_ref, e, owners[b], columns, owners[b] < owners[e])
            for b in range(across)
        ]
        for e in range(across)
    ]
    rows_update(turned_ref, [kv_ref], switches, state, True)

    column = lax.broadcasted_iota(jnp.int32, (1, columns), 1)
    for e in range(across):
        position = lax.rem(column, q_rows) + owners[e] * q_rows
        start = jnp.int32(0)
        for t in range(turns):
            length = meta_ref[1 + t]
            inside = (position >= start) & (position < start + length)
            rows_ref[t : t + 1, :] = jnp.where(inside, 1.0, 0.0)
            if e == 0:
                count = jnp.full((1, HD), length, jnp.int32).astype(jnp.float32)
                inverse_ref[t : t + 1, :] = 1.0 / count
            start = start + length
        for r in range(repeat):
            mine = (column >= r * q_rows) & (column < (r + 1) * q_rows)
            member_ref[e, r * turns : (r + 1) * turns, :] = jnp.where(
                mine, rows_ref[...], 0.0
            ).astype(jnp.bfloat16)
    weight_copy.wait()


def attend_first(across, turns, meta, flags, own, queries, rows, weight):
    q_rows = rows.shape[2]
    repeat = own.shape[1] // HD // across
    columns = repeat * q_rows
    f32, b16 = jnp.float32, jnp.bfloat16
    return call(
        functools.partial(first_kernel, across, turns),
        [
            jax.ShapeDtypeStruct((across, HD, columns), b16),
            jax.ShapeDtypeStruct((across,) + flags.shape, f32),
            jax.ShapeDtypeStruct((across, repeat * turns, columns), b16),
            jax.ShapeDtypeStruct((turns, HD), f32),
            jax.ShapeDtypeStruct(weight.shape, weight.dtype),
            jax.ShapeDtypeStruct((across, 1, columns), f32),
            jax.ShapeDtypeStruct((across, 1, columns), f32),
            jax.ShapeDtypeStruct((across, HD, columns), f32),
        ],
        in_specs=[in_smem] + [in_vmem] * (across + 2) + [anywhere],
        scratch_shapes=[pltpu.VMEM((turns, columns), f32), pltpu.SemaphoreType.DMA(())],
        limit=big_limit,
    )(meta, flags, own, *queries, rows, weight)


def next_kernel(across, down, distances, turns, last, flags_ref, turned_ref, *refs):
    state_at = len(distances) + (2 in distances)
    below, state, refs = refs[:state_at], refs[state_at : state_at + 3], refs[state_at + 3 :]
    z, y = place(across)
    columns = turned_ref.shape[2]

    def update(rows, from_distances):
        switches = [
            [
                switch_of(flags_ref, e, block_at(z - distance, y, b, across), columns)
                for distance in from_distances
                for b in range(across)
            ]
            for e in range(across)
        ]
        rows_update(turned_ref, rows, switches, state, False)

    for number, distance in enumerate(distances, 1):
        rows = below[:number]
        final = number == len(distances)
        here = (z >= distance) if final else (z == distance)
        if 2 not in distances:
            pl.when(here)(functools.partial(update, rows, distances[:number]))
            continue
        at = distances.index(2)
        relayed = rows[:at] + below[-1:] + rows[at + 1 :]
        most = down - 1 if final else distance
        if most >= down - 1:
            pl.when(here & (z == down - 1))(
                functools.partial(update, relayed, distances[:number])
            )
        if distance < down - 1:
            pl.when(here & (z < down - 1))(functools.partial(update, rows, distances[:number]))

    if last:
        member_ref, inverse_ref, out_ref = refs
        rows = out_ref.shape[1]
        pooled = None
        for e in range(across):
            attended = (state[2][e] / state[1][e]).astype(jnp.bfloat16)
            part = lax.dot_general(
                member_ref[e],
                attended,
                (((1,), (1,)), ((), ())),
                preferred_element_type=jnp.float32,
            )
            pooled = part if pooled is None else pooled + part
        for r in range(pooled.shape[0] // turns):
            mean = pooled[r * turns : (r + 1) * turns] * inverse_ref[...]
            for s in range(out_ref.shape[0]):
                out_ref[s, :, r * HD : (r + 1) * HD] = mean[s * rows : (s + 1) * rows]


def attend_next(across, down, distances, turns, turned, flags, below, state, pool, out_piece):
    last = pool is not None
    args = [flags, turned, *below, *state]
    if last:
        args += list(pool)
        out_shape, aliases = [jax.ShapeDtypeStruct(out_piece, jnp.float32)], {}
    else:
        out_shape = [jax.ShapeDtypeStruct(part.shape, part.dtype) for part in state]
        aliases = {2 + len(below) + i: i for i in range(len(state))}
    return call(
        functools.partial(next_kernel, across, down, distances, turns, last),
        out_shape,
        in_specs=[in_vmem] * len(args),
        input_output_aliases=aliases,
    )(*args)


def project_kernel(across, other, meta_ref, parts_ref, weight_ref, out_ref):
    side = 1 - meta_ref[0] if other else meta_ref[0]
    groups = []
    for y in range(across):
        total = parts_ref[y]
        for s in range(y + across, parts_ref.shape[0], across):
            total = total + parts_ref[s]
        groups.append(total)
    total = jnp.concatenate(groups, axis=1)
    rows = total.shape[0]
    high = total.astype(jnp.bfloat16)
    low = (total - high.astype(jnp.float32)).astype(jnp.bfloat16)
    both = jnp.concatenate([high, low], axis=0)
    half = out_ref.shape[1]
    step = math.gcd(half, 512)
    for c in range(half // step):
        start = pl.multiple_of(side * half + c * step, step)
        product = jnp.dot(
            both, weight_ref[:, pl.ds(start, step)], preferred_element_type=jnp.float32
        )
        out_ref[:, c * step : (c + 1) * step] = product[:rows] + product[rows:]


def project(across, other, meta, parts, weight):
    return call(
        functools.partial(project_kernel, across, other),
        jax.ShapeDtypeStruct((parts.shape[1], weight.shape[1] // 2), jnp.float32),
        in_specs=[in_smem, in_vmem, in_vmem],
    )(meta, parts, weight)


def on_device(count, queries, key_states, value_states, out_weight, turn_lengths, block_flags):
    across = key_states.shape[1] // HD
    down = count // across
    turns = turn_lengths.shape[0]

    def over(rows, shift):
        pairs = [(i, i - i % across + (i + shift) % across) for i in range(count)]
        return lax.ppermute(rows, "seq", pairs)

    def up(rows, distance, targets):
        pairs = [
            ((z - distance) * across + y, z * across + y)
            for z in targets
            if z >= distance
            for y in range(across)
        ]
        return lax.ppermute(rows, "seq", pairs)

    _, y = place(across)
    my_head = lax.axis_index("head").astype(jnp.int32)
    meta = jnp.concatenate([my_head[None], turn_lengths])
    heads = []
    for shift in range(across):
        at = lax.rem(y + shift, across)
        heads.append(pair(pick(key_states, at, across), pick(value_states, at, across)))
    padded = -(-count // 16) * 16
    flags = jnp.pad(block_flags[0], (0, padded - count))[:, None]
    sent = []
    for shift in range(1, across):
        group = pick(queries, lax.rem(y + shift, across), across)
        below = jnp.broadcast_to(flags, (padded, group.shape[1])).astype(group.dtype)
        sent.append(jnp.concatenate([group, below], axis=0))
    flags = jnp.broadcast_to(flags, (padded, HD)).astype(jnp.float32)
    others = [over(group, shift) for shift, group in enumerate(sent, 1)]
    rows = join([heads[0]] + [over(heads[shift], shift) for shift in range(1, across)], sent[0])
    below = [rows]
    for distance in range(1, down):
        below.append(up(rows, distance, range(down - 1 if distance == 2 else down)))
    relayed = up(below[1], 1, [down - 1])
    turned, flags, member, inverse, weight, *state = attend_first(
        across, turns, meta, flags, queries, others, rows, out_weight
    )
    out_piece = (count, turns // count, queries.shape[1] // across)
    stages = [[1]] + [list(range(d, min(d + 2, down))) for d in range(2, down, 2)]
    for distances in stages:
        last = distances == stages[-1]
        state = attend_next(
            across,
            down,
            distances,
            turns,
            turned,
            flags,
            [below[distance] for distance in distances] + ([relayed] if 2 in distances else []),
            state,
            (member, inverse) if last else None,
            out_piece,
        )
    parts = lax.all_to_all(state[0], "seq", split_axis=0, concat_axis=0, tiled=True)
    others = project(across, True, meta, parts, weight)
    others = lax.ppermute(others, "head", [(0, 1), (1, 0)])
    return project(across, False, meta, parts, weight) + others


def solution(mesh):
    in_specs = (
        P(("conv", "seq"), "head"),
        P(("conv", "seq"), "head"),
        P(("conv", "seq"), "head"),
        P("head", None),
        P("conv"),
        P(("conv", "seq"), None),
    )
    out_specs = P(("conv", "seq"), "head")
    return jax.shard_map(
        functools.partial(on_device, mesh.shape["seq"]),
        mesh=mesh,
        in_specs=in_specs,
        out_specs=out_specs,
        check_vma=False,
    )
```

```python
import functools
import math

import jax
import jax.numpy as jnp
from jax import lax
from jax.experimental import pallas as pl
from jax.experimental.pallas import tpu as pltpu
from jax.sharding import PartitionSpec as P

HD = 128

big_negative = -1e30
log_two_e = 1.4426950408889634

big_limit = 48 * 1024 * 1024
small_cost = pl.CostEstimate(flops=1024, bytes_accessed=1024, transcendentals=0)

in_vmem = pl.BlockSpec(memory_space=pltpu.VMEM)
in_smem = pl.BlockSpec(memory_space=pltpu.SMEM)
anywhere = pl.BlockSpec(memory_space=pl.ANY)


def place(across):
    index = lax.axis_index("seq")
    return index // across, lax.rem(index, across)


def block_at(z, y, e, across):
    return z * across + lax.rem(y - e + across, across)


def call(kernel, out_shape, **settings):
    limit = settings.pop("limit", 16 * 1024 * 1024)
    return pl.pallas_call(
        kernel,
        out_shape=out_shape,
        out_specs=jax.tree.map(lambda _: in_vmem, out_shape),
        compiler_params=pltpu.CompilerParams(vmem_limit_bytes=limit),
        cost_estimate=small_cost,
        **settings,
    )


def pick(rows, number, parts):
    width = rows.shape[1] // parts
    picked = rows[:, :width]
    for part in range(1, parts):
        picked = jnp.where(number == part, rows[:, part * width : (part + 1) * width], picked)
    return picked


def pair(keys, values):
    which = lax.broadcasted_iota(jnp.int32, (2,) + keys.shape, 0)
    return jnp.where(which == 0, keys[None], values[None])


def join_kernel(*refs):
    *parts, _, out_ref = refs
    for e, part in enumerate(parts):
        out_ref[e] = part[...]


def join(parts, after):
    shape = jax.ShapeDtypeStruct((len(parts),) + parts[0].shape, parts[0].dtype)
    return call(join_kernel, shape, in_specs=[in_vmem] * len(parts) + [anywhere])(*parts, after)


def rows_update(turned_ref, rows_refs, switches, state, first):
    top, total_sum, totals = state
    across, _, columns = turned_ref.shape
    rows = rows_refs[0].shape[2]
    count = across * len(rows_refs)
    factor = log_two_e / math.sqrt(HD)
    keys = [kv_ref[:, 0].reshape(across * rows, HD) for kv_ref in rows_refs]
    values = [kv_ref[:, 1].reshape(across * rows, HD).T for kv_ref in rows_refs]
    logits = [
        [jnp.dot(part, turned_ref[e], preferred_element_type=jnp.float32) for part in keys]
        for e in range(across)
    ]
    if first:
        key_pos = lax.broadcasted_iota(jnp.int32, (rows, 1), 0)
        column = lax.broadcasted_iota(jnp.int32, (1, columns), 1)
        causal = key_pos <= lax.rem(column, rows)
    for e in range(across):
        blocks = [
            logits[e][b // across][b % across * rows : (b % across + 1) * rows] for b in range(count)
        ]
        if first:
            blocks[e] = jnp.where(causal, blocks[e], big_negative)
        new_top = None if first else top[e]
        for b in range(count):
            block_top = jnp.ceil(jnp.max(blocks[b], axis=0, keepdims=True) * factor)
            if switches[e][b] is not None:
                block_top = jnp.where(switches[e][b], block_top, big_negative)
            new_top = block_top if new_top is None else jnp.maximum(new_top, block_top)
        weights, block_sum = [], None
        for b in range(count):
            against = new_top
            if switches[e][b] is not None:
                against = jnp.where(switches[e][b], new_top, -big_negative)
            weights.append(jnp.exp2(blocks[b] * factor - against))
            part = jnp.sum(weights[b], axis=0, keepdims=True)
            block_sum = part if block_sum is None else block_sum + part
        update = None
        for i, part in enumerate(values):
            mine = weights[i * across : (i + 1) * across]
            mine = jnp.concatenate([w.astype(jnp.bfloat16) for w in mine], axis=0)
            part = jnp.dot(part, mine, preferred_element_type=jnp.float32)
            update = part if update is None else update + part
        if not first:
            rescale = jnp.exp2(top[e] - new_top)
            block_sum = total_sum[e] * rescale + block_sum
            update = totals[e] * rescale + update
        top[e] = new_top
        total_sum[e] = block_sum
        totals[e] = update


def switch_of(flags_ref, e, owner, columns, allowed=None):
    flag = flags_ref[e, pl.ds(jnp.maximum(owner, 0), 1), :]
    if allowed is not None:
        flag = flag * jnp.where(allowed, 1.0, 0.0)
    return jnp.concatenate([flag] * (columns // HD), axis=1) > 0.5


def weight_piece(weight_ref, out_ref, start, sem):
    return pltpu.make_async_copy(weight_ref.at[start : start + out_ref.shape[0]], out_ref, sem)


def first_kernel(across, turns, meta_ref, own_flags_ref, *refs):
    queries, refs = refs[:across], refs[across:]
    kv_ref, weight_ref, turned_ref, flags_ref, member_ref, inverse_ref, weight_out = refs[:7]
    state, rows_ref, copied = refs[7:10], refs[10], refs[11]
    weight_copy = weight_piece(weight_ref, weight_out, 0, copied)
    weight_copy.start()
    z, y = place(across)
    q_rows = kv_ref.shape[2]
    repeat = queries[0].shape[1] // HD
    columns = repeat * q_rows
    for e in range(across):
        for r in range(repeat):
            turned_ref[e, :, r * q_rows : (r + 1) * q_rows] = queries[e][
                0:q_rows, r * HD : (r + 1) * HD
            ].T
    flags_ref[0] = own_flags_ref[...]
    for e in range(1, across):
        flags_ref[e] = queries[e][q_rows:, 0:HD].astype(jnp.float32)
    owners = [block_at(z, y, e, across) for e in range(across)]
    switches = [
        [
            None if e == b else switch_of(flags_ref, e, owners[b], columns, owners[b] < owners[e])
            for b in range(across)
        ]
        for e in range(across)
    ]
    rows_update(turned_ref, [kv_ref], switches, state, True)

    column = lax.broadcasted_iota(jnp.int32, (1, columns), 1)
    for e in range(across):
        position = lax.rem(column, q_rows) + owners[e] * q_rows
        start = jnp.int32(0)
        for t in range(turns):
            length = meta_ref[t]
            inside = (position >= start) & (position < start + length)
            rows_ref[t : t + 1, :] = jnp.where(inside, 1.0, 0.0)
            if e == 0:
                count = jnp.full((1, HD), length, jnp.int32).astype(jnp.float32)
                inverse_ref[t : t + 1, :] = 1.0 / count
            start = start + length
        for r in range(repeat):
            mine = (column >= r * q_rows) & (column < (r + 1) * q_rows)
            member_ref[e, r * turns : (r + 1) * turns, :] = jnp.where(
                mine, rows_ref[...], 0.0
            ).astype(jnp.bfloat16)
    weight_copy.wait()


def attend_first(across, turns, meta, flags, queries, rows, weight, piece):
    q_rows = rows.shape[2]
    repeat = queries[0].shape[1] // HD
    columns = repeat * q_rows
    f32, b16 = jnp.float32, jnp.bfloat16
    return call(
        functools.partial(first_kernel, across, turns),
        [
            jax.ShapeDtypeStruct((across, HD, columns), b16),
            jax.ShapeDtypeStruct((across,) + flags.shape, f32),
            jax.ShapeDtypeStruct((across, repeat * turns, columns), b16),
            jax.ShapeDtypeStruct((turns, HD), f32),
            jax.ShapeDtypeStruct((piece, weight.shape[1]), weight.dtype),
            jax.ShapeDtypeStruct((across, 1, columns), f32),
            jax.ShapeDtypeStruct((across, 1, columns), f32),
            jax.ShapeDtypeStruct((across, HD, columns), f32),
        ],
        in_specs=[in_smem] + [in_vmem] * (across + 2) + [anywhere],
        scratch_shapes=[pltpu.VMEM((turns, columns), f32), pltpu.SemaphoreType.DMA(())],
        limit=big_limit,
    )(meta, flags, *queries, rows, weight)


def next_kernel(across, down, distances, turns, last, weight_at, flags_ref, turned_ref, *refs):
    below_count = len(distances) + (1 in distances) + (2 in distances)
    below, state, refs = refs[:below_count], refs[below_count : below_count + 3], refs[below_count + 3 :]
    if weight_at is not None:
        weight_ref, weight_out, copied = refs[0], refs[-2], refs[-1]
        refs = refs[1:-2]
        weight_copy = weight_piece(weight_ref, weight_out, weight_at, copied)
        weight_copy.start()
    z, y = place(across)
    columns = turned_ref.shape[2]

    def update(rows, from_distances):
        switches = [
            [
                switch_of(flags_ref, e, block_at(z - distance, y, b, across), columns)
                for distance in from_distances
                for b in range(across)
            ]
            for e in range(across)
        ]
        rows_update(turned_ref, rows, switches, state, False)

    def when(here, rows, number):
        pl.when(here)(functools.partial(update, rows, distances[:number]))

    for number, distance in enumerate(distances, 1):
        rows = below[:number]
        final = number == len(distances)
        here = (z >= distance) if final else (z == distance)
        if distances == [1]:
            even = lax.rem(z, 2) == 0
            when(here & even, below[:1], number)
            when(here & jnp.logical_not(even), below[1:], number)
        elif 2 in distances:
            at = distances.index(2)
            if final or distance == down - 1:
                when(here & (z == down - 1), rows[:at] + below[-1:] + rows[at + 1 :], number)
            if distance < down - 1:
                when(here & (z < down - 1), rows, number)
        else:
            when(here, rows, number)

    if weight_at is not None:
        weight_copy.wait()
    if last:
        member_ref, inverse_ref, out_ref = refs
        rows = out_ref.shape[1]
        pooled = None
        for e in range(across):
            attended = (state[2][e] / state[1][e]).astype(jnp.bfloat16)
            part = lax.dot_general(
                member_ref[e],
                attended,
                (((1,), (1,)), ((), ())),
                preferred_element_type=jnp.float32,
            )
            pooled = part if pooled is None else pooled + part
        for r in range(pooled.shape[0] // turns):
            mean = pooled[r * turns : (r + 1) * turns] * inverse_ref[...]
            for s in range(out_ref.shape[0]):
                out_ref[s, :, r * HD : (r + 1) * HD] = mean[s * rows : (s + 1) * rows]


def attend_next(across, down, distances, turns, turned, flags, below, state, pool, out_piece, weight, at, piece):
    last = pool is not None
    args = [flags, turned, *below, *state]
    in_specs = [in_vmem] * len(args)
    aliases, scratch = {}, []
    if at is not None:
        args.append(weight)
        in_specs.append(anywhere)
        scratch = [pltpu.SemaphoreType.DMA(())]
    if last:
        args += list(pool)
        in_specs += [in_vmem] * len(pool)
        out_shape = [jax.ShapeDtypeStruct(out_piece, jnp.float32)]
    else:
        out_shape = [jax.ShapeDtypeStruct(part.shape, part.dtype) for part in state]
        aliases = {2 + len(below) + i: i for i in range(len(state))}
    if at is not None:
        out_shape.append(jax.ShapeDtypeStruct((piece, weight.shape[1]), weight.dtype))
    return call(
        functools.partial(next_kernel, across, down, distances, turns, last, at),
        out_shape,
        in_specs=in_specs,
        scratch_shapes=scratch,
        input_output_aliases=aliases,
        limit=big_limit if at is not None else 16 * 1024 * 1024,
    )(*args)


def project_kernel(across, other, parts_ref, *refs):
    weights, out_ref = refs[:-1], refs[-1]
    side = lax.axis_index("head")
    if other:
        side = 1 - side
    groups = []
    for y in range(across):
        total = parts_ref[y]
        for s in range(y + across, parts_ref.shape[0], across):
            total = total + parts_ref[s]
        groups.append(total)
    total = jnp.concatenate(groups, axis=1)
    rows = total.shape[0]
    high = total.astype(jnp.bfloat16)
    low = (total - high.astype(jnp.float32)).astype(jnp.bfloat16)
    both = jnp.concatenate([high, low], axis=0)
    half = out_ref.shape[1]
    step = math.gcd(half, 512)
    for c in range(half // step):
        start = pl.multiple_of(side * half + c * step, step)
        product, at = None, 0
        for weight_ref in weights:
            depth = weight_ref.shape[0]
            part = jnp.dot(
                both[:, at : at + depth],
                weight_ref[:, pl.ds(start, step)],
                preferred_element_type=jnp.float32,
            )
            product = part if product is None else product + part
            at += depth
        out_ref[:, c * step : (c + 1) * step] = product[:rows] + product[rows:]


def project(across, other, parts, weights):
    return call(
        functools.partial(project_kernel, across, other),
        jax.ShapeDtypeStruct((parts.shape[1], weights[0].shape[1] // 2), jnp.float32),
        in_specs=[in_vmem] * (1 + len(weights)),
    )(parts, *weights)


def on_device(count, queries, key_states, value_states, out_weight, turn_lengths, block_flags):
    across = key_states.shape[1] // HD
    down = count // across
    turns = turn_lengths.shape[0]

    def over(rows, shift):
        pairs = [(i, i - i % across + (i + shift) % across) for i in range(count)]
        return lax.ppermute(rows, "seq", pairs)

    def up(rows, distance, targets):
        pairs = [
            ((z - distance) * across + y, z * across + y)
            for z in targets
            if z >= distance
            for y in range(across)
        ]
        return lax.ppermute(rows, "seq", pairs)

    _, y = place(across)
    heads = []
    for shift in range(across):
        at = lax.rem(y + shift, across)
        heads.append(pair(pick(key_states, at, across), pick(value_states, at, across)))
    meta = lax.optimization_barrier(jnp.concatenate([turn_lengths, block_flags[0]]))
    padded = -(-count // 16) * 16
    flags = jnp.pad(meta[turns:], (0, padded - count))[:, None]
    groups = [pick(queries, lax.rem(y + shift, across), across) for shift in range(across)]
    sent = []
    for group in groups[1:]:
        under = jnp.broadcast_to(flags, (padded, group.shape[1])).astype(group.dtype)
        sent.append(jnp.concatenate([group, under], axis=0))
    flags = jnp.broadcast_to(flags, (padded, HD)).astype(jnp.float32)
    others = [over(group, shift) for shift, group in enumerate(sent, 1)]
    rows = join([heads[0]] + [over(heads[shift], shift) for shift in range(1, across)], sent[0])
    nearest = [up(rows, 1, range(parity, down, 2)) for parity in (0, 1)]
    farther = [
        up(rows, distance, range(down - 1 if distance == 2 else down))
        for distance in range(2, down)
    ]
    through = (down - 2) % 2
    *nearest, = lax.optimization_barrier((*nearest, *others))
    nearest, others = nearest[:2], nearest[2:]
    relayed = up(nearest[through], 1, [down - 1])
    depth = out_weight.shape[0]
    pieces = [3 * depth // 8, 2 * depth // 8, 3 * depth // 8]
    turned, flags, member, inverse, weight, *state = attend_first(
        across, turns, meta, flags, [groups[0], *others], rows, out_weight, pieces[0]
    )
    weights = [weight]
    out_piece = (count, turns // count, queries.shape[1] // across)
    stages = [[1]] + [list(range(d, min(d + 2, down))) for d in range(2, down, 2)]
    for number, distances in enumerate(stages):
        last = number == len(stages) - 1
        if number == 0:
            below = nearest
        else:
            below = [farther[distance - 2] for distance in distances]
            if 2 in distances:
                below.append(relayed)
        with_weight = last or number == 0
        state = attend_next(
            across,
            down,
            distances,
            turns,
            turned,
            flags,
            below,
            state,
            (member, inverse) if last else None,
            out_piece,
            out_weight,
            sum(pieces[: len(weights)]) if with_weight else None,
            pieces[len(weights)] if with_weight else None,
        )
        if with_weight:
            *state, weight = state
            weights.append(weight)
    parts = lax.all_to_all(state[0], "seq", split_axis=0, concat_axis=0, tiled=True)
    theirs = project(across, True, parts, weights)
    theirs = lax.ppermute(theirs, "head", [(0, 1), (1, 0)])
    return project(across, False, parts, weights) + theirs


def solution(mesh):
    in_specs = (
        P(("conv", "seq"), "head"),
        P(("conv", "seq"), "head"),
        P(("conv", "seq"), "head"),
        P("head", None),
        P("conv"),
        P(("conv", "seq"), None),
    )
    out_specs = P(("conv", "seq"), "head")
    return jax.shard_map(
        functools.partial(on_device, mesh.shape["seq"]),
        mesh=mesh,
        in_specs=in_specs,
        out_specs=out_specs,
        check_vma=False,
    )
```

```python
import functools
import math

import jax
import jax.numpy as jnp
from jax import lax
from jax.experimental import pallas as pl
from jax.experimental.pallas import tpu as pltpu
from jax.sharding import PartitionSpec as P

HD = 128

big_negative = -1e30
log_two_e = 1.4426950408889634

big_limit = 45 * 1024 * 1024
small_cost = pl.CostEstimate(flops=1024, bytes_accessed=1024, transcendentals=0)

in_vmem = pl.BlockSpec(memory_space=pltpu.VMEM)
in_smem = pl.BlockSpec(memory_space=pltpu.SMEM)
anywhere = pl.BlockSpec(memory_space=pl.ANY)


def place(across):
    index = lax.axis_index("seq")
    return index // across, lax.rem(index, across)


def block_at(z, y, e, across):
    return z * across + lax.rem(y - e + across, across)


def call(kernel, out_shape, **settings):
    limit = settings.pop("limit", 16 * 1024 * 1024)
    return pl.pallas_call(
        kernel,
        out_shape=out_shape,
        out_specs=jax.tree.map(lambda _: in_vmem, out_shape),
        compiler_params=pltpu.CompilerParams(vmem_limit_bytes=limit),
        cost_estimate=small_cost,
        **settings,
    )


def pick(rows, number, parts):
    width = rows.shape[1] // parts
    picked = rows[:, :width]
    for part in range(1, parts):
        picked = jnp.where(number == part, rows[:, part * width : (part + 1) * width], picked)
    return picked


def pair(keys, values):
    which = lax.broadcasted_iota(jnp.int32, (2,) + keys.shape, 0)
    return jnp.where(which == 0, keys[None], values[None])


def join_kernel(*refs):
    *parts, _, out_ref = refs
    for e, part in enumerate(parts):
        out_ref[e] = part[...]


def join(parts, after):
    shape = jax.ShapeDtypeStruct((len(parts),) + parts[0].shape, parts[0].dtype)
    return call(join_kernel, shape, in_specs=[in_vmem] * len(parts) + [anywhere])(*parts, after)


def rows_update(turned_ref, rows_refs, switches, state, first):
    top, total_sum, totals = state
    across, _, columns = turned_ref.shape
    rows = rows_refs[0].shape[2]
    count = across * len(rows_refs)
    factor = log_two_e / math.sqrt(HD)
    keys = [kv_ref[:, 0].reshape(across * rows, HD) for kv_ref in rows_refs]
    values = [kv_ref[:, 1].reshape(across * rows, HD).T for kv_ref in rows_refs]
    logits = [
        [jnp.dot(part, turned_ref[e], preferred_element_type=jnp.float32) for part in keys]
        for e in range(across)
    ]
    if first:
        key_pos = lax.broadcasted_iota(jnp.int32, (rows, 1), 0)
        column = lax.broadcasted_iota(jnp.int32, (1, columns), 1)
        causal = key_pos <= lax.rem(column, rows)
    for e in range(across):
        blocks = [
            logits[e][b // across][b % across * rows : (b % across + 1) * rows] for b in range(count)
        ]
        if first:
            blocks[e] = jnp.where(causal, blocks[e], big_negative)
        new_top = None if first else top[e]
        for b in range(count):
            block_top = jnp.ceil(jnp.max(blocks[b], axis=0, keepdims=True) * factor)
            if switches[e][b] is not None:
                block_top = jnp.where(switches[e][b], block_top, big_negative)
            new_top = block_top if new_top is None else jnp.maximum(new_top, block_top)
        weights, block_sum = [], None
        for b in range(count):
            against = new_top
            if switches[e][b] is not None:
                against = jnp.where(switches[e][b], new_top, -big_negative)
            weights.append(jnp.exp2(blocks[b] * factor - against))
            part = jnp.sum(weights[b], axis=0, keepdims=True)
            block_sum = part if block_sum is None else block_sum + part
        update = None
        for i, part in enumerate(values):
            mine = weights[i * across : (i + 1) * across]
            mine = jnp.concatenate([w.astype(jnp.bfloat16) for w in mine], axis=0)
            part = jnp.dot(part, mine, preferred_element_type=jnp.float32)
            update = part if update is None else update + part
        if not first:
            rescale = jnp.exp2(top[e] - new_top)
            block_sum = total_sum[e] * rescale + block_sum
            update = totals[e] * rescale + update
        top[e] = new_top
        total_sum[e] = block_sum
        totals[e] = update


def switch_of(flags_ref, e, owner, columns, allowed=None):
    flag = flags_ref[e, pl.ds(jnp.maximum(owner, 0), 1), :]
    if allowed is not None:
        flag = flag * jnp.where(allowed, 1.0, 0.0)
    return jnp.concatenate([flag] * (columns // HD), axis=1) > 0.5


def weight_piece(weight_ref, out_ref, start, sem):
    return pltpu.make_async_copy(weight_ref.at[start : start + out_ref.shape[0]], out_ref, sem)


def first_kernel(across, turns, meta_ref, own_flags_ref, *refs):
    queries, refs = refs[:across], refs[across:]
    kv_ref, weight_ref, turned_ref, flags_ref, member_ref, inverse_ref, weight_out = refs[:7]
    state, rows_ref, copied = refs[7:10], refs[10], refs[11]
    weight_copy = weight_piece(weight_ref, weight_out, 0, copied)
    weight_copy.start()
    z, y = place(across)
    q_rows = kv_ref.shape[2]
    repeat = queries[0].shape[1] // HD
    columns = repeat * q_rows
    for e in range(across):
        for r in range(repeat):
            turned_ref[e, :, r * q_rows : (r + 1) * q_rows] = queries[e][
                0:q_rows, r * HD : (r + 1) * HD
            ].T
    flags_ref[0] = own_flags_ref[...]
    for e in range(1, across):
        flags_ref[e] = queries[e][q_rows:, 0:HD].astype(jnp.float32)
    owners = [block_at(z, y, e, across) for e in range(across)]
    switches = [
        [
            None if e == b else switch_of(flags_ref, e, owners[b], columns, owners[b] < owners[e])
            for b in range(across)
        ]
        for e in range(across)
    ]
    rows_update(turned_ref, [kv_ref], switches, state, True)

    column = lax.broadcasted_iota(jnp.int32, (1, columns), 1)
    for e in range(across):
        position = lax.rem(column, q_rows) + owners[e] * q_rows
        start = jnp.int32(0)
        for t in range(turns):
            length = meta_ref[t]
            inside = (position >= start) & (position < start + length)
            rows_ref[t : t + 1, :] = jnp.where(inside, 1.0, 0.0)
            if e == 0:
                count = jnp.full((1, HD), length, jnp.int32).astype(jnp.float32)
                inverse_ref[t : t + 1, :] = 1.0 / count
            start = start + length
        for r in range(repeat):
            mine = (column >= r * q_rows) & (column < (r + 1) * q_rows)
            member_ref[e, r * turns : (r + 1) * turns, :] = jnp.where(
                mine, rows_ref[...], 0.0
            ).astype(jnp.bfloat16)
    weight_copy.wait()


def attend_first(across, turns, meta, flags, queries, rows, weight, piece):
    q_rows = rows.shape[2]
    repeat = queries[0].shape[1] // HD
    columns = repeat * q_rows
    f32, b16 = jnp.float32, jnp.bfloat16
    return call(
        functools.partial(first_kernel, across, turns),
        [
            jax.ShapeDtypeStruct((across, HD, columns), b16),
            jax.ShapeDtypeStruct((across,) + flags.shape, f32),
            jax.ShapeDtypeStruct((across, repeat * turns, columns), b16),
            jax.ShapeDtypeStruct((turns, HD), f32),
            jax.ShapeDtypeStruct((piece, weight.shape[1]), weight.dtype),
            jax.ShapeDtypeStruct((across, 1, columns), f32),
            jax.ShapeDtypeStruct((across, 1, columns), f32),
            jax.ShapeDtypeStruct((across, HD, columns), f32),
        ],
        in_specs=[in_smem] + [in_vmem] * (across + 2) + [anywhere],
        scratch_shapes=[pltpu.VMEM((turns, columns), f32), pltpu.SemaphoreType.DMA(())],
        limit=big_limit,
    )(meta, flags, *queries, rows, weight)


def next_kernel(across, down, distances, turns, last, weight_at, flags_ref, turned_ref, *refs):
    below_count = len(distances) + (2 in distances)
    below, state, refs = refs[:below_count], refs[below_count : below_count + 3], refs[below_count + 3 :]
    if weight_at is not None:
        weight_ref, weight_out, copied = refs[0], refs[-2], refs[-1]
        refs = refs[1:-2]
        weight_copy = weight_piece(weight_ref, weight_out, weight_at, copied)
        weight_copy.start()
    z, y = place(across)
    columns = turned_ref.shape[2]

    def update(rows, from_distances):
        switches = [
            [
                switch_of(flags_ref, e, block_at(z - distance, y, b, across), columns)
                for distance in from_distances
                for b in range(across)
            ]
            for e in range(across)
        ]
        rows_update(turned_ref, rows, switches, state, False)

    def when(here, rows, number):
        pl.when(here)(functools.partial(update, rows, distances[:number]))

    for number, distance in enumerate(distances, 1):
        rows = below[:number]
        final = number == len(distances)
        here = (z >= distance) if final else (z == distance)
        if 2 in distances:
            at = distances.index(2)
            if final or distance == down - 1:
                when(here & (z == down - 1), rows[:at] + below[-1:] + rows[at + 1 :], number)
            if distance < down - 1:
                when(here & (z < down - 1), rows, number)
        else:
            when(here, rows, number)

    if weight_at is not None:
        weight_copy.wait()
    if last:
        member_ref, inverse_ref, out_ref = refs
        rows = out_ref.shape[1]
        pooled = None
        for e in range(across):
            attended = (state[2][e] / state[1][e]).astype(jnp.bfloat16)
            part = lax.dot_general(
                member_ref[e],
                attended,
                (((1,), (1,)), ((), ())),
                preferred_element_type=jnp.float32,
            )
            pooled = part if pooled is None else pooled + part
        for r in range(pooled.shape[0] // turns):
            mean = pooled[r * turns : (r + 1) * turns] * inverse_ref[...]
            for s in range(out_ref.shape[0]):
                out_ref[s, :, r * HD : (r + 1) * HD] = mean[s * rows : (s + 1) * rows]


def attend_next(across, down, distances, turns, turned, flags, below, state, pool, out_piece, weight, at, piece):
    last = pool is not None
    args = [flags, turned, *below, *state]
    in_specs = [in_vmem] * len(args)
    aliases, scratch = {}, []
    if at is not None:
        args.append(weight)
        in_specs.append(anywhere)
        scratch = [pltpu.SemaphoreType.DMA(())]
    if last:
        args += list(pool)
        in_specs += [in_vmem] * len(pool)
        out_shape = [jax.ShapeDtypeStruct(out_piece, jnp.float32)]
    else:
        out_shape = [jax.ShapeDtypeStruct(part.shape, part.dtype) for part in state]
        aliases = {2 + len(below) + i: i for i in range(len(state))}
    if at is not None:
        out_shape.append(jax.ShapeDtypeStruct((piece, weight.shape[1]), weight.dtype))
    return call(
        functools.partial(next_kernel, across, down, distances, turns, last, at),
        out_shape,
        in_specs=in_specs,
        scratch_shapes=scratch,
        input_output_aliases=aliases,
        limit=big_limit if at is not None else 16 * 1024 * 1024,
    )(*args)


def project_kernel(across, other, parts_ref, *refs):
    weights, out_ref = refs[:-1], refs[-1]
    side = lax.axis_index("head")
    if other:
        side = 1 - side
    groups = []
    for y in range(across):
        total = parts_ref[y]
        for s in range(y + across, parts_ref.shape[0], across):
            total = total + parts_ref[s]
        groups.append(total)
    total = jnp.concatenate(groups, axis=1)
    rows = total.shape[0]
    high = total.astype(jnp.bfloat16)
    low = (total - high.astype(jnp.float32)).astype(jnp.bfloat16)
    both = jnp.concatenate([high, low], axis=0)
    half = out_ref.shape[1]
    step = math.gcd(half, 512)
    for c in range(half // step):
        start = pl.multiple_of(side * half + c * step, step)
        product, at = None, 0
        for weight_ref in weights:
            depth = weight_ref.shape[0]
            part = jnp.dot(
                both[:, at : at + depth],
                weight_ref[:, pl.ds(start, step)],
                preferred_element_type=jnp.float32,
            )
            product = part if product is None else product + part
            at += depth
        out_ref[:, c * step : (c + 1) * step] = product[:rows] + product[rows:]


def project(across, other, parts, weights):
    return call(
        functools.partial(project_kernel, across, other),
        jax.ShapeDtypeStruct((parts.shape[1], weights[0].shape[1] // 2), jnp.float32),
        in_specs=[in_vmem] * (1 + len(weights)),
    )(parts, *weights)


def on_device(count, queries, key_states, value_states, out_weight, turn_lengths, block_flags):
    across = key_states.shape[1] // HD
    down = count // across
    turns = turn_lengths.shape[0]

    def over(rows, shift):
        pairs = [(i, i - i % across + (i + shift) % across) for i in range(count)]
        return lax.ppermute(rows, "seq", pairs)

    def up(rows, distance, targets):
        pairs = [
            ((z - distance) * across + y, z * across + y)
            for z in targets
            if z >= distance
            for y in range(across)
        ]
        return lax.ppermute(rows, "seq", pairs)

    _, y = place(across)
    heads = []
    for shift in range(across):
        at = lax.rem(y + shift, across)
        heads.append(pair(pick(key_states, at, across), pick(value_states, at, across)))
    meta = lax.optimization_barrier(jnp.concatenate([turn_lengths, block_flags[0]]))
    padded = -(-count // 16) * 16
    flags = jnp.pad(meta[turns:], (0, padded - count))[:, None]
    groups = [pick(queries, lax.rem(y + shift, across), across) for shift in range(across)]
    sent = []
    for group in groups[1:]:
        under = jnp.broadcast_to(flags, (padded, group.shape[1])).astype(group.dtype)
        sent.append(jnp.concatenate([group, under], axis=0))
    flags = jnp.broadcast_to(flags, (padded, HD)).astype(jnp.float32)
    others = [over(group, shift) for shift, group in enumerate(sent, 1)]
    rows = join([heads[0]] + [over(heads[shift], shift) for shift in range(1, across)], sent[0])
    nearest = up(rows, 1, range(down))
    farther = [
        up(rows, distance, range(down - 1 if distance == 2 else down))
        for distance in range(2, down)
    ]
    nearest, *others = lax.optimization_barrier((nearest, *others))
    relayed = up(nearest, 1, [down - 1])
    depth = out_weight.shape[0]
    pieces = [4 * depth // 8, 2 * depth // 8, 2 * depth // 8]
    turned, flags, member, inverse, weight, *state = attend_first(
        across, turns, meta, flags, [groups[0], *others], rows, out_weight, pieces[0]
    )
    weights = [weight]
    out_piece = (count, turns // count, queries.shape[1] // across)
    stages = [[1]] + [list(range(d, min(d + 2, down))) for d in range(2, down, 2)]
    for number, distances in enumerate(stages):
        last = number == len(stages) - 1
        if number == 0:
            below = [nearest]
        else:
            below = [farther[distance - 2] for distance in distances]
            if 2 in distances:
                below.append(relayed)
        with_weight = last or number == 0
        state = attend_next(
            across,
            down,
            distances,
            turns,
            turned,
            flags,
            below,
            state,
            (member, inverse) if last else None,
            out_piece,
            out_weight,
            sum(pieces[: len(weights)]) if with_weight else None,
            pieces[len(weights)] if with_weight else None,
        )
        if with_weight:
            *state, weight = state
            weights.append(weight)
    parts = lax.all_to_all(state[0], "seq", split_axis=0, concat_axis=0, tiled=True)
    theirs = project(across, True, parts, weights)
    theirs = lax.ppermute(theirs, "head", [(0, 1), (1, 0)])
    return project(across, False, parts, weights) + theirs


def solution(mesh):
    in_specs = (
        P(("conv", "seq"), "head"),
        P(("conv", "seq"), "head"),
        P(("conv", "seq"), "head"),
        P("head", None),
        P("conv"),
        P(("conv", "seq"), None),
    )
    out_specs = P(("conv", "seq"), "head")
    return jax.shard_map(
        functools.partial(on_device, mesh.shape["seq"]),
        mesh=mesh,
        in_specs=in_specs,
        out_specs=out_specs,
        check_vma=False,
    )
```

```python
import functools
import math

import jax
import jax.numpy as jnp
from jax import lax
from jax.experimental import pallas as pl
from jax.experimental.pallas import tpu as pltpu
from jax.sharding import PartitionSpec as P

HD = 128

big_negative = -1e30
log_two_e = 1.4426950408889634

big_limit = 45 * 1024 * 1024
small_cost = pl.CostEstimate(flops=1024, bytes_accessed=1024, transcendentals=0)

in_vmem = pl.BlockSpec(memory_space=pltpu.VMEM)
in_smem = pl.BlockSpec(memory_space=pltpu.SMEM)
anywhere = pl.BlockSpec(memory_space=pl.ANY)


def place(across):
    index = lax.axis_index("seq")
    return index // across, lax.rem(index, across)


def block_at(z, y, e, across):
    return z * across + lax.rem(y - e + across, across)


def call(kernel, out_shape, **settings):
    limit = settings.pop("limit", 16 * 1024 * 1024)
    return pl.pallas_call(
        kernel,
        out_shape=out_shape,
        out_specs=jax.tree.map(lambda _: in_vmem, out_shape),
        compiler_params=pltpu.CompilerParams(vmem_limit_bytes=limit),
        cost_estimate=small_cost,
        **settings,
    )


def pick(rows, number, parts):
    width = rows.shape[1] // parts
    picked = rows[:, :width]
    for part in range(1, parts):
        picked = jnp.where(number == part, rows[:, part * width : (part + 1) * width], picked)
    return picked


def pair(keys, values):
    which = lax.broadcasted_iota(jnp.int32, (2,) + keys.shape, 0)
    return jnp.where(which == 0, keys[None], values[None])


def join_kernel(*refs):
    *parts, _, out_ref = refs
    for e, part in enumerate(parts):
        out_ref[e] = part[...]


def join(parts, after):
    shape = jax.ShapeDtypeStruct((len(parts),) + parts[0].shape, parts[0].dtype)
    return call(join_kernel, shape, in_specs=[in_vmem] * len(parts) + [anywhere])(*parts, after)


def rows_update(turned_ref, rows_refs, switches, state, first):
    top, total_sum, totals = state
    across, _, columns = turned_ref.shape
    rows = rows_refs[0].shape[2]
    count = across * len(rows_refs)
    factor = log_two_e / math.sqrt(HD)
    keys = [kv_ref[:, 0].reshape(across * rows, HD) for kv_ref in rows_refs]
    values = [kv_ref[:, 1].reshape(across * rows, HD).T for kv_ref in rows_refs]
    logits = [
        [jnp.dot(part, turned_ref[e], preferred_element_type=jnp.float32) for part in keys]
        for e in range(across)
    ]
    if first:
        key_pos = lax.broadcasted_iota(jnp.int32, (rows, 1), 0)
        column = lax.broadcasted_iota(jnp.int32, (1, columns), 1)
        causal = key_pos <= lax.rem(column, rows)
    for e in range(across):
        blocks = [
            logits[e][b // across][b % across * rows : (b % across + 1) * rows] for b in range(count)
        ]
        if first:
            blocks[e] = jnp.where(causal, blocks[e], big_negative)
        new_top = None if first else top[e]
        for b in range(count):
            block_top = jnp.ceil(jnp.max(blocks[b], axis=0, keepdims=True) * factor)
            if switches[e][b] is not None:
                block_top = jnp.where(switches[e][b], block_top, big_negative)
            new_top = block_top if new_top is None else jnp.maximum(new_top, block_top)
        weights, block_sum = [], None
        for b in range(count):
            against = new_top
            if switches[e][b] is not None:
                against = jnp.where(switches[e][b], new_top, -big_negative)
            weights.append(jnp.exp2(blocks[b] * factor - against))
            part = jnp.sum(weights[b], axis=0, keepdims=True)
            block_sum = part if block_sum is None else block_sum + part
        update = None
        for i, part in enumerate(values):
            mine = weights[i * across : (i + 1) * across]
            mine = jnp.concatenate([w.astype(jnp.bfloat16) for w in mine], axis=0)
            part = jnp.dot(part, mine, preferred_element_type=jnp.float32)
            update = part if update is None else update + part
        if not first:
            rescale = jnp.exp2(top[e] - new_top)
            block_sum = total_sum[e] * rescale + block_sum
            update = totals[e] * rescale + update
        top[e] = new_top
        total_sum[e] = block_sum
        totals[e] = update


def switch_of(flags_ref, e, owner, columns, allowed=None):
    flag = flags_ref[e, pl.ds(jnp.maximum(owner, 0), 1), :]
    if allowed is not None:
        flag = flag * jnp.where(allowed, 1.0, 0.0)
    return jnp.concatenate([flag] * (columns // HD), axis=1) > 0.5


def weight_piece(weight_ref, out_ref, start, sem):
    return pltpu.make_async_copy(weight_ref.at[start : start + out_ref.shape[0]], out_ref, sem)


def first_kernel(across, turns, meta_ref, own_flags_ref, *refs):
    queries, refs = refs[:across], refs[across:]
    kv_ref, weight_ref, turned_ref, flags_ref, member_ref, inverse_ref, weight_out = refs[:7]
    state, rows_ref, copied = refs[7:10], refs[10], refs[11]
    weight_copy = weight_piece(weight_ref, weight_out, 0, copied)
    weight_copy.start()
    z, y = place(across)
    q_rows = kv_ref.shape[2]
    repeat = queries[0].shape[1] // HD
    columns = repeat * q_rows
    for e in range(across):
        for r in range(repeat):
            turned_ref[e, :, r * q_rows : (r + 1) * q_rows] = queries[e][
                0:q_rows, r * HD : (r + 1) * HD
            ].T
    flags_ref[0] = own_flags_ref[...]
    for e in range(1, across):
        flags_ref[e] = queries[e][q_rows:, 0:HD].astype(jnp.float32)
    owners = [block_at(z, y, e, across) for e in range(across)]
    switches = [
        [
            None if e == b else switch_of(flags_ref, e, owners[b], columns, owners[b] < owners[e])
            for b in range(across)
        ]
        for e in range(across)
    ]
    rows_update(turned_ref, [kv_ref], switches, state, True)

    column = lax.broadcasted_iota(jnp.int32, (1, columns), 1)
    for e in range(across):
        position = lax.rem(column, q_rows) + owners[e] * q_rows
        start = jnp.int32(0)
        for t in range(turns):
            length = meta_ref[t]
            inside = (position >= start) & (position < start + length)
            rows_ref[t : t + 1, :] = jnp.where(inside, 1.0, 0.0)
            if e == 0:
                count = jnp.full((1, HD), length, jnp.int32).astype(jnp.float32)
                inverse_ref[t : t + 1, :] = 1.0 / count
            start = start + length
        for r in range(repeat):
            mine = (column >= r * q_rows) & (column < (r + 1) * q_rows)
            member_ref[e, r * turns : (r + 1) * turns, :] = jnp.where(
                mine, rows_ref[...], 0.0
            ).astype(jnp.bfloat16)
    weight_copy.wait()


def attend_first(across, turns, meta, flags, queries, rows, weight, piece):
    q_rows = rows.shape[2]
    repeat = queries[0].shape[1] // HD
    columns = repeat * q_rows
    f32, b16 = jnp.float32, jnp.bfloat16
    return call(
        functools.partial(first_kernel, across, turns),
        [
            jax.ShapeDtypeStruct((across, HD, columns), b16),
            jax.ShapeDtypeStruct((across,) + flags.shape, f32),
            jax.ShapeDtypeStruct((across, repeat * turns, columns), b16),
            jax.ShapeDtypeStruct((turns, HD), f32),
            jax.ShapeDtypeStruct((piece, weight.shape[1]), weight.dtype),
            jax.ShapeDtypeStruct((across, 1, columns), f32),
            jax.ShapeDtypeStruct((across, 1, columns), f32),
            jax.ShapeDtypeStruct((across, HD, columns), f32),
        ],
        in_specs=[in_smem] + [in_vmem] * (across + 2) + [anywhere],
        scratch_shapes=[pltpu.VMEM((turns, columns), f32), pltpu.SemaphoreType.DMA(())],
        limit=big_limit,
    )(meta, flags, *queries, rows, weight)


def next_kernel(across, distances, turns, last, weight_at, flags_ref, turned_ref, *refs):
    below_count = len(distances)
    below, state, refs = refs[:below_count], refs[below_count : below_count + 3], refs[below_count + 3 :]
    if weight_at is not None:
        weight_ref, weight_out, copied = refs[0], refs[-2], refs[-1]
        refs = refs[1:-2]
        weight_copy = weight_piece(weight_ref, weight_out, weight_at, copied)
        weight_copy.start()
    z, y = place(across)
    columns = turned_ref.shape[2]

    def update(rows, from_distances):
        switches = [
            [
                switch_of(flags_ref, e, block_at(z - distance, y, b, across), columns)
                for distance in from_distances
                for b in range(across)
            ]
            for e in range(across)
        ]
        rows_update(turned_ref, rows, switches, state, False)

    for number, distance in enumerate(distances, 1):
        here = (z >= distance) if number == len(distances) else (z == distance)
        pl.when(here)(functools.partial(update, below[:number], distances[:number]))

    if weight_at is not None:
        weight_copy.wait()
    if last:
        member_ref, inverse_ref, out_ref = refs
        rows = out_ref.shape[1]
        pooled = None
        for e in range(across):
            attended = (state[2][e] / state[1][e]).astype(jnp.bfloat16)
            part = lax.dot_general(
                member_ref[e],
                attended,
                (((1,), (1,)), ((), ())),
                preferred_element_type=jnp.float32,
            )
            pooled = part if pooled is None else pooled + part
        for r in range(pooled.shape[0] // turns):
            mean = pooled[r * turns : (r + 1) * turns] * inverse_ref[...]
            for s in range(out_ref.shape[0]):
                out_ref[s, :, r * HD : (r + 1) * HD] = mean[s * rows : (s + 1) * rows]


def attend_next(across, distances, turns, turned, flags, below, state, pool, out_piece, weight, at, piece):
    last = pool is not None
    args = [flags, turned, *below, *state]
    in_specs = [in_vmem] * len(args)
    aliases, scratch = {}, []
    if at is not None:
        args.append(weight)
        in_specs.append(anywhere)
        scratch = [pltpu.SemaphoreType.DMA(())]
    if last:
        args += list(pool)
        in_specs += [in_vmem] * len(pool)
        out_shape = [jax.ShapeDtypeStruct(out_piece, jnp.float32)]
    else:
        out_shape = [jax.ShapeDtypeStruct(part.shape, part.dtype) for part in state]
        aliases = {2 + len(below) + i: i for i in range(len(state))}
    if at is not None:
        out_shape.append(jax.ShapeDtypeStruct((piece, weight.shape[1]), weight.dtype))
    return call(
        functools.partial(next_kernel, across, distances, turns, last, at),
        out_shape,
        in_specs=in_specs,
        scratch_shapes=scratch,
        input_output_aliases=aliases,
        limit=big_limit if at is not None else 16 * 1024 * 1024,
    )(*args)


def project_kernel(across, other, parts_ref, *refs):
    weights, out_ref = refs[:-1], refs[-1]
    side = lax.axis_index("head")
    if other:
        side = 1 - side
    groups = []
    for y in range(across):
        total = parts_ref[y]
        for s in range(y + across, parts_ref.shape[0], across):
            total = total + parts_ref[s]
        groups.append(total)
    total = jnp.concatenate(groups, axis=1)
    rows = total.shape[0]
    high = total.astype(jnp.bfloat16)
    low = (total - high.astype(jnp.float32)).astype(jnp.bfloat16)
    both = jnp.concatenate([high, low], axis=0)
    half = out_ref.shape[1]
    step = math.gcd(half, 512)
    for c in range(half // step):
        start = pl.multiple_of(side * half + c * step, step)
        product, at = None, 0
        for weight_ref in weights:
            depth = weight_ref.shape[0]
            part = jnp.dot(
                both[:, at : at + depth],
                weight_ref[:, pl.ds(start, step)],
                preferred_element_type=jnp.float32,
            )
            product = part if product is None else product + part
            at += depth
        out_ref[:, c * step : (c + 1) * step] = product[:rows] + product[rows:]


def project(across, other, parts, weights):
    return call(
        functools.partial(project_kernel, across, other),
        jax.ShapeDtypeStruct((parts.shape[1], weights[0].shape[1] // 2), jnp.float32),
        in_specs=[in_vmem] * (1 + len(weights)),
    )(parts, *weights)


def on_device(count, queries, key_states, value_states, out_weight, turn_lengths, block_flags):
    across = key_states.shape[1] // HD
    down = count // across
    turns = turn_lengths.shape[0]

    def over(rows, shift):
        pairs = [(i, i - i % across + (i + shift) % across) for i in range(count)]
        return lax.ppermute(rows, "seq", pairs)

    def up(rows, distance, lowest=0):
        step = distance * across
        pairs = [(i, i + step) for i in range(lowest * across, count - step)]
        return lax.ppermute(rows, "seq", pairs)

    _, y = place(across)
    heads = []
    for shift in range(across):
        at = lax.rem(y + shift, across)
        heads.append(pair(pick(key_states, at, across), pick(value_states, at, across)))
    meta = lax.optimization_barrier(jnp.concatenate([turn_lengths, block_flags[0]]))
    padded = -(-count // 16) * 16
    flags = jnp.pad(meta[turns:], (0, padded - count))[:, None]
    groups = [pick(queries, lax.rem(y + shift, across), across) for shift in range(across)]
    sent = []
    for group in groups[1:]:
        under = jnp.broadcast_to(flags, (padded, group.shape[1])).astype(group.dtype)
        sent.append(jnp.concatenate([group, under], axis=0))
    flags = jnp.broadcast_to(flags, (padded, HD)).astype(jnp.float32)
    others = [over(group, shift) for shift, group in enumerate(sent, 1)]
    rows = join([heads[0]] + [over(heads[shift], shift) for shift in range(1, across)], sent[0])
    below = [rows, up(rows, 1)] + [None] * (down - 2)
    for distance in range(3, down):
        below[distance] = up(rows, distance)
    below[1], *others = lax.optimization_barrier((below[1], *others))
    if down > 2:
        below[2] = up(below[1], 1, 1)
    depth = out_weight.shape[0]
    pieces = [4 * depth // 8, 2 * depth // 8, 2 * depth // 8]
    turned, flags, member, inverse, weight, *state = attend_first(
        across, turns, meta, flags, [groups[0], *others], rows, out_weight, pieces[0]
    )
    weights = [weight]
    out_piece = (count, turns // count, queries.shape[1] // across)
    stages = [[1]] + [list(range(d, min(d + 2, down))) for d in range(2, down, 2)]
    for number, distances in enumerate(stages):
        last = number == len(stages) - 1
        with_weight = last or number == 0
        state = attend_next(
            across,
            distances,
            turns,
            turned,
            flags,
            [below[distance] for distance in distances],
            state,
            (member, inverse) if last else None,
            out_piece,
            out_weight,
            sum(pieces[: len(weights)]) if with_weight else None,
            pieces[len(weights)] if with_weight else None,
        )
        if with_weight:
            *state, weight = state
            weights.append(weight)
    parts = lax.all_to_all(state[0], "seq", split_axis=0, concat_axis=0, tiled=True)
    theirs = project(across, True, parts, weights)
    theirs = lax.ppermute(theirs, "head", [(0, 1), (1, 0)])
    return project(across, False, parts, weights) + theirs


def solution(mesh):
    in_specs = (
        P(("conv", "seq"), "head"),
        P(("conv", "seq"), "head"),
        P(("conv", "seq"), "head"),
        P("head", None),
        P("conv"),
        P(("conv", "seq"), None),
    )
    out_specs = P(("conv", "seq"), "head")
    return jax.shard_map(
        functools.partial(on_device, mesh.shape["seq"]),
        mesh=mesh,
        in_specs=in_specs,
        out_specs=out_specs,
        check_vma=False,
    )
```

```python
import functools
import math

import jax
import jax.numpy as jnp
from jax import lax
from jax.experimental import pallas as pl
from jax.experimental.pallas import tpu as pltpu
from jax.sharding import PartitionSpec as P

HD = 128

big_negative = -1e30
log_two_e = 1.4426950408889634

big_limit = 45 * 1024 * 1024
small_cost = pl.CostEstimate(flops=1024, bytes_accessed=1024, transcendentals=0)

in_vmem = pl.BlockSpec(memory_space=pltpu.VMEM)
in_smem = pl.BlockSpec(memory_space=pltpu.SMEM)
anywhere = pl.BlockSpec(memory_space=pl.ANY)


def place(across):
    index = lax.axis_index("seq")
    return index // across, lax.rem(index, across)


def block_at(z, y, e, across):
    return z * across + lax.rem(y - e + across, across)


def call(kernel, out_shape, **settings):
    limit = settings.pop("limit", 16 * 1024 * 1024)
    return pl.pallas_call(
        kernel,
        out_shape=out_shape,
        out_specs=jax.tree.map(lambda _: in_vmem, out_shape),
        compiler_params=pltpu.CompilerParams(vmem_limit_bytes=limit),
        cost_estimate=small_cost,
        **settings,
    )


def pick(rows, number, parts):
    width = rows.shape[1] // parts
    picked = rows[:, :width]
    for part in range(1, parts):
        picked = jnp.where(number == part, rows[:, part * width : (part + 1) * width], picked)
    return picked


def pair(keys, values):
    which = lax.broadcasted_iota(jnp.int32, (2,) + keys.shape, 0)
    return jnp.where(which == 0, keys[None], values[None])


def join_kernel(*refs):
    *parts, _, out_ref = refs
    for e, part in enumerate(parts):
        out_ref[e] = part[...]


def join(parts, after):
    shape = jax.ShapeDtypeStruct((len(parts),) + parts[0].shape, parts[0].dtype)
    return call(join_kernel, shape, in_specs=[in_vmem] * len(parts) + [anywhere])(*parts, after)


def rows_update(turned_ref, rows_refs, switches, state, first):
    top, total_sum, totals = state
    across, _, columns = turned_ref.shape
    rows = rows_refs[0].shape[2]
    count = across * len(rows_refs)
    factor = log_two_e / math.sqrt(HD)
    keys = [kv_ref[:, 0].reshape(across * rows, HD) for kv_ref in rows_refs]
    values = [kv_ref[:, 1].reshape(across * rows, HD).T for kv_ref in rows_refs]
    logits = [
        [jnp.dot(part, turned_ref[e], preferred_element_type=jnp.float32) for part in keys]
        for e in range(across)
    ]
    if first:
        key_pos = lax.broadcasted_iota(jnp.int32, (rows, 1), 0)
        column = lax.broadcasted_iota(jnp.int32, (1, columns), 1)
        causal = key_pos <= lax.rem(column, rows)
    for e in range(across):
        blocks = [
            logits[e][b // across][b % across * rows : (b % across + 1) * rows] for b in range(count)
        ]
        if first:
            blocks[e] = jnp.where(causal, blocks[e], big_negative)
        new_top = None if first else top[e]
        for b in range(count):
            block_top = jnp.ceil(jnp.max(blocks[b], axis=0, keepdims=True) * factor)
            if switches[e][b] is not None:
                block_top = jnp.where(switches[e][b], block_top, big_negative)
            new_top = block_top if new_top is None else jnp.maximum(new_top, block_top)
        weights, block_sum = [], None
        for b in range(count):
            against = new_top
            if switches[e][b] is not None:
                against = jnp.where(switches[e][b], new_top, -big_negative)
            weights.append(jnp.exp2(blocks[b] * factor - against))
            part = jnp.sum(weights[b], axis=0, keepdims=True)
            block_sum = part if block_sum is None else block_sum + part
        update = None
        for i, part in enumerate(values):
            mine = weights[i * across : (i + 1) * across]
            mine = jnp.concatenate([w.astype(jnp.bfloat16) for w in mine], axis=0)
            part = jnp.dot(part, mine, preferred_element_type=jnp.float32)
            update = part if update is None else update + part
        if not first:
            rescale = jnp.exp2(top[e] - new_top)
            block_sum = total_sum[e] * rescale + block_sum
            update = totals[e] * rescale + update
        top[e] = new_top
        total_sum[e] = block_sum
        totals[e] = update


def switch_of(flags_ref, e, owner, columns, allowed=None):
    flag = flags_ref[e, pl.ds(jnp.maximum(owner, 0), 1), :]
    if allowed is not None:
        flag = flag * jnp.where(allowed, 1.0, 0.0)
    return jnp.concatenate([flag] * (columns // HD), axis=1) > 0.5


def weight_piece(weight_ref, out_ref, start, sem):
    return pltpu.make_async_copy(weight_ref.at[start : start + out_ref.shape[0]], out_ref, sem)


def first_kernel(across, turns, meta_ref, own_flags_ref, *refs):
    queries, refs = refs[:across], refs[across:]
    kv_ref, weight_ref, turned_ref, flags_ref, member_ref, inverse_ref, weight_out = refs[:7]
    state, rows_ref, copied = refs[7:10], refs[10], refs[11]
    weight_copy = weight_piece(weight_ref, weight_out, 0, copied)
    weight_copy.start()
    z, y = place(across)
    q_rows = kv_ref.shape[2]
    repeat = queries[0].shape[1] // HD
    columns = repeat * q_rows
    for e in range(across):
        for r in range(repeat):
            turned_ref[e, :, r * q_rows : (r + 1) * q_rows] = queries[e][
                0:q_rows, r * HD : (r + 1) * HD
            ].T
    flags_ref[0] = own_flags_ref[...]
    for e in range(1, across):
        flags_ref[e] = queries[e][q_rows:, 0:HD].astype(jnp.float32)
    owners = [block_at(z, y, e, across) for e in range(across)]
    switches = [
        [
            None if e == b else switch_of(flags_ref, e, owners[b], columns, owners[b] < owners[e])
            for b in range(across)
        ]
        for e in range(across)
    ]
    rows_update(turned_ref, [kv_ref], switches, state, True)

    column = lax.broadcasted_iota(jnp.int32, (1, columns), 1)
    for e in range(across):
        position = lax.rem(column, q_rows) + owners[e] * q_rows
        start = jnp.int32(0)
        for t in range(turns):
            length = meta_ref[t]
            inside = (position >= start) & (position < start + length)
            rows_ref[t : t + 1, :] = jnp.where(inside, 1.0, 0.0)
            if e == 0:
                count = jnp.full((1, HD), length, jnp.int32).astype(jnp.float32)
                inverse_ref[t : t + 1, :] = 1.0 / count
            start = start + length
        for r in range(repeat):
            mine = (column >= r * q_rows) & (column < (r + 1) * q_rows)
            member_ref[e, r * turns : (r + 1) * turns, :] = jnp.where(
                mine, rows_ref[...], 0.0
            ).astype(jnp.bfloat16)
    weight_copy.wait()


def attend_first(across, turns, meta, flags, queries, rows, weight, piece):
    q_rows = rows.shape[2]
    repeat = queries[0].shape[1] // HD
    columns = repeat * q_rows
    f32, b16 = jnp.float32, jnp.bfloat16
    return call(
        functools.partial(first_kernel, across, turns),
        [
            jax.ShapeDtypeStruct((across, HD, columns), b16),
            jax.ShapeDtypeStruct((across,) + flags.shape, f32),
            jax.ShapeDtypeStruct((across, repeat * turns, columns), b16),
            jax.ShapeDtypeStruct((turns, HD), f32),
            jax.ShapeDtypeStruct((piece, weight.shape[1]), weight.dtype),
            jax.ShapeDtypeStruct((across, 1, columns), f32),
            jax.ShapeDtypeStruct((across, 1, columns), f32),
            jax.ShapeDtypeStruct((across, HD, columns), f32),
        ],
        in_specs=[in_smem] + [in_vmem] * (across + 2) + [anywhere],
        scratch_shapes=[pltpu.VMEM((turns, columns), f32), pltpu.SemaphoreType.DMA(())],
        limit=big_limit,
    )(meta, flags, *queries, rows, weight)


def next_kernel(across, distances, turns, last, weight_at, flags_ref, turned_ref, *refs):
    below_count = len(distances)
    below, state, refs = refs[:below_count], refs[below_count : below_count + 3], refs[below_count + 3 :]
    if weight_at is not None:
        weight_ref, weight_out, copied = refs[0], refs[-2], refs[-1]
        refs = refs[1:-2]
        weight_copy = weight_piece(weight_ref, weight_out, weight_at, copied)
        weight_copy.start()
    z, y = place(across)
    columns = turned_ref.shape[2]

    def update(rows, from_distances):
        switches = [
            [
                switch_of(flags_ref, e, block_at(z - distance, y, b, across), columns)
                for distance in from_distances
                for b in range(across)
            ]
            for e in range(across)
        ]
        rows_update(turned_ref, rows, switches, state, False)

    for number, distance in enumerate(distances, 1):
        here = (z >= distance) if number == len(distances) else (z == distance)
        pl.when(here)(functools.partial(update, below[:number], distances[:number]))

    if weight_at is not None:
        weight_copy.wait()
    if last:
        member_ref, inverse_ref, out_ref = refs
        rows = out_ref.shape[1]
        pooled = None
        for e in range(across):
            attended = (state[2][e] / state[1][e]).astype(jnp.bfloat16)
            part = lax.dot_general(
                member_ref[e],
                attended,
                (((1,), (1,)), ((), ())),
                preferred_element_type=jnp.float32,
            )
            pooled = part if pooled is None else pooled + part
        for r in range(pooled.shape[0] // turns):
            mean = pooled[r * turns : (r + 1) * turns] * inverse_ref[...]
            for s in range(out_ref.shape[0]):
                out_ref[s, :, r * HD : (r + 1) * HD] = mean[s * rows : (s + 1) * rows]


def attend_next(across, distances, turns, turned, flags, below, state, pool, out_piece, weight, at, piece):
    last = pool is not None
    args = [flags, turned, *below, *state]
    in_specs = [in_vmem] * len(args)
    aliases, scratch = {}, []
    if at is not None:
        args.append(weight)
        in_specs.append(anywhere)
        scratch = [pltpu.SemaphoreType.DMA(())]
    if last:
        args += list(pool)
        in_specs += [in_vmem] * len(pool)
        out_shape = [jax.ShapeDtypeStruct(out_piece, jnp.float32)]
    else:
        out_shape = [jax.ShapeDtypeStruct(part.shape, part.dtype) for part in state]
        aliases = {2 + len(below) + i: i for i in range(len(state))}
    if at is not None:
        out_shape.append(jax.ShapeDtypeStruct((piece, weight.shape[1]), weight.dtype))
    return call(
        functools.partial(next_kernel, across, distances, turns, last, at),
        out_shape,
        in_specs=in_specs,
        scratch_shapes=scratch,
        input_output_aliases=aliases,
        limit=big_limit if at is not None else 16 * 1024 * 1024,
    )(*args)


def project_kernel(across, other, parts_ref, *refs):
    weights, out_ref = refs[:-1], refs[-1]
    side = lax.axis_index("head")
    if other:
        side = 1 - side
    groups = []
    for y in range(across):
        total = parts_ref[y]
        for s in range(y + across, parts_ref.shape[0], across):
            total = total + parts_ref[s]
        groups.append(total)
    total = jnp.concatenate(groups, axis=1)
    rows = total.shape[0]
    high = total.astype(jnp.bfloat16)
    low = (total - high.astype(jnp.float32)).astype(jnp.bfloat16)
    both = jnp.concatenate([high, low], axis=0)
    half = out_ref.shape[1]
    step = math.gcd(half, 512)
    for c in range(half // step):
        start = pl.multiple_of(side * half + c * step, step)
        product, at = None, 0
        for weight_ref in weights:
            depth = weight_ref.shape[0]
            part = jnp.dot(
                both[:, at : at + depth],
                weight_ref[:, pl.ds(start, step)],
                preferred_element_type=jnp.float32,
            )
            product = part if product is None else product + part
            at += depth
        out_ref[:, c * step : (c + 1) * step] = product[:rows] + product[rows:]


def project(across, other, parts, weights):
    return call(
        functools.partial(project_kernel, across, other),
        jax.ShapeDtypeStruct((parts.shape[1], weights[0].shape[1] // 2), jnp.float32),
        in_specs=[in_vmem] * (1 + len(weights)),
    )(parts, *weights)


def on_device(count, queries, key_states, value_states, out_weight, turn_lengths, block_flags):
    across = key_states.shape[1] // HD
    down = count // across
    turns = turn_lengths.shape[0]

    def over(rows, shift):
        pairs = [(i, i - i % across + (i + shift) % across) for i in range(count)]
        return lax.ppermute(rows, "seq", pairs)

    def up(rows, distance, lowest=0):
        step = distance * across
        pairs = [(i, i + step) for i in range(lowest * across, count - step)]
        return lax.ppermute(rows, "seq", pairs)

    _, y = place(across)
    heads = []
    for shift in range(across):
        at = lax.rem(y + shift, across)
        heads.append(pair(pick(key_states, at, across), pick(value_states, at, across)))
    meta = lax.optimization_barrier(jnp.concatenate([turn_lengths, block_flags[0]]))
    padded = -(-count // 16) * 16
    flags = jnp.pad(meta[turns:], (0, padded - count))[:, None]
    groups = [pick(queries, lax.rem(y + shift, across), across) for shift in range(across)]
    sent = []
    for group in groups[1:]:
        under = jnp.broadcast_to(flags, (padded, group.shape[1])).astype(group.dtype)
        sent.append(jnp.concatenate([group, under], axis=0))
    flags = jnp.broadcast_to(flags, (padded, HD)).astype(jnp.float32)
    others = [over(group, shift) for shift, group in enumerate(sent, 1)]
    rows = join([heads[0]] + [over(heads[shift], shift) for shift in range(1, across)], sent[0])
    below = [rows, up(rows, 1)] + [None] * (down - 2)
    for distance in range(3, down):
        below[distance] = up(rows, distance)
    if down > 2:
        below[2] = up(below[1], 1, 1)
    depth = out_weight.shape[0]
    pieces = [4 * depth // 8, 2 * depth // 8, 2 * depth // 8]
    turned, flags, member, inverse, weight, *state = attend_first(
        across, turns, meta, flags, [groups[0], *others], rows, out_weight, pieces[0]
    )
    weights = [weight]
    out_piece = (count, turns // count, queries.shape[1] // across)
    stages = [[1]] + [list(range(d, min(d + 2, down))) for d in range(2, down, 2)]
    for number, distances in enumerate(stages):
        last = number == len(stages) - 1
        with_weight = last or number == 0
        state = attend_next(
            across,
            distances,
            turns,
            turned,
            flags,
            [below[distance] for distance in distances],
            state,
            (member, inverse) if last else None,
            out_piece,
            out_weight,
            sum(pieces[: len(weights)]) if with_weight else None,
            pieces[len(weights)] if with_weight else None,
        )
        if with_weight:
            *state, weight = state
            weights.append(weight)
    parts = lax.all_to_all(state[0], "seq", split_axis=0, concat_axis=0, tiled=True)
    theirs = project(across, True, parts, weights)
    theirs = lax.ppermute(theirs, "head", [(0, 1), (1, 0)])
    return project(across, False, parts, weights) + theirs


def solution(mesh):
    in_specs = (
        P(("conv", "seq"), "head"),
        P(("conv", "seq"), "head"),
        P(("conv", "seq"), "head"),
        P("head", None),
        P("conv"),
        P(("conv", "seq"), None),
    )
    out_specs = P(("conv", "seq"), "head")
    return jax.shard_map(
        functools.partial(on_device, mesh.shape["seq"]),
        mesh=mesh,
        in_specs=in_specs,
        out_specs=out_specs,
        check_vma=False,
    )
```

```python
import functools
import math

import jax
import jax.numpy as jnp
from jax import lax
from jax.experimental import pallas as pl
from jax.experimental.pallas import tpu as pltpu
from jax.sharding import PartitionSpec as P

HD = 128

big_negative = -1e30
log_two_e = 1.4426950408889634

big_limit = 45 * 1024 * 1024
small_cost = pl.CostEstimate(flops=1024, bytes_accessed=1024, transcendentals=0)

in_vmem = pl.BlockSpec(memory_space=pltpu.VMEM)
in_smem = pl.BlockSpec(memory_space=pltpu.SMEM)
anywhere = pl.BlockSpec(memory_space=pl.ANY)


def place(across):
    index = lax.axis_index("seq")
    return index // across, lax.rem(index, across)


def block_at(z, y, e, across):
    return z * across + lax.rem(y - e + across, across)


def call(kernel, out_shape, **settings):
    limit = settings.pop("limit", 16 * 1024 * 1024)
    return pl.pallas_call(
        kernel,
        out_shape=out_shape,
        out_specs=jax.tree.map(lambda _: in_vmem, out_shape),
        compiler_params=pltpu.CompilerParams(vmem_limit_bytes=limit),
        cost_estimate=small_cost,
        **settings,
    )


def pick(rows, number, parts):
    width = rows.shape[1] // parts
    picked = rows[:, :width]
    for part in range(1, parts):
        picked = jnp.where(number == part, rows[:, part * width : (part + 1) * width], picked)
    return picked


def pair(keys, values):
    which = lax.broadcasted_iota(jnp.int32, (2,) + keys.shape, 0)
    return jnp.where(which == 0, keys[None], values[None])


def join_kernel(*refs):
    *parts, out_ref = refs
    for e, part in enumerate(parts):
        out_ref[e] = part[...]


def join(parts):
    shape = jax.ShapeDtypeStruct((len(parts),) + parts[0].shape, parts[0].dtype)
    return call(join_kernel, shape, in_specs=[in_vmem] * len(parts))(*parts)


def rows_update(turned_ref, rows_refs, switches, state, first):
    top, total_sum, totals = state
    across, _, columns = turned_ref.shape
    rows = rows_refs[0].shape[2]
    count = across * len(rows_refs)
    factor = log_two_e / math.sqrt(HD)
    keys = [kv_ref[:, 0].reshape(across * rows, HD) for kv_ref in rows_refs]
    values = [kv_ref[:, 1].reshape(across * rows, HD).T for kv_ref in rows_refs]
    logits = [
        [jnp.dot(part, turned_ref[e], preferred_element_type=jnp.float32) for part in keys]
        for e in range(across)
    ]
    if first:
        key_pos = lax.broadcasted_iota(jnp.int32, (rows, 1), 0)
        column = lax.broadcasted_iota(jnp.int32, (1, columns), 1)
        causal = key_pos <= lax.rem(column, rows)
    for e in range(across):
        blocks = [
            logits[e][b // across][b % across * rows : (b % across + 1) * rows] for b in range(count)
        ]
        if first:
            blocks[e] = jnp.where(causal, blocks[e], big_negative)
        new_top = None if first else top[e]
        for b in range(count):
            block_top = jnp.ceil(jnp.max(blocks[b], axis=0, keepdims=True) * factor)
            if switches[e][b] is not None:
                block_top = jnp.where(switches[e][b], block_top, big_negative)
            new_top = block_top if new_top is None else jnp.maximum(new_top, block_top)
        weights, block_sum = [], None
        for b in range(count):
            against = new_top
            if switches[e][b] is not None:
                against = jnp.where(switches[e][b], new_top, -big_negative)
            weights.append(jnp.exp2(blocks[b] * factor - against))
            part = jnp.sum(weights[b], axis=0, keepdims=True)
            block_sum = part if block_sum is None else block_sum + part
        update = None
        for i, part in enumerate(values):
            mine = weights[i * across : (i + 1) * across]
            mine = jnp.concatenate([w.astype(jnp.bfloat16) for w in mine], axis=0)
            part = jnp.dot(part, mine, preferred_element_type=jnp.float32)
            update = part if update is None else update + part
        if not first:
            rescale = jnp.exp2(top[e] - new_top)
            block_sum = total_sum[e] * rescale + block_sum
            update = totals[e] * rescale + update
        top[e] = new_top
        total_sum[e] = block_sum
        totals[e] = update


def switch_of(flags_ref, e, owner, columns, allowed=None):
    flag = flags_ref[e, pl.ds(jnp.maximum(owner, 0), 1), :]
    if allowed is not None:
        flag = flag * jnp.where(allowed, 1.0, 0.0)
    return jnp.concatenate([flag] * (columns // HD), axis=1) > 0.5


def member_kernel(across, turns, meta_ref, after_ref, member_ref, inverse_ref, rows_ref):
    del after_ref
    z, y = place(across)
    columns = rows_ref.shape[1]
    repeat = member_ref.shape[1] // turns
    q_rows = columns // repeat
    owners = [block_at(z, y, e, across) for e in range(across)]
    column = lax.broadcasted_iota(jnp.int32, (1, columns), 1)
    for e in range(across):
        position = lax.rem(column, q_rows) + owners[e] * q_rows
        start = jnp.int32(0)
        for t in range(turns):
            length = meta_ref[t]
            inside = (position >= start) & (position < start + length)
            rows_ref[t : t + 1, :] = jnp.where(inside, 1.0, 0.0)
            if e == 0:
                count = jnp.full((1, HD), length, jnp.int32).astype(jnp.float32)
                inverse_ref[t : t + 1, :] = 1.0 / count
            start = start + length
        for r in range(repeat):
            mine = (column >= r * q_rows) & (column < (r + 1) * q_rows)
            member_ref[e, r * turns : (r + 1) * turns, :] = jnp.where(
                mine, rows_ref[...], 0.0
            ).astype(jnp.bfloat16)


def members(across, turns, meta, group):
    q_rows, width = group.shape
    repeat = width // HD
    columns = repeat * q_rows
    return call(
        functools.partial(member_kernel, across, turns),
        [
            jax.ShapeDtypeStruct((across, repeat * turns, columns), jnp.bfloat16),
            jax.ShapeDtypeStruct((turns, HD), jnp.float32),
        ],
        in_specs=[in_smem, anywhere],
        scratch_shapes=[pltpu.VMEM((turns, columns), jnp.float32)],
    )(meta, group)


def weight_piece(weight_ref, out_ref, start, sem):
    return pltpu.make_async_copy(weight_ref.at[start : start + out_ref.shape[0]], out_ref, sem)


def first_kernel(across, own_flags_ref, *refs):
    queries, refs = refs[:across], refs[across:]
    kv_ref, weight_ref, turned_ref, flags_ref, weight_out = refs[:5]
    state, copied = refs[5:8], refs[8]
    weight_copy = weight_piece(weight_ref, weight_out, 0, copied)
    weight_copy.start()
    z, y = place(across)
    q_rows = kv_ref.shape[2]
    repeat = queries[0].shape[1] // HD
    columns = repeat * q_rows
    for e in range(across):
        for r in range(repeat):
            turned_ref[e, :, r * q_rows : (r + 1) * q_rows] = queries[e][
                0:q_rows, r * HD : (r + 1) * HD
            ].T
    flags_ref[0] = own_flags_ref[...]
    for e in range(1, across):
        flags_ref[e] = queries[e][q_rows:, 0:HD].astype(jnp.float32)
    owners = [block_at(z, y, e, across) for e in range(across)]
    switches = [
        [
            None if e == b else switch_of(flags_ref, e, owners[b], columns, owners[b] < owners[e])
            for b in range(across)
        ]
        for e in range(across)
    ]
    rows_update(turned_ref, [kv_ref], switches, state, True)

    weight_copy.wait()


def attend_first(across, flags, queries, rows, weight, piece):
    q_rows = rows.shape[2]
    repeat = queries[0].shape[1] // HD
    columns = repeat * q_rows
    f32, b16 = jnp.float32, jnp.bfloat16
    return call(
        functools.partial(first_kernel, across),
        [
            jax.ShapeDtypeStruct((across, HD, columns), b16),
            jax.ShapeDtypeStruct((across,) + flags.shape, f32),
            jax.ShapeDtypeStruct((piece, weight.shape[1]), weight.dtype),
            jax.ShapeDtypeStruct((across, 1, columns), f32),
            jax.ShapeDtypeStruct((across, 1, columns), f32),
            jax.ShapeDtypeStruct((across, HD, columns), f32),
        ],
        in_specs=[in_vmem] * (across + 2) + [anywhere],
        scratch_shapes=[pltpu.SemaphoreType.DMA(())],
        limit=big_limit,
    )(flags, *queries, rows, weight)


def next_kernel(across, distances, turns, last, weight_at, flags_ref, turned_ref, *refs):
    below_count = len(distances)
    below, state, refs = refs[:below_count], refs[below_count : below_count + 3], refs[below_count + 3 :]
    if weight_at is not None:
        weight_ref, weight_out, copied = refs[0], refs[-2], refs[-1]
        refs = refs[1:-2]
        weight_copy = weight_piece(weight_ref, weight_out, weight_at, copied)
        weight_copy.start()
    z, y = place(across)
    columns = turned_ref.shape[2]

    def update(rows, from_distances):
        switches = [
            [
                switch_of(flags_ref, e, block_at(z - distance, y, b, across), columns)
                for distance in from_distances
                for b in range(across)
            ]
            for e in range(across)
        ]
        rows_update(turned_ref, rows, switches, state, False)

    for number, distance in enumerate(distances, 1):
        here = (z >= distance) if number == len(distances) else (z == distance)
        pl.when(here)(functools.partial(update, below[:number], distances[:number]))

    if weight_at is not None:
        weight_copy.wait()
    if last:
        member_ref, inverse_ref, out_ref = refs
        rows = out_ref.shape[1]
        pooled = None
        for e in range(across):
            attended = (state[2][e] / state[1][e]).astype(jnp.bfloat16)
            part = lax.dot_general(
                member_ref[e],
                attended,
                (((1,), (1,)), ((), ())),
                preferred_element_type=jnp.float32,
            )
            pooled = part if pooled is None else pooled + part
        for r in range(pooled.shape[0] // turns):
            mean = pooled[r * turns : (r + 1) * turns] * inverse_ref[...]
            for s in range(out_ref.shape[0]):
                out_ref[s, :, r * HD : (r + 1) * HD] = mean[s * rows : (s + 1) * rows]


def attend_next(across, distances, turns, turned, flags, below, state, pool, out_piece, weight, at, piece):
    last = pool is not None
    args = [flags, turned, *below, *state]
    in_specs = [in_vmem] * len(args)
    aliases, scratch = {}, []
    if at is not None:
        args.append(weight)
        in_specs.append(anywhere)
        scratch = [pltpu.SemaphoreType.DMA(())]
    if last:
        args += list(pool)
        in_specs += [in_vmem] * len(pool)
        out_shape = [jax.ShapeDtypeStruct(out_piece, jnp.float32)]
    else:
        out_shape = [jax.ShapeDtypeStruct(part.shape, part.dtype) for part in state]
        aliases = {2 + len(below) + i: i for i in range(len(state))}
    if at is not None:
        out_shape.append(jax.ShapeDtypeStruct((piece, weight.shape[1]), weight.dtype))
    return call(
        functools.partial(next_kernel, across, distances, turns, last, at),
        out_shape,
        in_specs=in_specs,
        scratch_shapes=scratch,
        input_output_aliases=aliases,
        limit=big_limit if at is not None else 16 * 1024 * 1024,
    )(*args)


def project_kernel(across, other, parts_ref, *refs):
    weights, out_ref = refs[:-1], refs[-1]
    side = lax.axis_index("head")
    if other:
        side = 1 - side
    groups = []
    for y in range(across):
        total = parts_ref[y]
        for s in range(y + across, parts_ref.shape[0], across):
            total = total + parts_ref[s]
        groups.append(total)
    total = jnp.concatenate(groups, axis=1)
    rows = total.shape[0]
    high = total.astype(jnp.bfloat16)
    low = (total - high.astype(jnp.float32)).astype(jnp.bfloat16)
    both = jnp.concatenate([high, low], axis=0)
    half = out_ref.shape[1]
    step = math.gcd(half, 512)
    for c in range(half // step):
        start = pl.multiple_of(side * half + c * step, step)
        product, at = None, 0
        for weight_ref in weights:
            depth = weight_ref.shape[0]
            part = jnp.dot(
                both[:, at : at + depth],
                weight_ref[:, pl.ds(start, step)],
                preferred_element_type=jnp.float32,
            )
            product = part if product is None else product + part
            at += depth
        out_ref[:, c * step : (c + 1) * step] = product[:rows] + product[rows:]


def project(across, other, parts, weights):
    return call(
        functools.partial(project_kernel, across, other),
        jax.ShapeDtypeStruct((parts.shape[1], weights[0].shape[1] // 2), jnp.float32),
        in_specs=[in_vmem] * (1 + len(weights)),
    )(parts, *weights)


def on_device(count, queries, key_states, value_states, out_weight, turn_lengths, block_flags):
    across = key_states.shape[1] // HD
    down = count // across
    turns = turn_lengths.shape[0]

    def over(rows, shift):
        pairs = [(i, i - i % across + (i + shift) % across) for i in range(count)]
        return lax.ppermute(rows, "seq", pairs)

    def up(rows, distance, lowest=0):
        step = distance * across
        pairs = [(i, i + step) for i in range(lowest * across, count - step)]
        return lax.ppermute(rows, "seq", pairs)

    _, y = place(across)
    heads = []
    for shift in range(across):
        at = lax.rem(y + shift, across)
        heads.append(pair(pick(key_states, at, across), pick(value_states, at, across)))
    rows = join([heads[0]] + [over(heads[shift], shift) for shift in range(1, across)])
    rows, queries = lax.optimization_barrier((rows, queries))
    meta = lax.optimization_barrier(jnp.concatenate([turn_lengths, block_flags[0]]))
    padded = -(-count // 16) * 16
    flags = jnp.pad(meta[turns:], (0, padded - count))[:, None]
    groups = [pick(queries, lax.rem(y + shift, across), across) for shift in range(across)]
    sent = []
    for group in groups[1:]:
        under = jnp.broadcast_to(flags, (padded, group.shape[1])).astype(group.dtype)
        sent.append(jnp.concatenate([group, under], axis=0))
    flags = jnp.broadcast_to(flags, (padded, HD)).astype(jnp.float32)
    below = [rows, up(rows, 1)] + [None] * (down - 2)
    member, inverse = members(across, turns, meta, groups[0])
    far, inverse, *sent = lax.optimization_barrier((rows, inverse, *sent))
    others = [over(group, shift) for shift, group in enumerate(sent, 1)]
    for distance in range(3, down):
        below[distance] = up(far, distance)
    if down > 2:
        below[2] = up(below[1], 1, 1)
    depth = out_weight.shape[0]
    pieces = [4 * depth // 8, 2 * depth // 8, 2 * depth // 8]
    turned, flags, weight, *state = attend_first(
        across, flags, [groups[0], *others], rows, out_weight, pieces[0]
    )
    weights = [weight]
    out_piece = (count, turns // count, queries.shape[1] // across)
    stages = [[1]] + [list(range(d, min(d + 2, down))) for d in range(2, down, 2)]
    for number, distances in enumerate(stages):
        last = number == len(stages) - 1
        with_weight = last or number == 0
        state = attend_next(
            across,
            distances,
            turns,
            turned,
            flags,
            [below[distance] for distance in distances],
            state,
            (member, inverse) if last else None,
            out_piece,
            out_weight,
            sum(pieces[: len(weights)]) if with_weight else None,
            pieces[len(weights)] if with_weight else None,
        )
        if with_weight:
            *state, weight = state
            weights.append(weight)
    parts = lax.all_to_all(state[0], "seq", split_axis=0, concat_axis=0, tiled=True)
    theirs = project(across, True, parts, weights)
    theirs = lax.ppermute(theirs, "head", [(0, 1), (1, 0)])
    return project(across, False, parts, weights) + theirs


def solution(mesh):
    in_specs = (
        P(("conv", "seq"), "head"),
        P(("conv", "seq"), "head"),
        P(("conv", "seq"), "head"),
        P("head", None),
        P("conv"),
        P(("conv", "seq"), None),
    )
    out_specs = P(("conv", "seq"), "head")
    return jax.shard_map(
        functools.partial(on_device, mesh.shape["seq"]),
        mesh=mesh,
        in_specs=in_specs,
        out_specs=out_specs,
        check_vma=False,
    )
```

```python
import functools
import math

import jax
import jax.numpy as jnp
from jax import lax
from jax.experimental import pallas as pl
from jax.experimental.pallas import tpu as pltpu
from jax.sharding import PartitionSpec as P

HD = 128

big_negative = -1e30
log_two_e = 1.4426950408889634

big_limit = 45 * 1024 * 1024
small_cost = pl.CostEstimate(flops=1024, bytes_accessed=1024, transcendentals=0)

in_vmem = pl.BlockSpec(memory_space=pltpu.VMEM)
in_smem = pl.BlockSpec(memory_space=pltpu.SMEM)
anywhere = pl.BlockSpec(memory_space=pl.ANY)


def place(across):
    index = lax.axis_index("seq")
    return index // across, lax.rem(index, across)


def block_at(z, y, e, across):
    return z * across + lax.rem(y - e + across, across)


def call(kernel, out_shape, **settings):
    limit = settings.pop("limit", 16 * 1024 * 1024)
    return pl.pallas_call(
        kernel,
        out_shape=out_shape,
        out_specs=jax.tree.map(lambda _: in_vmem, out_shape),
        compiler_params=pltpu.CompilerParams(vmem_limit_bytes=limit),
        cost_estimate=small_cost,
        **settings,
    )


def pick(rows, number, parts):
    width = rows.shape[1] // parts
    picked = rows[:, :width]
    for part in range(1, parts):
        picked = jnp.where(number == part, rows[:, part * width : (part + 1) * width], picked)
    return picked


def pair(keys, values):
    which = lax.broadcasted_iota(jnp.int32, (2,) + keys.shape, 0)
    return jnp.where(which == 0, keys[None], values[None])


def join_kernel(*refs):
    *parts, out_ref = refs
    for e, part in enumerate(parts):
        out_ref[e] = part[...]


def join(parts):
    shape = jax.ShapeDtypeStruct((len(parts),) + parts[0].shape, parts[0].dtype)
    return call(join_kernel, shape, in_specs=[in_vmem] * len(parts))(*parts)


def rows_update(turned_ref, rows_refs, switches, state, first):
    top, total_sum, totals = state
    across, _, columns = turned_ref.shape
    rows = rows_refs[0].shape[2]
    count = across * len(rows_refs)
    factor = log_two_e / math.sqrt(HD)
    keys = [kv_ref[:, 0].reshape(across * rows, HD) for kv_ref in rows_refs]
    values = [kv_ref[:, 1].reshape(across * rows, HD).T for kv_ref in rows_refs]
    logits = [
        [jnp.dot(part, turned_ref[e], preferred_element_type=jnp.float32) for part in keys]
        for e in range(across)
    ]
    if first:
        key_pos = lax.broadcasted_iota(jnp.int32, (rows, 1), 0)
        column = lax.broadcasted_iota(jnp.int32, (1, columns), 1)
        causal = key_pos <= lax.rem(column, rows)
    for e in range(across):
        blocks = [
            logits[e][b // across][b % across * rows : (b % across + 1) * rows] for b in range(count)
        ]
        if first:
            blocks[e] = jnp.where(causal, blocks[e], big_negative)
        new_top = None if first else top[e]
        for b in range(count):
            block_top = jnp.ceil(jnp.max(blocks[b], axis=0, keepdims=True) * factor)
            if switches[e][b] is not None:
                block_top = jnp.where(switches[e][b], block_top, big_negative)
            new_top = block_top if new_top is None else jnp.maximum(new_top, block_top)
        weights, block_sum = [], None
        for b in range(count):
            against = new_top
            if switches[e][b] is not None:
                against = jnp.where(switches[e][b], new_top, -big_negative)
            weights.append(jnp.exp2(blocks[b] * factor - against))
            part = jnp.sum(weights[b], axis=0, keepdims=True)
            block_sum = part if block_sum is None else block_sum + part
        update = None
        for i, part in enumerate(values):
            mine = weights[i * across : (i + 1) * across]
            mine = jnp.concatenate([w.astype(jnp.bfloat16) for w in mine], axis=0)
            part = jnp.dot(part, mine, preferred_element_type=jnp.float32)
            update = part if update is None else update + part
        if not first:
            rescale = jnp.exp2(top[e] - new_top)
            block_sum = total_sum[e] * rescale + block_sum
            update = totals[e] * rescale + update
        top[e] = new_top
        total_sum[e] = block_sum
        totals[e] = update


def switch_of(flags_ref, e, owner, columns, allowed=None):
    flag = flags_ref[e, pl.ds(jnp.maximum(owner, 0), 1), :]
    if allowed is not None:
        flag = flag * jnp.where(allowed, 1.0, 0.0)
    return jnp.concatenate([flag] * (columns // HD), axis=1) > 0.5


def member_kernel(across, turns, meta_ref, after_ref, member_ref, inverse_ref, rows_ref):
    del after_ref
    z, y = place(across)
    columns = rows_ref.shape[1]
    repeat = member_ref.shape[1] // turns
    q_rows = columns // repeat
    owners = [block_at(z, y, e, across) for e in range(across)]
    column = lax.broadcasted_iota(jnp.int32, (1, columns), 1)
    for e in range(across):
        position = lax.rem(column, q_rows) + owners[e] * q_rows
        start = jnp.int32(0)
        for t in range(turns):
            length = meta_ref[t]
            inside = (position >= start) & (position < start + length)
            rows_ref[t : t + 1, :] = jnp.where(inside, 1.0, 0.0)
            if e == 0:
                count = jnp.full((1, HD), length, jnp.int32).astype(jnp.float32)
                inverse_ref[t : t + 1, :] = 1.0 / count
            start = start + length
        for r in range(repeat):
            mine = (column >= r * q_rows) & (column < (r + 1) * q_rows)
            member_ref[e, r * turns : (r + 1) * turns, :] = jnp.where(
                mine, rows_ref[...], 0.0
            ).astype(jnp.bfloat16)


def members(across, turns, meta, group):
    q_rows, width = group.shape
    repeat = width // HD
    columns = repeat * q_rows
    return call(
        functools.partial(member_kernel, across, turns),
        [
            jax.ShapeDtypeStruct((across, repeat * turns, columns), jnp.bfloat16),
            jax.ShapeDtypeStruct((turns, HD), jnp.float32),
        ],
        in_specs=[in_smem, anywhere],
        scratch_shapes=[pltpu.VMEM((turns, columns), jnp.float32)],
    )(meta, group)


def weight_piece(weight_ref, out_ref, start, sem):
    return pltpu.make_async_copy(weight_ref.at[start : start + out_ref.shape[0]], out_ref, sem)


def first_kernel(across, own_flags_ref, *refs):
    queries, refs = refs[:across], refs[across:]
    kv_ref, weight_ref, turned_ref, flags_ref, weight_out = refs[:5]
    state, copied = refs[5:8], refs[8]
    weight_copy = weight_piece(weight_ref, weight_out, 0, copied)
    weight_copy.start()
    z, y = place(across)
    q_rows = kv_ref.shape[2]
    repeat = queries[0].shape[1] // HD
    columns = repeat * q_rows
    for e in range(across):
        for r in range(repeat):
            turned_ref[e, :, r * q_rows : (r + 1) * q_rows] = queries[e][
                0:q_rows, r * HD : (r + 1) * HD
            ].T
    flags_ref[0] = own_flags_ref[...]
    for e in range(1, across):
        flags_ref[e] = queries[e][q_rows:, 0:HD].astype(jnp.float32)
    owners = [block_at(z, y, e, across) for e in range(across)]
    switches = [
        [
            None if e == b else switch_of(flags_ref, e, owners[b], columns, owners[b] < owners[e])
            for b in range(across)
        ]
        for e in range(across)
    ]
    rows_update(turned_ref, [kv_ref], switches, state, True)

    weight_copy.wait()


def attend_first(across, flags, queries, rows, weight, piece):
    q_rows = rows.shape[2]
    repeat = queries[0].shape[1] // HD
    columns = repeat * q_rows
    f32, b16 = jnp.float32, jnp.bfloat16
    return call(
        functools.partial(first_kernel, across),
        [
            jax.ShapeDtypeStruct((across, HD, columns), b16),
            jax.ShapeDtypeStruct((across,) + flags.shape, f32),
            jax.ShapeDtypeStruct((piece, weight.shape[1]), weight.dtype),
            jax.ShapeDtypeStruct((across, 1, columns), f32),
            jax.ShapeDtypeStruct((across, 1, columns), f32),
            jax.ShapeDtypeStruct((across, HD, columns), f32),
        ],
        in_specs=[in_vmem] * (across + 2) + [anywhere],
        scratch_shapes=[pltpu.SemaphoreType.DMA(())],
        limit=big_limit,
    )(flags, *queries, rows, weight)


def next_kernel(across, distances, turns, last, weight_at, flags_ref, turned_ref, *refs):
    below_count = len(distances)
    below, state, refs = refs[:below_count], refs[below_count : below_count + 3], refs[below_count + 3 :]
    if weight_at is not None:
        weight_ref, weight_out, copied = refs[0], refs[-2], refs[-1]
        refs = refs[1:-2]
        weight_copy = weight_piece(weight_ref, weight_out, weight_at, copied)
        weight_copy.start()
    z, y = place(across)
    columns = turned_ref.shape[2]

    def update(rows, from_distances):
        switches = [
            [
                switch_of(flags_ref, e, block_at(z - distance, y, b, across), columns)
                for distance in from_distances
                for b in range(across)
            ]
            for e in range(across)
        ]
        rows_update(turned_ref, rows, switches, state, False)

    for number, distance in enumerate(distances, 1):
        here = (z >= distance) if number == len(distances) else (z == distance)
        pl.when(here)(functools.partial(update, below[:number], distances[:number]))

    if weight_at is not None:
        weight_copy.wait()
    if last:
        member_ref, inverse_ref, out_ref = refs
        rows = out_ref.shape[1]
        pooled = None
        for e in range(across):
            attended = (state[2][e] / state[1][e]).astype(jnp.bfloat16)
            part = lax.dot_general(
                member_ref[e],
                attended,
                (((1,), (1,)), ((), ())),
                preferred_element_type=jnp.float32,
            )
            pooled = part if pooled is None else pooled + part
        for r in range(pooled.shape[0] // turns):
            mean = pooled[r * turns : (r + 1) * turns] * inverse_ref[...]
            for s in range(out_ref.shape[0]):
                out_ref[s, :, r * HD : (r + 1) * HD] = mean[s * rows : (s + 1) * rows]


def attend_next(across, distances, turns, turned, flags, below, state, pool, out_piece, weight, at, piece):
    last = pool is not None
    args = [flags, turned, *below, *state]
    in_specs = [in_vmem] * len(args)
    aliases, scratch = {}, []
    if at is not None:
        args.append(weight)
        in_specs.append(anywhere)
        scratch = [pltpu.SemaphoreType.DMA(())]
    if last:
        args += list(pool)
        in_specs += [in_vmem] * len(pool)
        out_shape = [jax.ShapeDtypeStruct(out_piece, jnp.float32)]
    else:
        out_shape = [jax.ShapeDtypeStruct(part.shape, part.dtype) for part in state]
        aliases = {2 + len(below) + i: i for i in range(len(state))}
    if at is not None:
        out_shape.append(jax.ShapeDtypeStruct((piece, weight.shape[1]), weight.dtype))
    return call(
        functools.partial(next_kernel, across, distances, turns, last, at),
        out_shape,
        in_specs=in_specs,
        scratch_shapes=scratch,
        input_output_aliases=aliases,
        limit=big_limit if at is not None else 16 * 1024 * 1024,
    )(*args)


def project_kernel(across, other, parts_ref, *refs):
    weights, out_ref = refs[:-1], refs[-1]
    side = lax.axis_index("head")
    if other:
        side = 1 - side
    groups = []
    for y in range(across):
        total = parts_ref[y]
        for s in range(y + across, parts_ref.shape[0], across):
            total = total + parts_ref[s]
        groups.append(total)
    total = jnp.concatenate(groups, axis=1)
    rows = total.shape[0]
    high = total.astype(jnp.bfloat16)
    low = (total - high.astype(jnp.float32)).astype(jnp.bfloat16)
    both = jnp.concatenate([high, low], axis=0)
    half = out_ref.shape[1]
    step = math.gcd(half, 512)
    for c in range(half // step):
        start = pl.multiple_of(side * half + c * step, step)
        product, at = None, 0
        for weight_ref in weights:
            depth = weight_ref.shape[0]
            part = jnp.dot(
                both[:, at : at + depth],
                weight_ref[:, pl.ds(start, step)],
                preferred_element_type=jnp.float32,
            )
            product = part if product is None else product + part
            at += depth
        out_ref[:, c * step : (c + 1) * step] = product[:rows] + product[rows:]


def project(across, other, parts, weights):
    return call(
        functools.partial(project_kernel, across, other),
        jax.ShapeDtypeStruct((parts.shape[1], weights[0].shape[1] // 2), jnp.float32),
        in_specs=[in_vmem] * (1 + len(weights)),
    )(parts, *weights)


def on_device(count, queries, key_states, value_states, out_weight, turn_lengths, block_flags):
    across = key_states.shape[1] // HD
    down = count // across
    turns = turn_lengths.shape[0]

    def over(rows, shift):
        pairs = [(i, i - i % across + (i + shift) % across) for i in range(count)]
        return lax.ppermute(rows, "seq", pairs)

    def up(rows, distance, lowest=0):
        step = distance * across
        pairs = [(i, i + step) for i in range(lowest * across, count - step)]
        return lax.ppermute(rows, "seq", pairs)

    _, y = place(across)
    heads = []
    for shift in range(across):
        at = lax.rem(y + shift, across)
        heads.append(pair(pick(key_states, at, across), pick(value_states, at, across)))
    rows = join([heads[0]] + [over(heads[shift], shift) for shift in range(1, across)])
    rows, queries = lax.optimization_barrier((rows, queries))
    meta = lax.optimization_barrier(jnp.concatenate([turn_lengths, block_flags[0]]))
    padded = -(-count // 16) * 16
    flags = jnp.pad(meta[turns:], (0, padded - count))[:, None]
    groups = [pick(queries, lax.rem(y + shift, across), across) for shift in range(across)]
    sent = []
    for group in groups[1:]:
        under = jnp.broadcast_to(flags, (padded, group.shape[1])).astype(group.dtype)
        sent.append(jnp.concatenate([group, under], axis=0))
    flags = jnp.broadcast_to(flags, (padded, HD)).astype(jnp.float32)
    below = [rows, up(rows, 1)] + [None] * (down - 2)
    member, inverse = members(across, turns, meta, groups[0])
    far, inverse, *sent = lax.optimization_barrier((rows, inverse, *sent))
    others = [over(group, shift) for shift, group in enumerate(sent, 1)]
    for distance in range(3, down):
        below[distance] = up(far, distance)
    if down > 2:
        below[2] = up(below[1], 1, 1)
    depth = out_weight.shape[0]
    pieces = [4 * depth // 8, 2 * depth // 8, 2 * depth // 8]
    turned, flags, weight, *state = attend_first(
        across, flags, [groups[0], *others], rows, out_weight, pieces[0]
    )
    weights = [weight]
    out_piece = (count, turns // count, queries.shape[1] // across)
    stages = [[1]] + [list(range(d, min(d + 2, down))) for d in range(3, down, 2)] + [[2]]
    for number, distances in enumerate(stages):
        last = number == len(stages) - 1
        with_weight = number < 2
        state = attend_next(
            across,
            distances,
            turns,
            turned,
            flags,
            [below[distance] for distance in distances],
            state,
            (member, inverse) if last else None,
            out_piece,
            out_weight,
            sum(pieces[: len(weights)]) if with_weight else None,
            pieces[len(weights)] if with_weight else None,
        )
        if with_weight:
            *state, weight = state
            weights.append(weight)
    parts = lax.all_to_all(state[0], "seq", split_axis=0, concat_axis=0, tiled=True)
    theirs = project(across, True, parts, weights)
    theirs = lax.ppermute(theirs, "head", [(0, 1), (1, 0)])
    return project(across, False, parts, weights) + theirs


def solution(mesh):
    in_specs = (
        P(("conv", "seq"), "head"),
        P(("conv", "seq"), "head"),
        P(("conv", "seq"), "head"),
        P("head", None),
        P("conv"),
        P(("conv", "seq"), None),
    )
    out_specs = P(("conv", "seq"), "head")
    return jax.shard_map(
        functools.partial(on_device, mesh.shape["seq"]),
        mesh=mesh,
        in_specs=in_specs,
        out_specs=out_specs,
        check_vma=False,
    )
```

```python
import functools
import math

import jax
import jax.numpy as jnp
from jax import lax
from jax.experimental import pallas as pl
from jax.experimental.pallas import tpu as pltpu
from jax.sharding import PartitionSpec as P

HD = 128

big_negative = -1e30
log_two_e = 1.4426950408889634

big_limit = 45 * 1024 * 1024
short_flops, long_flops = 2e9, 4e9

in_vmem = pl.BlockSpec(memory_space=pltpu.VMEM)
in_smem = pl.BlockSpec(memory_space=pltpu.SMEM)
anywhere = pl.BlockSpec(memory_space=pl.ANY)


def place(across):
    index = lax.axis_index("seq")
    return index // across, lax.rem(index, across)


def block_at(z, y, e, across):
    return z * across + lax.rem(y - e + across, across)


def cost_of(flops):
    return pl.CostEstimate(flops=int(flops), bytes_accessed=1024, transcendentals=0)


def call(kernel, out_shape, **settings):
    limit = settings.pop("limit", 16 * 1024 * 1024)
    cost = cost_of(settings.pop("cost", 0))
    return pl.pallas_call(
        kernel,
        out_shape=out_shape,
        out_specs=jax.tree.map(lambda _: in_vmem, out_shape),
        compiler_params=pltpu.CompilerParams(vmem_limit_bytes=limit),
        cost_estimate=cost,
        **settings,
    )


def pick(rows, number, parts):
    width = rows.shape[1] // parts
    picked = rows[:, :width]
    for part in range(1, parts):
        picked = jnp.where(number == part, rows[:, part * width : (part + 1) * width], picked)
    return picked


def pair(keys, values):
    which = lax.broadcasted_iota(jnp.int32, (2,) + keys.shape, 0)
    return jnp.where(which == 0, keys[None], values[None])


def join_kernel(*refs):
    *parts, out_ref = refs
    for e, part in enumerate(parts):
        out_ref[e] = part[...]


def join(parts):
    shape = jax.ShapeDtypeStruct((len(parts),) + parts[0].shape, parts[0].dtype)
    return call(join_kernel, shape, in_specs=[in_vmem] * len(parts))(*parts)


def rows_update(turned_ref, rows_refs, switches, state, first):
    top, total_sum, totals = state
    across, _, columns = turned_ref.shape
    rows = rows_refs[0][0].shape[1]
    count = across * len(rows_refs)
    factor = log_two_e / math.sqrt(HD)
    keys = [jnp.concatenate([part[0] for part in parts], axis=0) for parts in rows_refs]
    values = [jnp.concatenate([part[1] for part in parts], axis=0).T for parts in rows_refs]
    logits = [
        [jnp.dot(part, turned_ref[e], preferred_element_type=jnp.float32) for part in keys]
        for e in range(across)
    ]
    if first:
        key_pos = lax.broadcasted_iota(jnp.int32, (rows, 1), 0)
        column = lax.broadcasted_iota(jnp.int32, (1, columns), 1)
        causal = key_pos <= lax.rem(column, rows)
    for e in range(across):
        blocks = [
            logits[e][b // across][b % across * rows : (b % across + 1) * rows] for b in range(count)
        ]
        if first:
            blocks[e] = jnp.where(causal, blocks[e], big_negative)
        new_top = None if first else top[e]
        for b in range(count):
            block_top = jnp.ceil(jnp.max(blocks[b], axis=0, keepdims=True) * factor)
            if switches[e][b] is not None:
                block_top = jnp.where(switches[e][b], block_top, big_negative)
            new_top = block_top if new_top is None else jnp.maximum(new_top, block_top)
        weights, block_sum = [], None
        for b in range(count):
            against = new_top
            if switches[e][b] is not None:
                against = jnp.where(switches[e][b], new_top, -big_negative)
            weights.append(jnp.exp2(blocks[b] * factor - against))
            part = jnp.sum(weights[b], axis=0, keepdims=True)
            block_sum = part if block_sum is None else block_sum + part
        update = None
        for i, part in enumerate(values):
            mine = weights[i * across : (i + 1) * across]
            mine = jnp.concatenate([w.astype(jnp.bfloat16) for w in mine], axis=0)
            part = jnp.dot(part, mine, preferred_element_type=jnp.float32)
            update = part if update is None else update + part
        if not first:
            rescale = jnp.exp2(top[e] - new_top)
            block_sum = total_sum[e] * rescale + block_sum
            update = totals[e] * rescale + update
        top[e] = new_top
        total_sum[e] = block_sum
        totals[e] = update


def switch_of(flags_ref, e, owner, columns, allowed=None):
    flag = flags_ref[e, pl.ds(jnp.maximum(owner, 0), 1), :]
    if allowed is not None:
        flag = flag * jnp.where(allowed, 1.0, 0.0)
    return jnp.concatenate([flag] * (columns // HD), axis=1) > 0.5


def weight_piece(weight_ref, out_ref, start, sem):
    return pltpu.make_async_copy(weight_ref.at[start : start + out_ref.shape[0]], out_ref, sem)


def member_kernel(across, turns, meta_ref, _, weight_ref, member_ref, inverse_ref, weight_out, rows_ref, copied):
    weight_copy = weight_piece(weight_ref, weight_out, 0, copied)
    weight_copy.start()
    z, y = place(across)
    columns = rows_ref.shape[1]
    repeat = member_ref.shape[1] // turns
    q_rows = columns // repeat
    owners = [block_at(z, y, e, across) for e in range(across)]
    column = lax.broadcasted_iota(jnp.int32, (1, columns), 1)
    for e in range(across):
        position = lax.rem(column, q_rows) + owners[e] * q_rows
        start = jnp.int32(0)
        for t in range(turns):
            length = meta_ref[t]
            inside = (position >= start) & (position < start + length)
            rows_ref[t : t + 1, :] = jnp.where(inside, 1.0, 0.0)
            if e == 0:
                count = jnp.full((1, HD), length, jnp.int32).astype(jnp.float32)
                inverse_ref[t : t + 1, :] = 1.0 / count
            start = start + length
        for r in range(repeat):
            mine = (column >= r * q_rows) & (column < (r + 1) * q_rows)
            member_ref[e, r * turns : (r + 1) * turns, :] = jnp.where(
                mine, rows_ref[...], 0.0
            ).astype(jnp.bfloat16)
    weight_copy.wait()


def members(across, turns, meta, group, weight, piece):
    q_rows, width = group.shape
    repeat = width // HD
    columns = repeat * q_rows
    return call(
        functools.partial(member_kernel, across, turns),
        [
            jax.ShapeDtypeStruct((across, repeat * turns, columns), jnp.bfloat16),
            jax.ShapeDtypeStruct((turns, HD), jnp.float32),
            jax.ShapeDtypeStruct((piece, weight.shape[1]), weight.dtype),
        ],
        in_specs=[in_smem, anywhere, anywhere],
        scratch_shapes=[pltpu.VMEM((turns, columns), jnp.float32), pltpu.SemaphoreType.DMA(())],
        limit=big_limit,
        cost=long_flops,
    )(meta, group, weight)


def first_kernel(across, weight_at, own_flags_ref, *refs):
    queries, refs = refs[:across], refs[across:]
    kv_ref, weight_ref, turned_ref, flags_ref, weight_out = refs[:5]
    state, copied = refs[5:8], refs[8]
    weight_copy = weight_piece(weight_ref, weight_out, weight_at, copied)
    weight_copy.start()
    z, y = place(across)
    q_rows = kv_ref.shape[2]
    repeat = queries[0].shape[1] // HD
    columns = repeat * q_rows
    for e in range(across):
        for r in range(repeat):
            turned_ref[e, :, r * q_rows : (r + 1) * q_rows] = queries[e][
                0:q_rows, r * HD : (r + 1) * HD
            ].T
    flags_ref[0] = own_flags_ref[...]
    for e in range(1, across):
        flags_ref[e] = queries[e][q_rows:, 0:HD].astype(jnp.float32)
    owners = [block_at(z, y, e, across) for e in range(across)]
    switches = [
        [
            None if e == b else switch_of(flags_ref, e, owners[b], columns, owners[b] < owners[e])
            for b in range(across)
        ]
        for e in range(across)
    ]
    rows_update(turned_ref, [[kv_ref.at[e] for e in range(across)]], switches, state, True)

    weight_copy.wait()


def attend_first(across, flags, queries, rows, weight, at, piece):
    q_rows = rows.shape[2]
    repeat = queries[0].shape[1] // HD
    columns = repeat * q_rows
    f32, b16 = jnp.float32, jnp.bfloat16
    return call(
        functools.partial(first_kernel, across, at),
        [
            jax.ShapeDtypeStruct((across, HD, columns), b16),
            jax.ShapeDtypeStruct((across,) + flags.shape, f32),
            jax.ShapeDtypeStruct((piece, weight.shape[1]), weight.dtype),
            jax.ShapeDtypeStruct((across, 1, columns), f32),
            jax.ShapeDtypeStruct((across, 1, columns), f32),
            jax.ShapeDtypeStruct((across, HD, columns), f32),
        ],
        in_specs=[in_vmem] * (across + 2) + [anywhere],
        scratch_shapes=[pltpu.SemaphoreType.DMA(())],
        limit=big_limit,
    )(flags, *queries, rows, weight)


def next_kernel(across, distances, turns, last, weight_at, flags_ref, turned_ref, *refs):
    below = []
    for distance in distances:
        if distance < 3:
            below.append([refs[0].at[e] for e in range(across)])
            refs = refs[1:]
        else:
            below.append(refs[:across])
            refs = refs[across:]
    state, refs = refs[:3], refs[3:]
    if weight_at is not None:
        weight_ref, weight_out, copied = refs[0], refs[-2], refs[-1]
        refs = refs[1:-2]
        weight_copy = weight_piece(weight_ref, weight_out, weight_at, copied)
        weight_copy.start()
    z, y = place(across)
    columns = turned_ref.shape[2]

    def update(rows, from_distances):
        switches = [
            [
                switch_of(flags_ref, e, block_at(z - distance, y, b, across), columns)
                for distance in from_distances
                for b in range(across)
            ]
            for e in range(across)
        ]
        rows_update(turned_ref, rows, switches, state, False)

    for number, distance in enumerate(distances, 1):
        here = (z >= distance) if number == len(distances) else (z == distance)
        pl.when(here)(functools.partial(update, below[:number], distances[:number]))

    if weight_at is not None:
        weight_copy.wait()
    if last:
        member_ref, inverse_ref, out_ref = refs
        rows = out_ref.shape[1]
        pooled = None
        for e in range(across):
            attended = (state[2][e] / state[1][e]).astype(jnp.bfloat16)
            part = lax.dot_general(
                member_ref[e],
                attended,
                (((1,), (1,)), ((), ())),
                preferred_element_type=jnp.float32,
            )
            pooled = part if pooled is None else pooled + part
        for r in range(pooled.shape[0] // turns):
            mean = pooled[r * turns : (r + 1) * turns] * inverse_ref[...]
            for s in range(out_ref.shape[0]):
                out_ref[s, :, r * HD : (r + 1) * HD] = mean[s * rows : (s + 1) * rows]


def attend_next(across, distances, turns, turned, flags, below, state, pool, out_piece, weight, at, piece):
    last = pool is not None
    args = [flags, turned, *below, *state]
    in_specs = [in_vmem] * len(args)
    aliases, scratch = {}, []
    if at is not None:
        args.append(weight)
        in_specs.append(anywhere)
        scratch = [pltpu.SemaphoreType.DMA(())]
    if last:
        args += list(pool)
        in_specs += [in_vmem] * len(pool)
        out_shape = [jax.ShapeDtypeStruct(out_piece, jnp.float32)]
    else:
        out_shape = [jax.ShapeDtypeStruct(part.shape, part.dtype) for part in state]
        aliases = {2 + len(below) + i: i for i in range(len(state))}
    if at is not None:
        out_shape.append(jax.ShapeDtypeStruct((piece, weight.shape[1]), weight.dtype))
    return call(
        functools.partial(next_kernel, across, distances, turns, last, at),
        out_shape,
        in_specs=in_specs,
        scratch_shapes=scratch,
        input_output_aliases=aliases,
        cost=short_flops,
        limit=big_limit if at is not None else 16 * 1024 * 1024,
    )(*args)


def project_kernel(across, other, parts_ref, *refs):
    weights, out_ref = refs[:-1], refs[-1]
    side = lax.axis_index("head")
    if other:
        side = 1 - side
    groups = []
    for y in range(across):
        total = parts_ref[y]
        for s in range(y + across, parts_ref.shape[0], across):
            total = total + parts_ref[s]
        groups.append(total)
    total = jnp.concatenate(groups, axis=1)
    rows = total.shape[0]
    high = total.astype(jnp.bfloat16)
    low = (total - high.astype(jnp.float32)).astype(jnp.bfloat16)
    both = jnp.concatenate([high, low], axis=0)
    half = out_ref.shape[1]
    step = math.gcd(half, 512)
    for c in range(half // step):
        start = pl.multiple_of(side * half + c * step, step)
        product, at = None, 0
        for weight_ref in weights:
            depth = weight_ref.shape[0]
            part = jnp.dot(
                both[:, at : at + depth],
                weight_ref[:, pl.ds(start, step)],
                preferred_element_type=jnp.float32,
            )
            product = part if product is None else product + part
            at += depth
        out_ref[:, c * step : (c + 1) * step] = product[:rows] + product[rows:]


def project(across, other, parts, weights):
    return call(
        functools.partial(project_kernel, across, other),
        jax.ShapeDtypeStruct((parts.shape[1], weights[0].shape[1] // 2), jnp.float32),
        in_specs=[in_vmem] * (1 + len(weights)),
    )(parts, *weights)


def on_device(count, queries, key_states, value_states, out_weight, turn_lengths, block_flags):
    across = key_states.shape[1] // HD
    down = count // across
    turns = turn_lengths.shape[0]

    def over(rows, shift):
        pairs = [(i, i - i % across + (i + shift) % across) for i in range(count)]
        return lax.ppermute(rows, "seq", pairs)

    def up(rows, distance, lowest=0):
        step = distance * across
        pairs = [(i, i + step) for i in range(lowest * across, count - step)]
        return lax.ppermute(rows, "seq", pairs)

    depth = out_weight.shape[0]
    pieces = [depth // 8, 4 * depth // 8, 2 * depth // 8, depth // 8]
    _, y = place(across)
    heads = []
    for shift in range(across):
        at = lax.rem(y + shift, across)
        heads.append(pair(pick(key_states, at, across), pick(value_states, at, across)))
    swapped = [over(heads[shift], shift) for shift in range(1, across)]
    rows = join([heads[0]] + swapped)
    rows, queries = lax.optimization_barrier((rows, queries))
    meta = lax.optimization_barrier(jnp.concatenate([turn_lengths, block_flags[0]]))
    padded = -(-count // 16) * 16
    flags = jnp.pad(meta[turns:], (0, padded - count))[:, None]
    groups = [pick(queries, lax.rem(y + shift, across), across) for shift in range(across)]
    sent = []
    for group in groups[1:]:
        under = jnp.broadcast_to(flags, (padded, group.shape[1])).astype(group.dtype)
        sent.append(jnp.concatenate([group, under], axis=0))
    flags = jnp.broadcast_to(flags, (padded, HD)).astype(jnp.float32)
    below = [[rows], up(rows, 1)] + [None] * (down - 2)
    early = [up(heads[0], distance) for distance in range(3, down)]
    member, inverse, weight = members(across, turns, meta, groups[0], out_weight, pieces[0])
    inverse, *swapped = lax.optimization_barrier((inverse, *swapped))
    others = [over(group, shift) for shift, group in enumerate(sent, 1)]
    below[1], *early = lax.optimization_barrier((below[1], *early))
    for distance in range(3, down):
        late = [up(part, distance) for part in swapped]
        below[distance] = [early[distance - 3]] + late
    if down > 2:
        below[2] = [up(below[1], 1, 1)]
    below[1] = [below[1]]
    weights = [weight]
    turned, flags, weight, *state = attend_first(
        across, flags, [groups[0], *others], rows, out_weight, pieces[0], pieces[1]
    )
    weights.append(weight)
    out_piece = (count, turns // count, queries.shape[1] // across)
    stages = [list(range(d, min(d + 2, down))) for d in range(3, down, 2)] + [[1], [2]]
    for number, distances in enumerate(stages):
        last = number == len(stages) - 1
        with_weight = last or distances == [1]
        state = attend_next(
            across,
            distances,
            turns,
            turned,
            flags,
            [part for distance in distances for part in below[distance]],
            state,
            (member, inverse) if last else None,
            out_piece,
            out_weight,
            sum(pieces[: len(weights)]) if with_weight else None,
            pieces[len(weights)] if with_weight else None,
        )
        if with_weight:
            *state, weight = state
            weights.append(weight)
    parts = lax.all_to_all(state[0], "seq", split_axis=0, concat_axis=0, tiled=True)
    theirs = project(across, True, parts, weights)
    theirs = lax.ppermute(theirs, "head", [(0, 1), (1, 0)])
    return project(across, False, parts, weights) + theirs


def solution(mesh):
    in_specs = (
        P(("conv", "seq"), "head"),
        P(("conv", "seq"), "head"),
        P(("conv", "seq"), "head"),
        P("head", None),
        P("conv"),
        P(("conv", "seq"), None),
    )
    out_specs = P(("conv", "seq"), "head")
    return jax.shard_map(
        functools.partial(on_device, mesh.shape["seq"]),
        mesh=mesh,
        in_specs=in_specs,
        out_specs=out_specs,
        check_vma=False,
    )
```

```python
import functools
import math

import jax
import jax.numpy as jnp
from jax import lax
from jax.experimental import pallas as pl
from jax.experimental.pallas import tpu as pltpu
from jax.sharding import PartitionSpec as P

HD = 128

big_negative = -1e30
log_two_e = 1.4426950408889634

big_limit = 45 * 1024 * 1024
small_cost = pl.CostEstimate(flops=1024, bytes_accessed=1024, transcendentals=0)

in_vmem = pl.BlockSpec(memory_space=pltpu.VMEM)
in_smem = pl.BlockSpec(memory_space=pltpu.SMEM)
anywhere = pl.BlockSpec(memory_space=pl.ANY)


def place(across):
    index = lax.axis_index("seq")
    return index // across, lax.rem(index, across)


def block_at(z, y, e, across):
    return z * across + lax.rem(y - e + across, across)


def call(kernel, out_shape, **settings):
    limit = settings.pop("limit", 16 * 1024 * 1024)
    return pl.pallas_call(
        kernel,
        out_shape=out_shape,
        out_specs=jax.tree.map(lambda _: in_vmem, out_shape),
        compiler_params=pltpu.CompilerParams(vmem_limit_bytes=limit),
        cost_estimate=small_cost,
        **settings,
    )


def pick(rows, number, parts):
    width = rows.shape[1] // parts
    picked = rows[:, :width]
    for part in range(1, parts):
        picked = jnp.where(number == part, rows[:, part * width : (part + 1) * width], picked)
    return picked


def pair(keys, values):
    which = lax.broadcasted_iota(jnp.int32, (2,) + keys.shape, 0)
    return jnp.where(which == 0, keys[None], values[None])


def join_kernel(*refs):
    *parts, out_ref = refs
    for e, part in enumerate(parts):
        out_ref[e] = part[...]


def join(parts):
    shape = jax.ShapeDtypeStruct((len(parts),) + parts[0].shape, parts[0].dtype)
    return call(join_kernel, shape, in_specs=[in_vmem] * len(parts))(*parts)


def rows_update(turned_ref, rows_refs, switches, state, first, keep=True):
    top, total_sum, totals = state
    across, _, columns = turned_ref.shape
    rows = rows_refs[0].shape[2]
    count = across * len(rows_refs)
    factor = log_two_e / math.sqrt(HD)
    keys = [kv_ref[:, 0].reshape(across * rows, HD) for kv_ref in rows_refs]
    values = [kv_ref[:, 1].reshape(across * rows, HD).T for kv_ref in rows_refs]
    logits = [
        [jnp.dot(part, turned_ref[e], preferred_element_type=jnp.float32) for part in keys]
        for e in range(across)
    ]
    if first:
        key_pos = lax.broadcasted_iota(jnp.int32, (rows, 1), 0)
        column = lax.broadcasted_iota(jnp.int32, (1, columns), 1)
        causal = key_pos <= lax.rem(column, rows)
    results = []
    for e in range(across):
        blocks = [
            logits[e][b // across][b % across * rows : (b % across + 1) * rows] for b in range(count)
        ]
        if first:
            blocks[e] = jnp.where(causal, blocks[e], big_negative)
        new_top = None if first else top[e]
        for b in range(count):
            block_top = jnp.ceil(jnp.max(blocks[b], axis=0, keepdims=True) * factor)
            if switches[e][b] is not None:
                block_top = jnp.where(switches[e][b], block_top, big_negative)
            new_top = block_top if new_top is None else jnp.maximum(new_top, block_top)
        weights, block_sum = [], None
        for b in range(count):
            against = new_top
            if switches[e][b] is not None:
                against = jnp.where(switches[e][b], new_top, -big_negative)
            weights.append(jnp.exp2(blocks[b] * factor - against))
            part = jnp.sum(weights[b], axis=0, keepdims=True)
            block_sum = part if block_sum is None else block_sum + part
        update = None
        for i, part in enumerate(values):
            mine = weights[i * across : (i + 1) * across]
            mine = jnp.concatenate([w.astype(jnp.bfloat16) for w in mine], axis=0)
            part = jnp.dot(part, mine, preferred_element_type=jnp.float32)
            update = part if update is None else update + part
        if not first:
            rescale = jnp.exp2(top[e] - new_top)
            block_sum = total_sum[e] * rescale + block_sum
            update = totals[e] * rescale + update
        if keep:
            top[e] = new_top
            total_sum[e] = block_sum
            totals[e] = update
        results.append((block_sum, update))
    return results


def switch_of(flags_ref, e, owner, columns, allowed=None):
    flag = flags_ref[e, pl.ds(jnp.maximum(owner, 0), 1), :]
    if allowed is not None:
        flag = flag * jnp.where(allowed, 1.0, 0.0)
    return jnp.concatenate([flag] * (columns // HD), axis=1) > 0.5


def member_kernel(across, turns, meta_ref, after_ref, member_ref, inverse_ref, rows_ref):
    del after_ref
    z, y = place(across)
    columns = rows_ref.shape[1]
    repeat = member_ref.shape[1] // turns
    q_rows = columns // repeat
    owners = [block_at(z, y, e, across) for e in range(across)]
    column = lax.broadcasted_iota(jnp.int32, (1, columns), 1)
    for e in range(across):
        position = lax.rem(column, q_rows) + owners[e] * q_rows
        start = jnp.int32(0)
        for t in range(turns):
            length = meta_ref[t]
            inside = (position >= start) & (position < start + length)
            rows_ref[t : t + 1, :] = jnp.where(inside, 1.0, 0.0)
            if e == 0:
                count = jnp.full((1, HD), length, jnp.int32).astype(jnp.float32)
                inverse_ref[t : t + 1, :] = 1.0 / count
            start = start + length
        for r in range(repeat):
            mine = (column >= r * q_rows) & (column < (r + 1) * q_rows)
            member_ref[e, r * turns : (r + 1) * turns, :] = jnp.where(
                mine, rows_ref[...], 0.0
            ).astype(jnp.bfloat16)


def members(across, turns, meta, group):
    q_rows, width = group.shape
    repeat = width // HD
    columns = repeat * q_rows
    return call(
        functools.partial(member_kernel, across, turns),
        [
            jax.ShapeDtypeStruct((across, repeat * turns, columns), jnp.bfloat16),
            jax.ShapeDtypeStruct((turns, HD), jnp.float32),
        ],
        in_specs=[in_smem, anywhere],
        scratch_shapes=[pltpu.VMEM((turns, columns), jnp.float32)],
    )(meta, group)


def weight_piece(weight_ref, out_ref, start, sem):
    return pltpu.make_async_copy(weight_ref.at[start : start + out_ref.shape[0]], out_ref, sem)


def first_kernel(across, own_flags_ref, *refs):
    queries, refs = refs[:across], refs[across:]
    kv_ref, weight_ref, turned_ref, flags_ref, weight_out = refs[:5]
    state, copied = refs[5:8], refs[8]
    weight_copy = weight_piece(weight_ref, weight_out, 0, copied)
    weight_copy.start()
    z, y = place(across)
    q_rows = kv_ref.shape[2]
    repeat = queries[0].shape[1] // HD
    columns = repeat * q_rows
    for e in range(across):
        for r in range(repeat):
            turned_ref[e, :, r * q_rows : (r + 1) * q_rows] = queries[e][
                0:q_rows, r * HD : (r + 1) * HD
            ].T
    flags_ref[0] = own_flags_ref[...]
    for e in range(1, across):
        flags_ref[e] = queries[e][q_rows:, 0:HD].astype(jnp.float32)
    owners = [block_at(z, y, e, across) for e in range(across)]
    switches = [
        [
            None if e == b else switch_of(flags_ref, e, owners[b], columns, owners[b] < owners[e])
            for b in range(across)
        ]
        for e in range(across)
    ]
    rows_update(turned_ref, [kv_ref], switches, state, True)

    weight_copy.wait()


def attend_first(across, flags, queries, rows, weight, piece):
    q_rows = rows.shape[2]
    repeat = queries[0].shape[1] // HD
    columns = repeat * q_rows
    f32, b16 = jnp.float32, jnp.bfloat16
    return call(
        functools.partial(first_kernel, across),
        [
            jax.ShapeDtypeStruct((across, HD, columns), b16),
            jax.ShapeDtypeStruct((across,) + flags.shape, f32),
            jax.ShapeDtypeStruct((piece, weight.shape[1]), weight.dtype),
            jax.ShapeDtypeStruct((across, 1, columns), f32),
            jax.ShapeDtypeStruct((across, 1, columns), f32),
            jax.ShapeDtypeStruct((across, HD, columns), f32),
        ],
        in_specs=[in_vmem] * (across + 2) + [anywhere],
        scratch_shapes=[pltpu.SemaphoreType.DMA(())],
        limit=big_limit,
    )(flags, *queries, rows, weight)


def next_kernel(across, distances, turns, last, weight_at, flags_ref, turned_ref, *refs):
    below_count = len(distances)
    below, state, refs = refs[:below_count], refs[below_count : below_count + 3], refs[below_count + 3 :]
    if weight_at is not None:
        weight_ref, weight_out, copied = refs[0], refs[-2], refs[-1]
        refs = refs[1:-2]
        weight_copy = weight_piece(weight_ref, weight_out, weight_at, copied)
        weight_copy.start()
    z, y = place(across)
    columns = turned_ref.shape[2]

    def update(rows, from_distances):
        switches = [
            [
                switch_of(flags_ref, e, block_at(z - distance, y, b, across), columns)
                for distance in from_distances
                for b in range(across)
            ]
            for e in range(across)
        ]
        results = rows_update(turned_ref, rows, switches, state, False, not last)
        if last:
            finish(results)

    def finish(results):
        member_ref, inverse_ref, out_ref = refs
        rows = out_ref.shape[1]
        pooled = None
        for e, (sums, totals) in enumerate(results):
            attended = (totals * (1.0 / sums)).astype(jnp.bfloat16)
            part = lax.dot_general(
                member_ref[e],
                attended,
                (((1,), (1,)), ((), ())),
                preferred_element_type=jnp.float32,
            )
            pooled = part if pooled is None else pooled + part
        for r in range(pooled.shape[0] // turns):
            mean = pooled[r * turns : (r + 1) * turns] * inverse_ref[...]
            for s in range(out_ref.shape[0]):
                out_ref[s, :, r * HD : (r + 1) * HD] = mean[s * rows : (s + 1) * rows]

    for number, distance in enumerate(distances, 1):
        here = (z >= distance) if number == len(distances) else (z == distance)
        pl.when(here)(functools.partial(update, below[:number], distances[:number]))
    if last:

        @pl.when(z < distances[0])
        def _():
            finish([(state[1][e], state[2][e]) for e in range(across)])

    if weight_at is not None:
        weight_copy.wait()


def attend_next(across, distances, turns, turned, flags, below, state, pool, out_piece, weight, at, piece):
    last = pool is not None
    args = [flags, turned, *below, *state]
    in_specs = [in_vmem] * len(args)
    aliases, scratch = {}, []
    if at is not None:
        args.append(weight)
        in_specs.append(anywhere)
        scratch = [pltpu.SemaphoreType.DMA(())]
    if last:
        args += list(pool)
        in_specs += [in_vmem] * len(pool)
        out_shape = [jax.ShapeDtypeStruct(out_piece, jnp.float32)]
    else:
        out_shape = [jax.ShapeDtypeStruct(part.shape, part.dtype) for part in state]
        aliases = {2 + len(below) + i: i for i in range(len(state))}
    if at is not None:
        out_shape.append(jax.ShapeDtypeStruct((piece, weight.shape[1]), weight.dtype))
    return call(
        functools.partial(next_kernel, across, distances, turns, last, at),
        out_shape,
        in_specs=in_specs,
        scratch_shapes=scratch,
        input_output_aliases=aliases,
        limit=big_limit if at is not None else 16 * 1024 * 1024,
    )(*args)


def project_kernel(across, other, parts_ref, *refs):
    weights, out_ref = refs[:-1], refs[-1]
    side = lax.axis_index("head")
    if other:
        side = 1 - side
    groups = []
    for y in range(across):
        total = parts_ref[y]
        for s in range(y + across, parts_ref.shape[0], across):
            total = total + parts_ref[s]
        groups.append(total)
    total = jnp.concatenate(groups, axis=1)
    rows = total.shape[0]
    high = total.astype(jnp.bfloat16)
    low = (total - high.astype(jnp.float32)).astype(jnp.bfloat16)
    both = jnp.concatenate([high, low], axis=0)
    half = out_ref.shape[1]
    step = math.gcd(half, 512)
    for c in range(half // step):
        start = pl.multiple_of(side * half + c * step, step)
        product, at = None, 0
        for weight_ref in weights:
            depth = weight_ref.shape[0]
            part = jnp.dot(
                both[:, at : at + depth],
                weight_ref[:, pl.ds(start, step)],
                preferred_element_type=jnp.float32,
            )
            product = part if product is None else product + part
            at += depth
        out_ref[:, c * step : (c + 1) * step] = product[:rows] + product[rows:]


def project(across, other, parts, weights):
    return call(
        functools.partial(project_kernel, across, other),
        jax.ShapeDtypeStruct((parts.shape[1], weights[0].shape[1] // 2), jnp.float32),
        in_specs=[in_vmem] * (1 + len(weights)),
    )(parts, *weights)


def on_device(count, queries, key_states, value_states, out_weight, turn_lengths, block_flags):
    across = key_states.shape[1] // HD
    down = count // across
    turns = turn_lengths.shape[0]

    def over(rows, shift):
        pairs = [(i, i - i % across + (i + shift) % across) for i in range(count)]
        return lax.ppermute(rows, "seq", pairs)

    def up(rows, distance, lowest=0):
        step = distance * across
        pairs = [(i, i + step) for i in range(lowest * across, count - step)]
        return lax.ppermute(rows, "seq", pairs)

    _, y = place(across)
    def head_of(shift):
        at = lax.rem(y + shift, across)
        return pair(pick(key_states, at, across), pick(value_states, at, across))

    heads = [head_of(shift) for shift in range(1, across)]
    *heads, key_states, value_states = lax.optimization_barrier((*heads, key_states, value_states))
    heads = [head_of(0)] + heads
    rows = join([heads[0]] + [over(heads[shift], shift) for shift in range(1, across)])
    rows, queries = lax.optimization_barrier((rows, queries))
    meta = lax.optimization_barrier(jnp.concatenate([turn_lengths, block_flags[0]]))
    padded = -(-count // 16) * 16
    flags = jnp.pad(meta[turns:], (0, padded - count))[:, None]
    groups = [pick(queries, lax.rem(y + shift, across), across) for shift in range(across)]
    sent = []
    for group in groups[1:]:
        under = jnp.broadcast_to(flags, (padded, group.shape[1])).astype(group.dtype)
        sent.append(jnp.concatenate([group, under], axis=0))
    flags = jnp.broadcast_to(flags, (padded, HD)).astype(jnp.float32)
    below = [rows, up(rows, 1)] + [None] * (down - 2)
    member, inverse = members(across, turns, meta, groups[0])
    far, inverse, *sent = lax.optimization_barrier((rows, inverse, *sent))
    others = [over(group, shift) for shift, group in enumerate(sent, 1)]
    for distance in range(3, down):
        below[distance] = up(far, distance)
    if down > 2:
        below[2] = up(below[1], 1, 1)
    depth = out_weight.shape[0]
    pieces = [4 * depth // 8, 2 * depth // 8, 2 * depth // 8]
    turned, flags, weight, *state = attend_first(
        across, flags, [groups[0], *others], rows, out_weight, pieces[0]
    )
    weights = [weight]
    out_piece = (count, turns // count, queries.shape[1] // across)
    stages = [[1]] + [list(range(d, min(d + 2, down))) for d in range(3, down, 2)] + [[2]]
    for number, distances in enumerate(stages):
        last = number == len(stages) - 1
        with_weight = number < 2
        state = attend_next(
            across,
            distances,
            turns,
            turned,
            flags,
            [below[distance] for distance in distances],
            state,
            (member, inverse) if last else None,
            out_piece,
            out_weight,
            sum(pieces[: len(weights)]) if with_weight else None,
            pieces[len(weights)] if with_weight else None,
        )
        if with_weight:
            *state, weight = state
            weights.append(weight)
    parts = lax.all_to_all(state[0], "seq", split_axis=0, concat_axis=0, tiled=True)
    theirs = project(across, True, parts, weights)
    theirs = lax.ppermute(theirs, "head", [(0, 1), (1, 0)])
    return project(across, False, parts, weights) + theirs


def solution(mesh):
    in_specs = (
        P(("conv", "seq"), "head"),
        P(("conv", "seq"), "head"),
        P(("conv", "seq"), "head"),
        P("head", None),
        P("conv"),
        P(("conv", "seq"), None),
    )
    out_specs = P(("conv", "seq"), "head")
    return jax.shard_map(
        functools.partial(on_device, mesh.shape["seq"]),
        mesh=mesh,
        in_specs=in_specs,
        out_specs=out_specs,
        check_vma=False,
    )
```

```python
import functools
import math

import jax
import jax.numpy as jnp
from jax import lax
from jax.experimental import pallas as pl
from jax.experimental.pallas import tpu as pltpu
from jax.sharding import PartitionSpec as P

HD = 128

big_negative = -1e30
log_two_e = 1.4426950408889634

big_limit = 45 * 1024 * 1024
small_cost = pl.CostEstimate(flops=1024, bytes_accessed=1024, transcendentals=0)

in_vmem = pl.BlockSpec(memory_space=pltpu.VMEM)
in_smem = pl.BlockSpec(memory_space=pltpu.SMEM)
anywhere = pl.BlockSpec(memory_space=pl.ANY)


def place(across):
    index = lax.axis_index("seq")
    return index // across, lax.rem(index, across)


def block_at(z, y, e, across):
    return z * across + lax.rem(y - e + across, across)


def call(kernel, out_shape, **settings):
    limit = settings.pop("limit", 16 * 1024 * 1024)
    return pl.pallas_call(
        kernel,
        out_shape=out_shape,
        out_specs=jax.tree.map(lambda _: in_vmem, out_shape),
        compiler_params=pltpu.CompilerParams(vmem_limit_bytes=limit),
        cost_estimate=small_cost,
        **settings,
    )


def pick(rows, number, parts):
    width = rows.shape[1] // parts
    picked = rows[:, :width]
    for part in range(1, parts):
        picked = jnp.where(number == part, rows[:, part * width : (part + 1) * width], picked)
    return picked


def pair(keys, values):
    which = lax.broadcasted_iota(jnp.int32, (2,) + keys.shape, 0)
    return jnp.where(which == 0, keys[None], values[None])


def join_kernel(*refs):
    *parts, out_ref = refs
    at = 0
    for part in parts:
        size = min(part.shape[0], out_ref.shape[0] - at)
        out_ref[at : at + size] = part[:size]
        at += size


def join_parts(parts, count):
    return join(parts, count)


def join(parts, count=None):
    count = sum(part.shape[0] for part in parts) if count is None else count
    shape = jax.ShapeDtypeStruct((count,) + parts[0].shape[1:], parts[0].dtype)
    return call(join_kernel, shape, in_specs=[in_vmem] * len(parts))(*parts)


def rows_update(turned_ref, rows_refs, switches, state, first):
    top, total_sum, totals = state
    across, _, columns = turned_ref.shape
    rows = rows_refs[0].shape[1]
    count = across * len(rows_refs)
    factor = log_two_e / math.sqrt(HD)
    keys = [
        jnp.concatenate([kv_ref[2 * e] for e in range(across)], axis=0) for kv_ref in rows_refs
    ]
    values = [
        jnp.concatenate([kv_ref[2 * e + 1] for e in range(across)], axis=0).T for kv_ref in rows_refs
    ]
    logits = [
        [jnp.dot(part, turned_ref[e], preferred_element_type=jnp.float32) for part in keys]
        for e in range(across)
    ]
    if first:
        key_pos = lax.broadcasted_iota(jnp.int32, (rows, 1), 0)
        column = lax.broadcasted_iota(jnp.int32, (1, columns), 1)
        causal = key_pos <= lax.rem(column, rows)
    for e in range(across):
        blocks = [
            logits[e][b // across][b % across * rows : (b % across + 1) * rows] for b in range(count)
        ]
        if first:
            blocks[e] = jnp.where(causal, blocks[e], big_negative)
        new_top = None if first else top[e]
        for b in range(count):
            block_top = jnp.ceil(jnp.max(blocks[b], axis=0, keepdims=True) * factor)
            if switches[e][b] is not None:
                block_top = jnp.where(switches[e][b], block_top, big_negative)
            new_top = block_top if new_top is None else jnp.maximum(new_top, block_top)
        weights, block_sum = [], None
        for b in range(count):
            against = new_top
            if switches[e][b] is not None:
                against = jnp.where(switches[e][b], new_top, -big_negative)
            weights.append(jnp.exp2(blocks[b] * factor - against))
            part = jnp.sum(weights[b], axis=0, keepdims=True)
            block_sum = part if block_sum is None else block_sum + part
        update = None
        for i, part in enumerate(values):
            mine = weights[i * across : (i + 1) * across]
            mine = jnp.concatenate([w.astype(jnp.bfloat16) for w in mine], axis=0)
            part = jnp.dot(part, mine, preferred_element_type=jnp.float32)
            update = part if update is None else update + part
        if not first:
            rescale = jnp.exp2(top[e] - new_top)
            block_sum = total_sum[e] * rescale + block_sum
            update = totals[e] * rescale + update
        top[e] = new_top
        total_sum[e] = block_sum
        totals[e] = update


def switch_of(flags_ref, e, owner, columns, allowed=None):
    flag = flags_ref[e, pl.ds(jnp.maximum(owner, 0), 1), :]
    if allowed is not None:
        flag = flag * jnp.where(allowed, 1.0, 0.0)
    return jnp.concatenate([flag] * (columns // HD), axis=1) > 0.5


def member_kernel(across, turns, meta_ref, after_ref, member_ref, inverse_ref, rows_ref):
    del after_ref
    z, y = place(across)
    columns = rows_ref.shape[1]
    repeat = member_ref.shape[1] // turns
    q_rows = columns // repeat
    owners = [block_at(z, y, e, across) for e in range(across)]
    column = lax.broadcasted_iota(jnp.int32, (1, columns), 1)
    for e in range(across):
        position = lax.rem(column, q_rows) + owners[e] * q_rows
        start = jnp.int32(0)
        for t in range(turns):
            length = meta_ref[t]
            inside = (position >= start) & (position < start + length)
            rows_ref[t : t + 1, :] = jnp.where(inside, 1.0, 0.0)
            if e == 0:
                count = jnp.full((1, HD), length, jnp.int32).astype(jnp.float32)
                inverse_ref[t : t + 1, :] = 1.0 / count
            start = start + length
        for r in range(repeat):
            mine = (column >= r * q_rows) & (column < (r + 1) * q_rows)
            member_ref[e, r * turns : (r + 1) * turns, :] = jnp.where(
                mine, rows_ref[...], 0.0
            ).astype(jnp.bfloat16)


def members(across, turns, meta, group):
    q_rows, width = group.shape
    repeat = width // HD
    columns = repeat * q_rows
    return call(
        functools.partial(member_kernel, across, turns),
        [
            jax.ShapeDtypeStruct((across, repeat * turns, columns), jnp.bfloat16),
            jax.ShapeDtypeStruct((turns, HD), jnp.float32),
        ],
        in_specs=[in_smem, anywhere],
        scratch_shapes=[pltpu.VMEM((turns, columns), jnp.float32)],
    )(meta, group)


def weight_piece(weight_ref, out_ref, start, sem):
    return pltpu.make_async_copy(weight_ref.at[start : start + out_ref.shape[0]], out_ref, sem)


def first_kernel(across, own_flags_ref, *refs):
    queries, refs = refs[:across], refs[across:]
    kv_ref, weight_ref, turned_ref, flags_ref, weight_out = refs[:5]
    state, copied = refs[5:8], refs[8]
    weight_copy = weight_piece(weight_ref, weight_out, 0, copied)
    weight_copy.start()
    z, y = place(across)
    q_rows = kv_ref.shape[1]
    repeat = queries[0].shape[1] // HD
    columns = repeat * q_rows
    for e in range(across):
        for r in range(repeat):
            turned_ref[e, :, r * q_rows : (r + 1) * q_rows] = queries[e][
                0:q_rows, r * HD : (r + 1) * HD
            ].T
    flags_ref[0] = own_flags_ref[...]
    for e in range(1, across):
        flags_ref[e] = queries[e][q_rows:, 0:HD].astype(jnp.float32)
    owners = [block_at(z, y, e, across) for e in range(across)]
    switches = [
        [
            None if e == b else switch_of(flags_ref, e, owners[b], columns, owners[b] < owners[e])
            for b in range(across)
        ]
        for e in range(across)
    ]
    rows_update(turned_ref, [kv_ref], switches, state, True)

    weight_copy.wait()


def attend_first(across, flags, queries, rows, weight, piece):
    q_rows = rows.shape[1]
    repeat = queries[0].shape[1] // HD
    columns = repeat * q_rows
    f32, b16 = jnp.float32, jnp.bfloat16
    return call(
        functools.partial(first_kernel, across),
        [
            jax.ShapeDtypeStruct((across, HD, columns), b16),
            jax.ShapeDtypeStruct((across,) + flags.shape, f32),
            jax.ShapeDtypeStruct((piece, weight.shape[1]), weight.dtype),
            jax.ShapeDtypeStruct((across, 1, columns), f32),
            jax.ShapeDtypeStruct((across, 1, columns), f32),
            jax.ShapeDtypeStruct((across, HD, columns), f32),
        ],
        in_specs=[in_vmem] * (across + 2) + [anywhere],
        scratch_shapes=[pltpu.SemaphoreType.DMA(())],
        limit=big_limit,
    )(flags, *queries, rows, weight)


def next_kernel(across, distances, turns, last, weight_at, flags_ref, turned_ref, *refs):
    below_count = len(distances)
    below, state, refs = refs[:below_count], refs[below_count : below_count + 3], refs[below_count + 3 :]
    if weight_at is not None:
        weight_ref, weight_out, copied = refs[0], refs[-2], refs[-1]
        refs = refs[1:-2]
        weight_copy = weight_piece(weight_ref, weight_out, weight_at, copied)
        weight_copy.start()
    z, y = place(across)
    columns = turned_ref.shape[2]

    def update(rows, from_distances):
        switches = [
            [
                switch_of(flags_ref, e, block_at(z - distance, y, b, across), columns)
                for distance in from_distances
                for b in range(across)
            ]
            for e in range(across)
        ]
        rows_update(turned_ref, rows, switches, state, False)

    for number, distance in enumerate(distances, 1):
        here = (z >= distance) if number == len(distances) else (z == distance)
        pl.when(here)(functools.partial(update, below[:number], distances[:number]))

    if weight_at is not None:
        weight_copy.wait()
    if last:
        member_ref, inverse_ref, out_ref = refs
        rows = out_ref.shape[1]
        pooled = None
        for e in range(across):
            attended = (state[2][e] / state[1][e]).astype(jnp.bfloat16)
            part = lax.dot_general(
                member_ref[e],
                attended,
                (((1,), (1,)), ((), ())),
                preferred_element_type=jnp.float32,
            )
            pooled = part if pooled is None else pooled + part
        for r in range(pooled.shape[0] // turns):
            mean = pooled[r * turns : (r + 1) * turns] * inverse_ref[...]
            for s in range(out_ref.shape[0]):
                out_ref[s, :, r * HD : (r + 1) * HD] = mean[s * rows : (s + 1) * rows]


def attend_next(across, distances, turns, turned, flags, below, state, pool, out_piece, weight, at, piece):
    last = pool is not None
    args = [flags, turned, *below, *state]
    in_specs = [in_vmem] * len(args)
    aliases, scratch = {}, []
    if at is not None:
        args.append(weight)
        in_specs.append(anywhere)
        scratch = [pltpu.SemaphoreType.DMA(())]
    if last:
        args += list(pool)
        in_specs += [in_vmem] * len(pool)
        out_shape = [jax.ShapeDtypeStruct(out_piece, jnp.float32)]
    else:
        out_shape = [jax.ShapeDtypeStruct(part.shape, part.dtype) for part in state]
        aliases = {2 + len(below) + i: i for i in range(len(state))}
    if at is not None:
        out_shape.append(jax.ShapeDtypeStruct((piece, weight.shape[1]), weight.dtype))
    return call(
        functools.partial(next_kernel, across, distances, turns, last, at),
        out_shape,
        in_specs=in_specs,
        scratch_shapes=scratch,
        input_output_aliases=aliases,
        limit=big_limit if at is not None else 16 * 1024 * 1024,
    )(*args)


def project_kernel(across, other, parts_ref, *refs):
    weights, out_ref = refs[:-1], refs[-1]
    side = lax.axis_index("head")
    if other:
        side = 1 - side
    groups = []
    for y in range(across):
        total = parts_ref[y]
        for s in range(y + across, parts_ref.shape[0], across):
            total = total + parts_ref[s]
        groups.append(total)
    total = jnp.concatenate(groups, axis=1)
    rows = total.shape[0]
    high = total.astype(jnp.bfloat16)
    low = (total - high.astype(jnp.float32)).astype(jnp.bfloat16)
    both = jnp.concatenate([high, low], axis=0)
    half = out_ref.shape[1]
    step = math.gcd(half, 512)
    for c in range(half // step):
        start = pl.multiple_of(side * half + c * step, step)
        product, at = None, 0
        for weight_ref in weights:
            depth = weight_ref.shape[0]
            part = jnp.dot(
                both[:, at : at + depth],
                weight_ref[:, pl.ds(start, step)],
                preferred_element_type=jnp.float32,
            )
            product = part if product is None else product + part
            at += depth
        out_ref[:, c * step : (c + 1) * step] = product[:rows] + product[rows:]


def project(across, other, parts, weights):
    return call(
        functools.partial(project_kernel, across, other),
        jax.ShapeDtypeStruct((parts.shape[1], weights[0].shape[1] // 2), jnp.float32),
        in_specs=[in_vmem] * (1 + len(weights)),
    )(parts, *weights)


def on_device(count, queries, key_states, value_states, out_weight, turn_lengths, block_flags):
    across = key_states.shape[1] // HD
    down = count // across
    turns = turn_lengths.shape[0]

    def over(rows, shift):
        pairs = [(i, i - i % across + (i + shift) % across) for i in range(count)]
        return lax.ppermute(rows, "seq", pairs)

    def up(rows, distance, lowest=0):
        step = distance * across
        pairs = [(i, i + step) for i in range(lowest * across, count - step)]
        return lax.ppermute(rows, "seq", pairs)

    _, y = place(across)
    heads = []
    for shift in range(across):
        at = lax.rem(y + shift, across)
        heads.append(pair(pick(key_states, at, across), pick(value_states, at, across)))
    swapped = [over(heads[shift], shift) for shift in range(1, across)]
    rows = join([heads[0]] + swapped)
    first = up(heads[0], 1)
    rest = up(join(swapped), 1)
    rows, queries = lax.optimization_barrier((rows, queries))
    meta = lax.optimization_barrier(jnp.concatenate([turn_lengths, block_flags[0]]))
    padded = -(-count // 16) * 16
    flags = jnp.pad(meta[turns:], (0, padded - count))[:, None]
    groups = [pick(queries, lax.rem(y + shift, across), across) for shift in range(across)]
    sent = []
    for group in groups[1:]:
        under = jnp.broadcast_to(flags, (padded, group.shape[1])).astype(group.dtype)
        sent.append(jnp.concatenate([group, under], axis=0))
    flags = jnp.broadcast_to(flags, (padded, HD)).astype(jnp.float32)
    below = [rows, join_parts([first, rest], 2 * across)] + [None] * (down - 2)
    far, *sent = lax.optimization_barrier((rows, *sent))
    others = [over(group, shift) for shift, group in enumerate(sent, 1)]
    for distance in range(3, down):
        below[distance] = up(far, distance)
    if down > 2:
        below[2] = up(below[1], 1, 1)
    member, inverse = members(across, turns, meta, groups[0])
    inverse, flags = lax.optimization_barrier((inverse, flags))
    depth = out_weight.shape[0]
    pieces = [4 * depth // 8, 2 * depth // 8, 2 * depth // 8]
    turned, flags, weight, *state = attend_first(
        across, flags, [groups[0], *others], rows, out_weight, pieces[0]
    )
    weights = [weight]
    out_piece = (count, turns // count, queries.shape[1] // across)
    stages = [[1]] + [list(range(d, min(d + 2, down))) for d in range(3, down, 2)] + [[2]]
    for number, distances in enumerate(stages):
        last = number == len(stages) - 1
        with_weight = number < 2
        state = attend_next(
            across,
            distances,
            turns,
            turned,
            flags,
            [below[distance] for distance in distances],
            state,
            (member, inverse) if last else None,
            out_piece,
            out_weight,
            sum(pieces[: len(weights)]) if with_weight else None,
            pieces[len(weights)] if with_weight else None,
        )
        if with_weight:
            *state, weight = state
            weights.append(weight)
    parts = lax.all_to_all(state[0], "seq", split_axis=0, concat_axis=0, tiled=True)
    theirs = project(across, True, parts, weights)
    theirs = lax.ppermute(theirs, "head", [(0, 1), (1, 0)])
    return project(across, False, parts, weights) + theirs


def solution(mesh):
    in_specs = (
        P(("conv", "seq"), "head"),
        P(("conv", "seq"), "head"),
        P(("conv", "seq"), "head"),
        P("head", None),
        P("conv"),
        P(("conv", "seq"), None),
    )
    out_specs = P(("conv", "seq"), "head")
    return jax.shard_map(
        functools.partial(on_device, mesh.shape["seq"]),
        mesh=mesh,
        in_specs=in_specs,
        out_specs=out_specs,
        check_vma=False,
    )
```

```python
import functools
import math

import jax
import jax.numpy as jnp
from jax import lax
from jax.experimental import pallas as pl
from jax.experimental.pallas import tpu as pltpu
from jax.sharding import PartitionSpec as P

HD = 128

big_negative = -1e30
log_two_e = 1.4426950408889634

big_limit = 45 * 1024 * 1024
long_flops = 4 * 10**9

in_vmem = pl.BlockSpec(memory_space=pltpu.VMEM)
in_smem = pl.BlockSpec(memory_space=pltpu.SMEM)
anywhere = pl.BlockSpec(memory_space=pl.ANY)


def place(across):
    index = lax.axis_index("seq")
    return index // across, lax.rem(index, across)


def block_at(z, y, e, across):
    return z * across + lax.rem(y - e + across, across)


def call(kernel, out_shape, **settings):
    limit = settings.pop("limit", 16 * 1024 * 1024)
    flops = settings.pop("flops", 1024)
    return pl.pallas_call(
        kernel,
        out_shape=out_shape,
        out_specs=jax.tree.map(lambda _: in_vmem, out_shape),
        compiler_params=pltpu.CompilerParams(vmem_limit_bytes=limit),
        cost_estimate=pl.CostEstimate(flops=flops, bytes_accessed=1024, transcendentals=0),
        **settings,
    )


def pick(rows, number, parts):
    width = rows.shape[1] // parts
    picked = rows[:, :width]
    for part in range(1, parts):
        picked = jnp.where(number == part, rows[:, part * width : (part + 1) * width], picked)
    return picked


def pair(keys, values):
    which = lax.broadcasted_iota(jnp.int32, (2,) + keys.shape, 0)
    return jnp.where(which == 0, keys[None], values[None])


def join_kernel(*refs):
    *parts, out_ref = refs
    at = 0
    for part in parts:
        out_ref[at : at + part.shape[0]] = part[...]
        at += part.shape[0]


def join(parts, flops=1024):
    count = sum(part.shape[0] for part in parts)
    shape = jax.ShapeDtypeStruct((count,) + parts[0].shape[1:], parts[0].dtype)
    return call(join_kernel, shape, in_specs=[in_vmem] * len(parts), flops=flops)(*parts)


def rows_update(turned_ref, rows_refs, switches, state, first):
    top, total_sum, totals = state
    across, _, columns = turned_ref.shape
    rows = rows_refs[0].shape[1]
    count = across * len(rows_refs)
    factor = log_two_e / math.sqrt(HD)
    keys = [
        jnp.concatenate([kv_ref[2 * e] for e in range(across)], axis=0) for kv_ref in rows_refs
    ]
    values = [
        jnp.concatenate([kv_ref[2 * e + 1] for e in range(across)], axis=0).T for kv_ref in rows_refs
    ]
    logits = [
        [jnp.dot(part, turned_ref[e], preferred_element_type=jnp.float32) for part in keys]
        for e in range(across)
    ]
    if first:
        key_pos = lax.broadcasted_iota(jnp.int32, (rows, 1), 0)
        column = lax.broadcasted_iota(jnp.int32, (1, columns), 1)
        causal = key_pos <= lax.rem(column, rows)
    for e in range(across):
        blocks = [
            logits[e][b // across][b % across * rows : (b % across + 1) * rows] for b in range(count)
        ]
        if first:
            blocks[e] = jnp.where(causal, blocks[e], big_negative)
        new_top = None if first else top[e]
        for b in range(count):
            block_top = jnp.ceil(jnp.max(blocks[b], axis=0, keepdims=True) * factor)
            if switches[e][b] is not None:
                block_top = jnp.where(switches[e][b], block_top, big_negative)
            new_top = block_top if new_top is None else jnp.maximum(new_top, block_top)
        weights, block_sum = [], None
        for b in range(count):
            against = new_top
            if switches[e][b] is not None:
                against = jnp.where(switches[e][b], new_top, -big_negative)
            weights.append(jnp.exp2(blocks[b] * factor - against))
            part = jnp.sum(weights[b], axis=0, keepdims=True)
            block_sum = part if block_sum is None else block_sum + part
        update = None
        for i, part in enumerate(values):
            mine = weights[i * across : (i + 1) * across]
            mine = jnp.concatenate([w.astype(jnp.bfloat16) for w in mine], axis=0)
            part = jnp.dot(part, mine, preferred_element_type=jnp.float32)
            update = part if update is None else update + part
        if not first:
            rescale = jnp.exp2(top[e] - new_top)
            block_sum = total_sum[e] * rescale + block_sum
            update = totals[e] * rescale + update
        top[e] = new_top
        total_sum[e] = block_sum
        totals[e] = update


def switch_of(flags_ref, e, owner, columns, allowed=None):
    flag = flags_ref[e, pl.ds(jnp.maximum(owner, 0), 1), :]
    if allowed is not None:
        flag = flag * jnp.where(allowed, 1.0, 0.0)
    return jnp.concatenate([flag] * (columns // HD), axis=1) > 0.5


def member_kernel(across, turns, meta_ref, after_ref, member_ref, inverse_ref, rows_ref):
    del after_ref
    z, y = place(across)
    columns = rows_ref.shape[1]
    repeat = member_ref.shape[1] // turns
    q_rows = columns // repeat
    owners = [block_at(z, y, e, across) for e in range(across)]
    column = lax.broadcasted_iota(jnp.int32, (1, columns), 1)
    for e in range(across):
        position = lax.rem(column, q_rows) + owners[e] * q_rows
        start = jnp.int32(0)
        for t in range(turns):
            length = meta_ref[t]
            inside = (position >= start) & (position < start + length)
            rows_ref[t : t + 1, :] = jnp.where(inside, 1.0, 0.0)
            if e == 0:
                count = jnp.full((1, HD), length, jnp.int32).astype(jnp.float32)
                inverse_ref[t : t + 1, :] = 1.0 / count
            start = start + length
        for r in range(repeat):
            mine = (column >= r * q_rows) & (column < (r + 1) * q_rows)
            member_ref[e, r * turns : (r + 1) * turns, :] = jnp.where(
                mine, rows_ref[...], 0.0
            ).astype(jnp.bfloat16)


def members(across, turns, meta, group):
    q_rows, width = group.shape
    repeat = width // HD
    columns = repeat * q_rows
    return call(
        functools.partial(member_kernel, across, turns),
        [
            jax.ShapeDtypeStruct((across, repeat * turns, columns), jnp.bfloat16),
            jax.ShapeDtypeStruct((turns, HD), jnp.float32),
        ],
        in_specs=[in_smem, anywhere],
        scratch_shapes=[pltpu.VMEM((turns, columns), jnp.float32)],
    )(meta, group)


def weight_piece(weight_ref, out_ref, start, sem):
    return pltpu.make_async_copy(weight_ref.at[start : start + out_ref.shape[0]], out_ref, sem)


def first_kernel(across, own_flags_ref, *refs):
    queries, refs = refs[:across], refs[across:]
    kv_ref, weight_ref, turned_ref, flags_ref, weight_out = refs[:5]
    state, copied = refs[5:8], refs[8]
    weight_copy = weight_piece(weight_ref, weight_out, 0, copied)
    weight_copy.start()
    z, y = place(across)
    q_rows = kv_ref.shape[1]
    repeat = queries[0].shape[1] // HD
    columns = repeat * q_rows
    for e in range(across):
        for r in range(repeat):
            turned_ref[e, :, r * q_rows : (r + 1) * q_rows] = queries[e][
                0:q_rows, r * HD : (r + 1) * HD
            ].T
    flags_ref[0] = own_flags_ref[...]
    for e in range(1, across):
        flags_ref[e] = queries[e][q_rows:, 0:HD].astype(jnp.float32)
    owners = [block_at(z, y, e, across) for e in range(across)]
    switches = [
        [
            None if e == b else switch_of(flags_ref, e, owners[b], columns, owners[b] < owners[e])
            for b in range(across)
        ]
        for e in range(across)
    ]
    rows_update(turned_ref, [kv_ref], switches, state, True)

    weight_copy.wait()


def attend_first(across, flags, queries, rows, weight, piece):
    q_rows = rows.shape[1]
    repeat = queries[0].shape[1] // HD
    columns = repeat * q_rows
    f32, b16 = jnp.float32, jnp.bfloat16
    return call(
        functools.partial(first_kernel, across),
        [
            jax.ShapeDtypeStruct((across, HD, columns), b16),
            jax.ShapeDtypeStruct((across,) + flags.shape, f32),
            jax.ShapeDtypeStruct((piece, weight.shape[1]), weight.dtype),
            jax.ShapeDtypeStruct((across, 1, columns), f32),
            jax.ShapeDtypeStruct((across, 1, columns), f32),
            jax.ShapeDtypeStruct((across, HD, columns), f32),
        ],
        in_specs=[in_vmem] * (across + 2) + [anywhere],
        scratch_shapes=[pltpu.SemaphoreType.DMA(())],
        limit=big_limit,
    )(flags, *queries, rows, weight)


def next_kernel(across, distances, turns, last, weight_at, flags_ref, turned_ref, *refs):
    below_count = len(distances)
    below, state, refs = refs[:below_count], refs[below_count : below_count + 3], refs[below_count + 3 :]
    if weight_at is not None:
        weight_ref, weight_out, copied = refs[0], refs[-2], refs[-1]
        refs = refs[1:-2]
        weight_copy = weight_piece(weight_ref, weight_out, weight_at, copied)
        weight_copy.start()
    z, y = place(across)
    columns = turned_ref.shape[2]

    def update(rows, from_distances):
        switches = [
            [
                switch_of(flags_ref, e, block_at(z - distance, y, b, across), columns)
                for distance in from_distances
                for b in range(across)
            ]
            for e in range(across)
        ]
        rows_update(turned_ref, rows, switches, state, False)

    for number, distance in enumerate(distances, 1):
        here = (z >= distance) if number == len(distances) else (z == distance)
        pl.when(here)(functools.partial(update, below[:number], distances[:number]))

    if weight_at is not None:
        weight_copy.wait()
    if last:
        member_ref, inverse_ref, out_ref = refs
        rows = out_ref.shape[1]
        pooled = None
        for e in range(across):
            attended = (state[2][e] / state[1][e]).astype(jnp.bfloat16)
            part = lax.dot_general(
                member_ref[e],
                attended,
                (((1,), (1,)), ((), ())),
                preferred_element_type=jnp.float32,
            )
            pooled = part if pooled is None else pooled + part
        for r in range(pooled.shape[0] // turns):
            mean = pooled[r * turns : (r + 1) * turns] * inverse_ref[...]
            for s in range(out_ref.shape[0]):
                out_ref[s, :, r * HD : (r + 1) * HD] = mean[s * rows : (s + 1) * rows]


def attend_next(across, distances, turns, turned, flags, below, state, pool, out_piece, weight, at, piece):
    last = pool is not None
    args = [flags, turned, *below, *state]
    in_specs = [in_vmem] * len(args)
    aliases, scratch = {}, []
    if at is not None:
        args.append(weight)
        in_specs.append(anywhere)
        scratch = [pltpu.SemaphoreType.DMA(())]
    if last:
        args += list(pool)
        in_specs += [in_vmem] * len(pool)
        out_shape = [jax.ShapeDtypeStruct(out_piece, jnp.float32)]
    else:
        out_shape = [jax.ShapeDtypeStruct(part.shape, part.dtype) for part in state]
        aliases = {2 + len(below) + i: i for i in range(len(state))}
    if at is not None:
        out_shape.append(jax.ShapeDtypeStruct((piece, weight.shape[1]), weight.dtype))
    return call(
        functools.partial(next_kernel, across, distances, turns, last, at),
        out_shape,
        in_specs=in_specs,
        scratch_shapes=scratch,
        input_output_aliases=aliases,
        limit=big_limit if at is not None else 16 * 1024 * 1024,
    )(*args)


def project_kernel(across, other, parts_ref, *refs):
    weights, out_ref = refs[:-1], refs[-1]
    side = lax.axis_index("head")
    if other:
        side = 1 - side
    groups = []
    for y in range(across):
        total = parts_ref[y]
        for s in range(y + across, parts_ref.shape[0], across):
            total = total + parts_ref[s]
        groups.append(total)
    total = jnp.concatenate(groups, axis=1)
    rows = total.shape[0]
    high = total.astype(jnp.bfloat16)
    low = (total - high.astype(jnp.float32)).astype(jnp.bfloat16)
    both = jnp.concatenate([high, low], axis=0)
    half = out_ref.shape[1]
    step = math.gcd(half, 512)
    for c in range(half // step):
        start = pl.multiple_of(side * half + c * step, step)
        product, at = None, 0
        for weight_ref in weights:
            depth = weight_ref.shape[0]
            part = jnp.dot(
                both[:, at : at + depth],
                weight_ref[:, pl.ds(start, step)],
                preferred_element_type=jnp.float32,
            )
            product = part if product is None else product + part
            at += depth
        out_ref[:, c * step : (c + 1) * step] = product[:rows] + product[rows:]


def project(across, other, parts, weights):
    return call(
        functools.partial(project_kernel, across, other),
        jax.ShapeDtypeStruct((parts.shape[1], weights[0].shape[1] // 2), jnp.float32),
        in_specs=[in_vmem] * (1 + len(weights)),
    )(parts, *weights)


def on_device(count, queries, key_states, value_states, out_weight, turn_lengths, block_flags):
    across = key_states.shape[1] // HD
    down = count // across
    turns = turn_lengths.shape[0]

    def over(rows, shift):
        pairs = [(i, i - i % across + (i + shift) % across) for i in range(count)]
        return lax.ppermute(rows, "seq", pairs)

    def up(rows, distance, lowest=0):
        step = distance * across
        pairs = [(i, i + step) for i in range(lowest * across, count - step)]
        return lax.ppermute(rows, "seq", pairs)

    _, y = place(across)
    heads = []
    for shift in range(across):
        at = lax.rem(y + shift, across)
        heads.append(pair(pick(key_states, at, across), pick(value_states, at, across)))
    swapped = [over(heads[shift], shift) for shift in range(1, across)]
    rows = join([heads[0]] + swapped)
    first = up(heads[0], 1)
    rest = up(join(swapped), 1)
    rows, queries = lax.optimization_barrier((rows, queries))
    meta = lax.optimization_barrier(jnp.concatenate([turn_lengths, block_flags[0]]))
    padded = -(-count // 16) * 16
    flags = jnp.pad(meta[turns:], (0, padded - count))[:, None]
    groups = [pick(queries, lax.rem(y + shift, across), across) for shift in range(across)]
    sent = []
    for group in groups[1:]:
        under = jnp.broadcast_to(flags, (padded, group.shape[1])).astype(group.dtype)
        sent.append(jnp.concatenate([group, under], axis=0))
    flags = jnp.broadcast_to(flags, (padded, HD)).astype(jnp.float32)
    below = [rows, join([first, rest], long_flops)] + [None] * (down - 2)
    member, inverse = members(across, turns, meta, groups[0])
    far, inverse = lax.optimization_barrier((rows, inverse))
    inverse, *sent = lax.optimization_barrier((inverse, *sent))
    others = [over(group, shift) for shift, group in enumerate(sent, 1)]
    for distance in range(3, down):
        below[distance] = up(far, distance)
    if down > 2:
        below[2] = up(below[1], 1, 1)
    depth = out_weight.shape[0]
    pieces = [4 * depth // 8, 2 * depth // 8, depth // 8, depth // 8]
    turned, flags, weight, *state = attend_first(
        across, flags, [groups[0], *others], rows, out_weight, pieces[0]
    )
    weights = [weight]
    out_piece = (count, turns // count, queries.shape[1] // across)
    stages = [[1]] + [list(range(d, min(d + 2, down))) for d in range(3, down, 2)] + [[2]]
    for number, distances in enumerate(stages):
        last = number == len(stages) - 1
        with_weight = number < 2 or last
        state = attend_next(
            across,
            distances,
            turns,
            turned,
            flags,
            [below[distance] for distance in distances],
            state,
            (member, inverse) if last else None,
            out_piece,
            out_weight,
            sum(pieces[: len(weights)]) if with_weight else None,
            pieces[len(weights)] if with_weight else None,
        )
        if with_weight:
            *state, weight = state
            weights.append(weight)
    parts = lax.all_to_all(state[0], "seq", split_axis=0, concat_axis=0, tiled=True)
    theirs = project(across, True, parts, weights)
    theirs = lax.ppermute(theirs, "head", [(0, 1), (1, 0)])
    return project(across, False, parts, weights) + theirs


def solution(mesh):
    in_specs = (
        P(("conv", "seq"), "head"),
        P(("conv", "seq"), "head"),
        P(("conv", "seq"), "head"),
        P("head", None),
        P("conv"),
        P(("conv", "seq"), None),
    )
    out_specs = P(("conv", "seq"), "head")
    return jax.shard_map(
        functools.partial(on_device, mesh.shape["seq"]),
        mesh=mesh,
        in_specs=in_specs,
        out_specs=out_specs,
        check_vma=False,
    )
```

```python
import functools
import math

import jax
import jax.numpy as jnp
from jax import lax
from jax.experimental import pallas as pl
from jax.experimental.pallas import tpu as pltpu
from jax.sharding import PartitionSpec as P

HD = 128

big_negative = -1e30
log_two_e = 1.4426950408889634

big_limit = 45 * 1024 * 1024
long_flops = 4 * 10**9

in_vmem = pl.BlockSpec(memory_space=pltpu.VMEM)
in_smem = pl.BlockSpec(memory_space=pltpu.SMEM)
anywhere = pl.BlockSpec(memory_space=pl.ANY)


def place(across):
    index = lax.axis_index("seq")
    return index // across, lax.rem(index, across)


def block_at(z, y, e, across):
    return z * across + lax.rem(y - e + across, across)


def call(kernel, out_shape, **settings):
    limit = settings.pop("limit", 16 * 1024 * 1024)
    flops = settings.pop("flops", 0)
    return pl.pallas_call(
        kernel,
        out_shape=out_shape,
        out_specs=jax.tree.map(lambda _: in_vmem, out_shape),
        compiler_params=pltpu.CompilerParams(vmem_limit_bytes=limit),
        cost_estimate=pl.CostEstimate(flops=flops, bytes_accessed=1024, transcendentals=0),
        **settings,
    )


def pick(rows, number, parts):
    width = rows.shape[1] // parts
    picked = rows[:, :width]
    for part in range(1, parts):
        picked = jnp.where(number == part, rows[:, part * width : (part + 1) * width], picked)
    return picked


def pair(keys, values):
    which = lax.broadcasted_iota(jnp.int32, (2,) + keys.shape, 0)
    return jnp.where(which == 0, keys[None], values[None])


def join_kernel(*refs):
    *parts, out_ref = refs
    at = 0
    for part in parts:
        out_ref[at : at + part.shape[0]] = part[...]
        at += part.shape[0]


def join(parts):
    count = sum(part.shape[0] for part in parts)
    shape = jax.ShapeDtypeStruct((count,) + parts[0].shape[1:], parts[0].dtype)
    return call(join_kernel, shape, in_specs=[in_vmem] * len(parts))(*parts)


def rows_update(turned_ref, rows_refs, switches, state, first):
    top, total_sum, totals = state
    across, _, columns = turned_ref.shape
    rows = rows_refs[0].shape[1]
    count = across * len(rows_refs)
    factor = log_two_e / math.sqrt(HD)
    keys = [
        jnp.concatenate([kv_ref[2 * e] for e in range(across)], axis=0) for kv_ref in rows_refs
    ]
    values = [
        jnp.concatenate([kv_ref[2 * e + 1] for e in range(across)], axis=0).T for kv_ref in rows_refs
    ]
    logits = [
        [jnp.dot(part, turned_ref[e], preferred_element_type=jnp.float32) for part in keys]
        for e in range(across)
    ]
    if first:
        key_pos = lax.broadcasted_iota(jnp.int32, (rows, 1), 0)
        column = lax.broadcasted_iota(jnp.int32, (1, columns), 1)
        causal = key_pos <= lax.rem(column, rows)
    for e in range(across):
        blocks = [
            logits[e][b // across][b % across * rows : (b % across + 1) * rows] for b in range(count)
        ]
        if first:
            blocks[e] = jnp.where(causal, blocks[e], big_negative)
        new_top = None if first else top[e]
        for b in range(count):
            block_top = jnp.ceil(jnp.max(blocks[b], axis=0, keepdims=True) * factor)
            if switches[e][b] is not None:
                block_top = jnp.where(switches[e][b], block_top, big_negative)
            new_top = block_top if new_top is None else jnp.maximum(new_top, block_top)
        weights, block_sum = [], None
        for b in range(count):
            against = new_top
            if switches[e][b] is not None:
                against = jnp.where(switches[e][b], new_top, -big_negative)
            weights.append(jnp.exp2(blocks[b] * factor - against))
            part = jnp.sum(weights[b], axis=0, keepdims=True)
            block_sum = part if block_sum is None else block_sum + part
        update = None
        for i, part in enumerate(values):
            mine = weights[i * across : (i + 1) * across]
            mine = jnp.concatenate([w.astype(jnp.bfloat16) for w in mine], axis=0)
            part = jnp.dot(part, mine, preferred_element_type=jnp.float32)
            update = part if update is None else update + part
        if not first:
            rescale = jnp.exp2(top[e] - new_top)
            block_sum = total_sum[e] * rescale + block_sum
            update = totals[e] * rescale + update
        top[e] = new_top
        total_sum[e] = block_sum
        totals[e] = update


def switch_of(flags_ref, e, owner, columns, allowed=None):
    flag = flags_ref[e, pl.ds(jnp.maximum(owner, 0), 1), :]
    if allowed is not None:
        flag = flag * jnp.where(allowed, 1.0, 0.0)
    return jnp.concatenate([flag] * (columns // HD), axis=1) > 0.5


def member_kernel(across, turns, meta_ref, after_ref, member_ref, inverse_ref, rows_ref):
    del after_ref
    z, y = place(across)
    columns = rows_ref.shape[1]
    repeat = member_ref.shape[1] // turns
    q_rows = columns // repeat
    owners = [block_at(z, y, e, across) for e in range(across)]
    column = lax.broadcasted_iota(jnp.int32, (1, columns), 1)
    for e in range(across):
        position = lax.rem(column, q_rows) + owners[e] * q_rows
        start = jnp.int32(0)
        for t in range(turns):
            length = meta_ref[t]
            inside = (position >= start) & (position < start + length)
            rows_ref[t : t + 1, :] = jnp.where(inside, 1.0, 0.0)
            if e == 0:
                count = jnp.full((1, HD), length, jnp.int32).astype(jnp.float32)
                inverse_ref[t : t + 1, :] = 1.0 / count
            start = start + length
        for r in range(repeat):
            mine = (column >= r * q_rows) & (column < (r + 1) * q_rows)
            member_ref[e, r * turns : (r + 1) * turns, :] = jnp.where(
                mine, rows_ref[...], 0.0
            ).astype(jnp.bfloat16)


def members(across, turns, meta, group):
    q_rows, width = group.shape
    repeat = width // HD
    columns = repeat * q_rows
    return call(
        functools.partial(member_kernel, across, turns),
        [
            jax.ShapeDtypeStruct((across, repeat * turns, columns), jnp.bfloat16),
            jax.ShapeDtypeStruct((turns, HD), jnp.float32),
        ],
        in_specs=[in_smem, anywhere],
        scratch_shapes=[pltpu.VMEM((turns, columns), jnp.float32)],
        flops=long_flops,
    )(meta, group)


def weight_piece(weight_ref, out_ref, start, sem):
    return pltpu.make_async_copy(weight_ref.at[start : start + out_ref.shape[0]], out_ref, sem)


def first_kernel(across, own_flags_ref, *refs):
    queries, refs = refs[:across], refs[across:]
    kv_ref, weight_ref, turned_ref, flags_ref, weight_out = refs[:5]
    state, copied = refs[5:8], refs[8]
    weight_copy = weight_piece(weight_ref, weight_out, 0, copied)
    weight_copy.start()
    z, y = place(across)
    q_rows = kv_ref.shape[1]
    repeat = queries[0].shape[1] // HD
    columns = repeat * q_rows
    for e in range(across):
        for r in range(repeat):
            turned_ref[e, :, r * q_rows : (r + 1) * q_rows] = queries[e][
                0:q_rows, r * HD : (r + 1) * HD
            ].T
    flags_ref[0] = own_flags_ref[...]
    for e in range(1, across):
        flags_ref[e] = queries[e][q_rows:, 0:HD].astype(jnp.float32)
    owners = [block_at(z, y, e, across) for e in range(across)]
    switches = [
        [
            None if e == b else switch_of(flags_ref, e, owners[b], columns, owners[b] < owners[e])
            for b in range(across)
        ]
        for e in range(across)
    ]
    rows_update(turned_ref, [kv_ref], switches, state, True)

    weight_copy.wait()


def attend_first(across, flags, queries, rows, weight, piece):
    q_rows = rows.shape[1]
    repeat = queries[0].shape[1] // HD
    columns = repeat * q_rows
    f32, b16 = jnp.float32, jnp.bfloat16
    return call(
        functools.partial(first_kernel, across),
        [
            jax.ShapeDtypeStruct((across, HD, columns), b16),
            jax.ShapeDtypeStruct((across,) + flags.shape, f32),
            jax.ShapeDtypeStruct((piece, weight.shape[1]), weight.dtype),
            jax.ShapeDtypeStruct((across, 1, columns), f32),
            jax.ShapeDtypeStruct((across, 1, columns), f32),
            jax.ShapeDtypeStruct((across, HD, columns), f32),
        ],
        in_specs=[in_vmem] * (across + 2) + [anywhere],
        scratch_shapes=[pltpu.SemaphoreType.DMA(())],
        limit=big_limit,
    )(flags, *queries, rows, weight)


def next_kernel(across, distances, turns, last, weight_at, flags_ref, turned_ref, *refs):
    below_count = len(distances)
    below, state, refs = refs[:below_count], refs[below_count : below_count + 3], refs[below_count + 3 :]
    if weight_at is not None:
        weight_ref, weight_out, copied = refs[0], refs[-2], refs[-1]
        refs = refs[1:-2]
        weight_copy = weight_piece(weight_ref, weight_out, weight_at, copied)
        weight_copy.start()
    z, y = place(across)
    columns = turned_ref.shape[2]

    def update(rows, from_distances):
        switches = [
            [
                switch_of(flags_ref, e, block_at(z - distance, y, b, across), columns)
                for distance in from_distances
                for b in range(across)
            ]
            for e in range(across)
        ]
        rows_update(turned_ref, rows, switches, state, False)

    for number, distance in enumerate(distances, 1):
        here = (z >= distance) if number == len(distances) else (z == distance)
        pl.when(here)(functools.partial(update, below[:number], distances[:number]))

    if weight_at is not None:
        weight_copy.wait()
    if last:
        member_ref, inverse_ref, out_ref = refs
        rows = out_ref.shape[1]
        pooled = None
        for e in range(across):
            attended = (state[2][e] / state[1][e]).astype(jnp.bfloat16)
            part = lax.dot_general(
                member_ref[e],
                attended,
                (((1,), (1,)), ((), ())),
                preferred_element_type=jnp.float32,
            )
            pooled = part if pooled is None else pooled + part
        for r in range(pooled.shape[0] // turns):
            mean = pooled[r * turns : (r + 1) * turns] * inverse_ref[...]
            for s in range(out_ref.shape[0]):
                out_ref[s, :, r * HD : (r + 1) * HD] = mean[s * rows : (s + 1) * rows]


def attend_next(across, distances, turns, turned, flags, below, state, pool, out_piece, weight, at, piece):
    last = pool is not None
    args = [flags, turned, *below, *state]
    in_specs = [in_vmem] * len(args)
    aliases, scratch = {}, []
    if at is not None:
        args.append(weight)
        in_specs.append(anywhere)
        scratch = [pltpu.SemaphoreType.DMA(())]
    if last:
        args += list(pool)
        in_specs += [in_vmem] * len(pool)
        out_shape = [jax.ShapeDtypeStruct(out_piece, jnp.float32)]
    else:
        out_shape = [jax.ShapeDtypeStruct(part.shape, part.dtype) for part in state]
        aliases = {2 + len(below) + i: i for i in range(len(state))}
    if at is not None:
        out_shape.append(jax.ShapeDtypeStruct((piece, weight.shape[1]), weight.dtype))
    return call(
        functools.partial(next_kernel, across, distances, turns, last, at),
        out_shape,
        in_specs=in_specs,
        scratch_shapes=scratch,
        input_output_aliases=aliases,
        limit=big_limit if at is not None else 16 * 1024 * 1024,
    )(*args)


def project_kernel(across, other, parts_ref, *refs):
    weights, out_ref = refs[:-1], refs[-1]
    side = lax.axis_index("head")
    if other:
        side = 1 - side
    groups = []
    for y in range(across):
        total = parts_ref[y]
        for s in range(y + across, parts_ref.shape[0], across):
            total = total + parts_ref[s]
        groups.append(total)
    total = jnp.concatenate(groups, axis=1)
    rows = total.shape[0]
    high = total.astype(jnp.bfloat16)
    low = (total - high.astype(jnp.float32)).astype(jnp.bfloat16)
    both = jnp.concatenate([high, low], axis=0)
    half = out_ref.shape[1]
    step = math.gcd(half, 512)
    for c in range(half // step):
        start = pl.multiple_of(side * half + c * step, step)
        product, at = None, 0
        for weight_ref in weights:
            depth = weight_ref.shape[0]
            part = jnp.dot(
                both[:, at : at + depth],
                weight_ref[:, pl.ds(start, step)],
                preferred_element_type=jnp.float32,
            )
            product = part if product is None else product + part
            at += depth
        out_ref[:, c * step : (c + 1) * step] = product[:rows] + product[rows:]


def project(across, other, parts, weights):
    return call(
        functools.partial(project_kernel, across, other),
        jax.ShapeDtypeStruct((parts.shape[1], weights[0].shape[1] // 2), jnp.float32),
        in_specs=[in_vmem] * (1 + len(weights)),
    )(parts, *weights)


def on_device(count, queries, key_states, value_states, out_weight, turn_lengths, block_flags):
    across = key_states.shape[1] // HD
    down = count // across
    turns = turn_lengths.shape[0]

    def over(rows, shift):
        pairs = [(i, i - i % across + (i + shift) % across) for i in range(count)]
        return lax.ppermute(rows, "seq", pairs)

    def up(rows, distance, lowest=0):
        step = distance * across
        pairs = [(i, i + step) for i in range(lowest * across, count - step)]
        return lax.ppermute(rows, "seq", pairs)

    _, y = place(across)
    heads = []
    for shift in range(across):
        at = lax.rem(y + shift, across)
        heads.append(pair(pick(key_states, at, across), pick(value_states, at, across)))
    swapped = [over(heads[shift], shift) for shift in range(1, across)]
    rows = join([heads[0]] + swapped)
    first = up(heads[0], 1)
    rest = up(join(swapped), 1)
    rows, queries = lax.optimization_barrier((rows, queries))
    meta = lax.optimization_barrier(jnp.concatenate([turn_lengths, block_flags[0]]))
    padded = -(-count // 16) * 16
    flags = jnp.pad(meta[turns:], (0, padded - count))[:, None]
    groups = [pick(queries, lax.rem(y + shift, across), across) for shift in range(across)]
    sent = []
    for group in groups[1:]:
        under = jnp.broadcast_to(flags, (padded, group.shape[1])).astype(group.dtype)
        sent.append(jnp.concatenate([group, under], axis=0))
    flags = jnp.broadcast_to(flags, (padded, HD)).astype(jnp.float32)
    below = [rows, join([first, rest])] + [None] * (down - 2)
    far, groups[0] = lax.optimization_barrier((rows, groups[0]))
    others = [over(group, shift) for shift, group in enumerate(sent, 1)]
    for distance in range(3, down):
        below[distance] = up(far, distance)
    if down > 2:
        below[2] = up(below[1], 1, 1)
    member, inverse = members(across, turns, meta, groups[0])
    inverse, flags = lax.optimization_barrier((inverse, flags))
    depth = out_weight.shape[0]
    pieces = [4 * depth // 8, 2 * depth // 8, 2 * depth // 8]
    turned, flags, weight, *state = attend_first(
        across, flags, [groups[0], *others], rows, out_weight, pieces[0]
    )
    weights = [weight]
    out_piece = (count, turns // count, queries.shape[1] // across)
    stages = [[1]] + [list(range(d, min(d + 2, down))) for d in range(3, down, 2)] + [[2]]
    for number, distances in enumerate(stages):
        last = number == len(stages) - 1
        with_weight = number < 2
        state = attend_next(
            across,
            distances,
            turns,
            turned,
            flags,
            [below[distance] for distance in distances],
            state,
            (member, inverse) if last else None,
            out_piece,
            out_weight,
            sum(pieces[: len(weights)]) if with_weight else None,
            pieces[len(weights)] if with_weight else None,
        )
        if with_weight:
            *state, weight = state
            weights.append(weight)
    parts = lax.all_to_all(state[0], "seq", split_axis=0, concat_axis=0, tiled=True)
    theirs = project(across, True, parts, weights)
    theirs = lax.ppermute(theirs, "head", [(0, 1), (1, 0)])
    return project(across, False, parts, weights) + theirs


def solution(mesh):
    in_specs = (
        P(("conv", "seq"), "head"),
        P(("conv", "seq"), "head"),
        P(("conv", "seq"), "head"),
        P("head", None),
        P("conv"),
        P(("conv", "seq"), None),
    )
    out_specs = P(("conv", "seq"), "head")
    return jax.shard_map(
        functools.partial(on_device, mesh.shape["seq"]),
        mesh=mesh,
        in_specs=in_specs,
        out_specs=out_specs,
        check_vma=False,
    )
```

```python
import functools
import math

import jax
import jax.numpy as jnp
from jax import lax
from jax.experimental import pallas as pl
from jax.experimental.pallas import tpu as pltpu
from jax.sharding import PartitionSpec as P

HD = 128

big_negative = -1e30
log_two_e = 1.4426950408889634

big_limit = 45 * 1024 * 1024
small_cost = pl.CostEstimate(flops=1024, bytes_accessed=1024, transcendentals=0)

in_vmem = pl.BlockSpec(memory_space=pltpu.VMEM)
in_smem = pl.BlockSpec(memory_space=pltpu.SMEM)
anywhere = pl.BlockSpec(memory_space=pl.ANY)


def place(across):
    index = lax.axis_index("seq")
    return index // across, lax.rem(index, across)


def block_at(z, y, e, across):
    return z * across + lax.rem(y - e + across, across)


def call(kernel, out_shape, **settings):
    limit = settings.pop("limit", 16 * 1024 * 1024)
    return pl.pallas_call(
        kernel,
        out_shape=out_shape,
        out_specs=jax.tree.map(lambda _: in_vmem, out_shape),
        compiler_params=pltpu.CompilerParams(vmem_limit_bytes=limit),
        cost_estimate=small_cost,
        **settings,
    )


def pick(rows, number, parts):
    width = rows.shape[1] // parts
    picked = rows[:, :width]
    for part in range(1, parts):
        picked = jnp.where(number == part, rows[:, part * width : (part + 1) * width], picked)
    return picked


def pair(keys, values):
    which = lax.broadcasted_iota(jnp.int32, (2,) + keys.shape, 0)
    return jnp.where(which == 0, keys[None], values[None])


def join_kernel(*refs):
    *parts, out_ref = refs
    at = 0
    for part in parts:
        size = min(part.shape[0], out_ref.shape[0] - at)
        out_ref[at : at + size] = part[:size]
        at += size


def join_parts(parts, count):
    return join(parts, count)


def join(parts, count=None):
    count = sum(part.shape[0] for part in parts) if count is None else count
    shape = jax.ShapeDtypeStruct((count,) + parts[0].shape[1:], parts[0].dtype)
    return call(join_kernel, shape, in_specs=[in_vmem] * len(parts))(*parts)


def rows_update(turned_ref, rows_refs, switches, state, first):
    top, total_sum, totals = state
    across, _, columns = turned_ref.shape
    rows = rows_refs[0].shape[1]
    count = across * len(rows_refs)
    factor = log_two_e / math.sqrt(HD)
    keys = [
        jnp.concatenate([kv_ref[2 * e] for e in range(across)], axis=0) for kv_ref in rows_refs
    ]
    values = [
        jnp.concatenate([kv_ref[2 * e + 1] for e in range(across)], axis=0).T for kv_ref in rows_refs
    ]
    logits = [
        [jnp.dot(part, turned_ref[e], preferred_element_type=jnp.float32) for part in keys]
        for e in range(across)
    ]
    if first:
        key_pos = lax.broadcasted_iota(jnp.int32, (rows, 1), 0)
        column = lax.broadcasted_iota(jnp.int32, (1, columns), 1)
        causal = key_pos <= lax.rem(column, rows)
    for e in range(across):
        blocks = [
            logits[e][b // across][b % across * rows : (b % across + 1) * rows] for b in range(count)
        ]
        if first:
            blocks[e] = jnp.where(causal, blocks[e], big_negative)
        new_top = None if first else top[e]
        for b in range(count):
            block_top = jnp.ceil(jnp.max(blocks[b], axis=0, keepdims=True) * factor)
            if switches[e][b] is not None:
                block_top = jnp.where(switches[e][b], block_top, big_negative)
            new_top = block_top if new_top is None else jnp.maximum(new_top, block_top)
        weights, block_sum = [], None
        for b in range(count):
            against = new_top
            if switches[e][b] is not None:
                against = jnp.where(switches[e][b], new_top, -big_negative)
            weights.append(jnp.exp2(blocks[b] * factor - against))
            part = jnp.sum(weights[b], axis=0, keepdims=True)
            block_sum = part if block_sum is None else block_sum + part
        update = None
        for i, part in enumerate(values):
            mine = weights[i * across : (i + 1) * across]
            mine = jnp.concatenate([w.astype(jnp.bfloat16) for w in mine], axis=0)
            part = jnp.dot(part, mine, preferred_element_type=jnp.float32)
            update = part if update is None else update + part
        if not first:
            rescale = jnp.exp2(top[e] - new_top)
            block_sum = total_sum[e] * rescale + block_sum
            update = totals[e] * rescale + update
        top[e] = new_top
        total_sum[e] = block_sum
        totals[e] = update


def switch_of(flags_ref, e, owner, columns, allowed=None):
    flag = flags_ref[e, pl.ds(jnp.maximum(owner, 0), 1), :]
    if allowed is not None:
        flag = flag * jnp.where(allowed, 1.0, 0.0)
    return jnp.concatenate([flag] * (columns // HD), axis=1) > 0.5


def member_kernel(across, turns, meta_ref, after_ref, member_ref, inverse_ref, rows_ref):
    del after_ref
    z, y = place(across)
    columns = rows_ref.shape[1]
    repeat = member_ref.shape[1] // turns
    q_rows = columns // repeat
    owners = [block_at(z, y, e, across) for e in range(across)]
    column = lax.broadcasted_iota(jnp.int32, (1, columns), 1)
    for e in range(across):
        position = lax.rem(column, q_rows) + owners[e] * q_rows
        start = jnp.int32(0)
        for t in range(turns):
            length = meta_ref[t]
            inside = (position >= start) & (position < start + length)
            rows_ref[t : t + 1, :] = jnp.where(inside, 1.0, 0.0)
            if e == 0:
                count = jnp.full((1, HD), length, jnp.int32).astype(jnp.float32)
                inverse_ref[t : t + 1, :] = 1.0 / count
            start = start + length
        for r in range(repeat):
            mine = (column >= r * q_rows) & (column < (r + 1) * q_rows)
            member_ref[e, r * turns : (r + 1) * turns, :] = jnp.where(
                mine, rows_ref[...], 0.0
            ).astype(jnp.bfloat16)


def members(across, turns, meta, group):
    q_rows, width = group.shape
    repeat = width // HD
    columns = repeat * q_rows
    return call(
        functools.partial(member_kernel, across, turns),
        [
            jax.ShapeDtypeStruct((across, repeat * turns, columns), jnp.bfloat16),
            jax.ShapeDtypeStruct((turns, HD), jnp.float32),
        ],
        in_specs=[in_smem, anywhere],
        scratch_shapes=[pltpu.VMEM((turns, columns), jnp.float32)],
    )(meta, group)


def weight_piece(weight_ref, out_ref, start, sem):
    return pltpu.make_async_copy(weight_ref.at[start : start + out_ref.shape[0]], out_ref, sem)


def first_kernel(across, own_flags_ref, *refs):
    queries, refs = refs[:across], refs[across:]
    kv_ref, weight_ref, turned_ref, flags_ref, weight_out = refs[:5]
    state, copied = refs[5:8], refs[8]
    weight_copy = weight_piece(weight_ref, weight_out, 0, copied)
    weight_copy.start()
    z, y = place(across)
    q_rows = kv_ref.shape[1]
    repeat = queries[0].shape[1] // HD
    columns = repeat * q_rows
    for e in range(across):
        for r in range(repeat):
            turned_ref[e, :, r * q_rows : (r + 1) * q_rows] = queries[e][
                0:q_rows, r * HD : (r + 1) * HD
            ].T
    flags_ref[0] = own_flags_ref[...]
    for e in range(1, across):
        flags_ref[e] = queries[e][q_rows:, 0:HD].astype(jnp.float32)
    owners = [block_at(z, y, e, across) for e in range(across)]
    switches = [
        [
            None if e == b else switch_of(flags_ref, e, owners[b], columns, owners[b] < owners[e])
            for b in range(across)
        ]
        for e in range(across)
    ]
    rows_update(turned_ref, [kv_ref], switches, state, True)

    weight_copy.wait()


def attend_first(across, flags, queries, rows, weight, piece):
    q_rows = rows.shape[1]
    repeat = queries[0].shape[1] // HD
    columns = repeat * q_rows
    f32, b16 = jnp.float32, jnp.bfloat16
    return call(
        functools.partial(first_kernel, across),
        [
            jax.ShapeDtypeStruct((across, HD, columns), b16),
            jax.ShapeDtypeStruct((across,) + flags.shape, f32),
            jax.ShapeDtypeStruct((piece, weight.shape[1]), weight.dtype),
            jax.ShapeDtypeStruct((across, 1, columns), f32),
            jax.ShapeDtypeStruct((across, 1, columns), f32),
            jax.ShapeDtypeStruct((across, HD, columns), f32),
        ],
        in_specs=[in_vmem] * (across + 2) + [anywhere],
        scratch_shapes=[pltpu.SemaphoreType.DMA(())],
        limit=big_limit,
    )(flags, *queries, rows, weight)


def next_kernel(across, distances, turns, last, weight_at, flags_ref, turned_ref, *refs):
    below_count = len(distances)
    below, state, refs = refs[:below_count], refs[below_count : below_count + 3], refs[below_count + 3 :]
    if weight_at is not None:
        weight_ref, weight_out, copied = refs[0], refs[-2], refs[-1]
        refs = refs[1:-2]
        weight_copy = weight_piece(weight_ref, weight_out, weight_at, copied)
        weight_copy.start()
    z, y = place(across)
    columns = turned_ref.shape[2]

    def update(rows, from_distances):
        switches = [
            [
                switch_of(flags_ref, e, block_at(z - distance, y, b, across), columns)
                for distance in from_distances
                for b in range(across)
            ]
            for e in range(across)
        ]
        rows_update(turned_ref, rows, switches, state, False)

    for number, distance in enumerate(distances, 1):
        here = (z >= distance) if number == len(distances) else (z == distance)
        pl.when(here)(functools.partial(update, below[:number], distances[:number]))

    if weight_at is not None:
        weight_copy.wait()
    if last:
        member_ref, inverse_ref, out_ref = refs
        rows = out_ref.shape[1] * turns // member_ref.shape[1]
        pooled = None
        for e in range(across):
            attended = (state[2][e] / state[1][e]).astype(jnp.bfloat16)
            part = lax.dot_general(
                member_ref[e],
                attended,
                (((1,), (1,)), ((), ())),
                preferred_element_type=jnp.float32,
            )
            pooled = part if pooled is None else pooled + part
        for r in range(pooled.shape[0] // turns):
            mean = pooled[r * turns : (r + 1) * turns] * inverse_ref[...]
            for s in range(out_ref.shape[0]):
                out_ref[s, r * rows : (r + 1) * rows, :] = mean[s * rows : (s + 1) * rows]


def attend_next(across, distances, turns, turned, flags, below, state, pool, out_piece, weight, at, piece):
    last = pool is not None
    args = [flags, turned, *below, *state]
    in_specs = [in_vmem] * len(args)
    aliases, scratch = {}, []
    if at is not None:
        args.append(weight)
        in_specs.append(anywhere)
        scratch = [pltpu.SemaphoreType.DMA(())]
    if last:
        args += list(pool)
        in_specs += [in_vmem] * len(pool)
        out_shape = [jax.ShapeDtypeStruct(out_piece, jnp.float32)]
    else:
        out_shape = [jax.ShapeDtypeStruct(part.shape, part.dtype) for part in state]
        aliases = {2 + len(below) + i: i for i in range(len(state))}
    if at is not None:
        out_shape.append(jax.ShapeDtypeStruct((piece, weight.shape[1]), weight.dtype))
    return call(
        functools.partial(next_kernel, across, distances, turns, last, at),
        out_shape,
        in_specs=in_specs,
        scratch_shapes=scratch,
        input_output_aliases=aliases,
        limit=big_limit if at is not None else 16 * 1024 * 1024,
    )(*args)


def project_kernel(across, other, parts_ref, *refs):
    weights, out_ref = refs[:-1], refs[-1]
    rows = out_ref.shape[0]
    side = lax.axis_index("head")
    if other:
        side = 1 - side
    groups = []
    for y in range(across):
        total = parts_ref[y]
        for s in range(y + across, parts_ref.shape[0], across):
            total = total + parts_ref[s]
        groups += [total[at : at + rows] for at in range(0, total.shape[0], rows)]
    total = jnp.concatenate(groups, axis=1)
    high = total.astype(jnp.bfloat16)
    low = (total - high.astype(jnp.float32)).astype(jnp.bfloat16)
    both = jnp.concatenate([high, low], axis=0)
    half = out_ref.shape[1]
    step = math.gcd(half, 512)
    for c in range(half // step):
        start = pl.multiple_of(side * half + c * step, step)
        product, at = None, 0
        for weight_ref in weights:
            depth = weight_ref.shape[0]
            part = jnp.dot(
                both[:, at : at + depth],
                weight_ref[:, pl.ds(start, step)],
                preferred_element_type=jnp.float32,
            )
            product = part if product is None else product + part
            at += depth
        out_ref[:, c * step : (c + 1) * step] = product[:rows] + product[rows:]


def project(across, other, rows, parts, weights):
    return call(
        functools.partial(project_kernel, across, other),
        jax.ShapeDtypeStruct((rows, weights[0].shape[1] // 2), jnp.float32),
        in_specs=[in_vmem] * (1 + len(weights)),
    )(parts, *weights)


def on_device(count, queries, key_states, value_states, out_weight, turn_lengths, block_flags):
    across = key_states.shape[1] // HD
    down = count // across
    turns = turn_lengths.shape[0]

    def over(rows, shift):
        pairs = [(i, i - i % across + (i + shift) % across) for i in range(count)]
        return lax.ppermute(rows, "seq", pairs)

    def up(rows, distance, lowest=0):
        step = distance * across
        pairs = [(i, i + step) for i in range(lowest * across, count - step)]
        return lax.ppermute(rows, "seq", pairs)

    _, y = place(across)
    heads = []
    for shift in range(across):
        at = lax.rem(y + shift, across)
        heads.append(pair(pick(key_states, at, across), pick(value_states, at, across)))
    swapped = [over(heads[shift], shift) for shift in range(1, across)]
    rows = join([heads[0]] + swapped)
    first = up(heads[0], 1)
    rest = up(join(swapped), 1)
    rows, queries = lax.optimization_barrier((rows, queries))
    meta = lax.optimization_barrier(jnp.concatenate([turn_lengths, block_flags[0]]))
    padded = -(-count // 16) * 16
    flags = jnp.pad(meta[turns:], (0, padded - count))[:, None]
    groups = [pick(queries, lax.rem(y + shift, across), across) for shift in range(across)]
    sent = []
    for group in groups[1:]:
        under = jnp.broadcast_to(flags, (padded, group.shape[1])).astype(group.dtype)
        sent.append(jnp.concatenate([group, under], axis=0))
    flags = jnp.broadcast_to(flags, (padded, HD)).astype(jnp.float32)
    below = [rows, join_parts([first, rest], 2 * across)] + [None] * (down - 2)
    far, *sent = lax.optimization_barrier((rows, *sent))
    others = [over(group, shift) for shift, group in enumerate(sent, 1)]
    for distance in range(3, down):
        below[distance] = up(far, distance)
    if down > 2:
        below[2] = up(below[1], 1, 1)
    member, inverse = members(across, turns, meta, groups[0])
    inverse, flags = lax.optimization_barrier((inverse, flags))
    depth = out_weight.shape[0]
    pieces = [4 * depth // 8, 2 * depth // 8, 2 * depth // 8]
    turned, flags, weight, *state = attend_first(
        across, flags, [groups[0], *others], rows, out_weight, pieces[0]
    )
    weights = [weight]
    out_piece = (count, turns // count * (queries.shape[1] // across // HD), HD)
    stages = [[1]] + [list(range(d, min(d + 2, down))) for d in range(3, down, 2)] + [[2]]
    for number, distances in enumerate(stages):
        last = number == len(stages) - 1
        with_weight = number < 2
        state = attend_next(
            across,
            distances,
            turns,
            turned,
            flags,
            [below[distance] for distance in distances],
            state,
            (member, inverse) if last else None,
            out_piece,
            out_weight,
            sum(pieces[: len(weights)]) if with_weight else None,
            pieces[len(weights)] if with_weight else None,
        )
        if with_weight:
            *state, weight = state
            weights.append(weight)
    parts = lax.all_to_all(state[0], "seq", split_axis=0, concat_axis=0, tiled=True)
    theirs = project(across, True, turns // count, parts, weights)
    theirs = lax.ppermute(theirs, "head", [(0, 1), (1, 0)])
    return project(across, False, turns // count, parts, weights) + theirs


def solution(mesh):
    in_specs = (
        P(("conv", "seq"), "head"),
        P(("conv", "seq"), "head"),
        P(("conv", "seq"), "head"),
        P("head", None),
        P("conv"),
        P(("conv", "seq"), None),
    )
    out_specs = P(("conv", "seq"), "head")
    return jax.shard_map(
        functools.partial(on_device, mesh.shape["seq"]),
        mesh=mesh,
        in_specs=in_specs,
        out_specs=out_specs,
        check_vma=False,
    )
```

```python
import functools
import math

import jax
import jax.numpy as jnp
from jax import lax
from jax.experimental import pallas as pl
from jax.experimental.pallas import tpu as pltpu
from jax.sharding import PartitionSpec as P

HD = 128

big_negative = -1e30
log_two_e = 1.4426950408889634

big_limit = 45 * 1024 * 1024
small_cost = pl.CostEstimate(flops=1024, bytes_accessed=1024, transcendentals=0)

in_vmem = pl.BlockSpec(memory_space=pltpu.VMEM)
in_smem = pl.BlockSpec(memory_space=pltpu.SMEM)
anywhere = pl.BlockSpec(memory_space=pl.ANY)


def place(across):
    index = lax.axis_index("seq")
    return index // across, lax.rem(index, across)


def block_at(z, y, e, across):
    return z * across + lax.rem(y - e + across, across)


def call(kernel, out_shape, **settings):
    limit = settings.pop("limit", 16 * 1024 * 1024)
    return pl.pallas_call(
        kernel,
        out_shape=out_shape,
        out_specs=jax.tree.map(lambda _: in_vmem, out_shape),
        compiler_params=pltpu.CompilerParams(vmem_limit_bytes=limit),
        cost_estimate=small_cost,
        **settings,
    )


def pick(rows, number, parts):
    width = rows.shape[1] // parts
    picked = rows[:, :width]
    for part in range(1, parts):
        picked = jnp.where(number == part, rows[:, part * width : (part + 1) * width], picked)
    return picked


def pair(keys, values):
    which = lax.broadcasted_iota(jnp.int32, (2,) + keys.shape, 0)
    return jnp.where(which == 0, keys[None], values[None])


def join_kernel(*refs):
    *parts, out_ref = refs
    at = 0
    for part in parts:
        size = min(part.shape[0], out_ref.shape[0] - at)
        out_ref[at : at + size] = part[:size]
        at += size


def join_parts(parts, count):
    return join(parts, count)


def join(parts, count=None):
    count = sum(part.shape[0] for part in parts) if count is None else count
    shape = jax.ShapeDtypeStruct((count,) + parts[0].shape[1:], parts[0].dtype)
    return call(join_kernel, shape, in_specs=[in_vmem] * len(parts))(*parts)


def rows_update(turned_ref, rows_refs, switches, state, first):
    top, total_sum, totals = state
    across, _, columns = turned_ref.shape
    rows = rows_refs[0].shape[1]
    count = across * len(rows_refs)
    factor = log_two_e / math.sqrt(HD)
    keys = [
        jnp.concatenate([kv_ref[2 * e] for e in range(across)], axis=0) for kv_ref in rows_refs
    ]
    values = [
        jnp.concatenate([kv_ref[2 * e + 1] for e in range(across)], axis=0).T for kv_ref in rows_refs
    ]
    span = columns // 2 if columns % 256 == 0 else columns
    pieces = [(e, slice(at, at + span)) for e in range(across) for at in range(0, columns, span)]
    logits = [
        [jnp.dot(part, turned_ref[e, :, cut], preferred_element_type=jnp.float32) for part in keys]
        for e, cut in pieces
    ]
    for number, (e, cut) in enumerate(pieces):
        blocks = [
            logits[number][b // across][b % across * rows : (b % across + 1) * rows]
            for b in range(count)
        ]
        on = [None if switch is None else switch[:, cut] for switch in switches[e]]
        if first:
            key_pos = lax.broadcasted_iota(jnp.int32, (rows, 1), 0)
            column = cut.start + lax.broadcasted_iota(jnp.int32, (1, span), 1)
            blocks[e] = jnp.where(key_pos <= lax.rem(column, rows), blocks[e], big_negative)
        new_top = None if first else top[e, :, cut]
        for b in range(count):
            block_top = jnp.ceil(jnp.max(blocks[b], axis=0, keepdims=True) * factor)
            if on[b] is not None:
                block_top = jnp.where(on[b], block_top, big_negative)
            new_top = block_top if new_top is None else jnp.maximum(new_top, block_top)
        weights, block_sum = [], None
        for b in range(count):
            against = new_top
            if on[b] is not None:
                against = jnp.where(on[b], new_top, -big_negative)
            weights.append(jnp.exp2(blocks[b] * factor - against))
            part = jnp.sum(weights[b], axis=0, keepdims=True)
            block_sum = part if block_sum is None else block_sum + part
        update = None
        for i, part in enumerate(values):
            mine = weights[i * across : (i + 1) * across]
            mine = jnp.concatenate([w.astype(jnp.bfloat16) for w in mine], axis=0)
            part = jnp.dot(part, mine, preferred_element_type=jnp.float32)
            update = part if update is None else update + part
        if not first:
            rescale = jnp.exp2(top[e, :, cut] - new_top)
            block_sum = total_sum[e, :, cut] * rescale + block_sum
            update = totals[e, :, cut] * rescale + update
        top[e, :, cut] = new_top
        total_sum[e, :, cut] = block_sum
        totals[e, :, cut] = update


def switch_of(flags_ref, e, owner, columns, allowed=None):
    flag = flags_ref[e, pl.ds(jnp.maximum(owner, 0), 1), :]
    if allowed is not None:
        flag = flag * jnp.where(allowed, 1.0, 0.0)
    return jnp.concatenate([flag] * (columns // HD), axis=1) > 0.5


def member_kernel(across, turns, meta_ref, after_ref, member_ref, inverse_ref, rows_ref):
    del after_ref
    z, y = place(across)
    columns = rows_ref.shape[1]
    repeat = member_ref.shape[1] // turns
    q_rows = columns // repeat
    owners = [block_at(z, y, e, across) for e in range(across)]
    column = lax.broadcasted_iota(jnp.int32, (1, columns), 1)
    for e in range(across):
        position = lax.rem(column, q_rows) + owners[e] * q_rows
        start = jnp.int32(0)
        for t in range(turns):
            length = meta_ref[t]
            inside = (position >= start) & (position < start + length)
            rows_ref[t : t + 1, :] = jnp.where(inside, 1.0, 0.0)
            if e == 0:
                count = jnp.full((1, HD), length, jnp.int32).astype(jnp.float32)
                inverse_ref[t : t + 1, :] = 1.0 / count
            start = start + length
        for r in range(repeat):
            mine = (column >= r * q_rows) & (column < (r + 1) * q_rows)
            member_ref[e, r * turns : (r + 1) * turns, :] = jnp.where(
                mine, rows_ref[...], 0.0
            ).astype(jnp.bfloat16)


def members(across, turns, meta, group):
    q_rows, width = group.shape
    repeat = width // HD
    columns = repeat * q_rows
    return call(
        functools.partial(member_kernel, across, turns),
        [
            jax.ShapeDtypeStruct((across, repeat * turns, columns), jnp.bfloat16),
            jax.ShapeDtypeStruct((turns, HD), jnp.float32),
        ],
        in_specs=[in_smem, anywhere],
        scratch_shapes=[pltpu.VMEM((turns, columns), jnp.float32)],
    )(meta, group)


def weight_piece(weight_ref, out_ref, start, sem):
    return pltpu.make_async_copy(weight_ref.at[start : start + out_ref.shape[0]], out_ref, sem)


def first_kernel(across, own_flags_ref, *refs):
    queries, refs = refs[:across], refs[across:]
    kv_ref, weight_ref, turned_ref, flags_ref, weight_out = refs[:5]
    state, copied = refs[5:8], refs[8]
    weight_copy = weight_piece(weight_ref, weight_out, 0, copied)
    weight_copy.start()
    z, y = place(across)
    q_rows = kv_ref.shape[1]
    repeat = queries[0].shape[1] // HD
    columns = repeat * q_rows
    for e in range(across):
        for r in range(repeat):
            turned_ref[e, :, r * q_rows : (r + 1) * q_rows] = queries[e][
                0:q_rows, r * HD : (r + 1) * HD
            ].T
    flags_ref[0] = own_flags_ref[...]
    for e in range(1, across):
        flags_ref[e] = queries[e][q_rows:, 0:HD].astype(jnp.float32)
    owners = [block_at(z, y, e, across) for e in range(across)]
    switches = [
        [
            None if e == b else switch_of(flags_ref, e, owners[b], columns, owners[b] < owners[e])
            for b in range(across)
        ]
        for e in range(across)
    ]
    rows_update(turned_ref, [kv_ref], switches, state, True)

    weight_copy.wait()


def attend_first(across, flags, queries, rows, weight, piece):
    q_rows = rows.shape[1]
    repeat = queries[0].shape[1] // HD
    columns = repeat * q_rows
    f32, b16 = jnp.float32, jnp.bfloat16
    return call(
        functools.partial(first_kernel, across),
        [
            jax.ShapeDtypeStruct((across, HD, columns), b16),
            jax.ShapeDtypeStruct((across,) + flags.shape, f32),
            jax.ShapeDtypeStruct((piece, weight.shape[1]), weight.dtype),
            jax.ShapeDtypeStruct((across, 1, columns), f32),
            jax.ShapeDtypeStruct((across, 1, columns), f32),
            jax.ShapeDtypeStruct((across, HD, columns), f32),
        ],
        in_specs=[in_vmem] * (across + 2) + [anywhere],
        scratch_shapes=[pltpu.SemaphoreType.DMA(())],
        limit=big_limit,
    )(flags, *queries, rows, weight)


def next_kernel(across, distances, turns, last, weight_at, flags_ref, turned_ref, *refs):
    below_count = len(distances)
    below, state, refs = refs[:below_count], refs[below_count : below_count + 3], refs[below_count + 3 :]
    if weight_at is not None:
        weight_ref, weight_out, copied = refs[0], refs[-2], refs[-1]
        refs = refs[1:-2]
        weight_copy = weight_piece(weight_ref, weight_out, weight_at, copied)
        weight_copy.start()
    z, y = place(across)
    columns = turned_ref.shape[2]

    def update(rows, from_distances):
        switches = [
            [
                switch_of(flags_ref, e, block_at(z - distance, y, b, across), columns)
                for distance in from_distances
                for b in range(across)
            ]
            for e in range(across)
        ]
        rows_update(turned_ref, rows, switches, state, False)

    for number, distance in enumerate(distances, 1):
        here = (z >= distance) if number == len(distances) else (z == distance)
        pl.when(here)(functools.partial(update, below[:number], distances[:number]))

    if weight_at is not None:
        weight_copy.wait()
    if last:
        member_ref, inverse_ref, out_ref = refs
        rows = out_ref.shape[1]
        pooled = None
        for e in range(across):
            attended = (state[2][e] / state[1][e]).astype(jnp.bfloat16)
            part = lax.dot_general(
                member_ref[e],
                attended,
                (((1,), (1,)), ((), ())),
                preferred_element_type=jnp.float32,
            )
            pooled = part if pooled is None else pooled + part
        for r in range(pooled.shape[0] // turns):
            mean = pooled[r * turns : (r + 1) * turns] * inverse_ref[...]
            for s in range(out_ref.shape[0]):
                out_ref[s, :, r * HD : (r + 1) * HD] = mean[s * rows : (s + 1) * rows]


def attend_next(across, distances, turns, turned, flags, below, state, pool, out_piece, weight, at, piece):
    last = pool is not None
    args = [flags, turned, *below, *state]
    in_specs = [in_vmem] * len(args)
    aliases, scratch = {}, []
    if at is not None:
        args.append(weight)
        in_specs.append(anywhere)
        scratch = [pltpu.SemaphoreType.DMA(())]
    if last:
        args += list(pool)
        in_specs += [in_vmem] * len(pool)
        out_shape = [jax.ShapeDtypeStruct(out_piece, jnp.float32)]
    else:
        out_shape = [jax.ShapeDtypeStruct(part.shape, part.dtype) for part in state]
        aliases = {2 + len(below) + i: i for i in range(len(state))}
    if at is not None:
        out_shape.append(jax.ShapeDtypeStruct((piece, weight.shape[1]), weight.dtype))
    return call(
        functools.partial(next_kernel, across, distances, turns, last, at),
        out_shape,
        in_specs=in_specs,
        scratch_shapes=scratch,
        input_output_aliases=aliases,
        limit=big_limit if at is not None else 16 * 1024 * 1024,
    )(*args)


def project_kernel(across, other, parts_ref, *refs):
    weights, out_ref = refs[:-1], refs[-1]
    side = lax.axis_index("head")
    if other:
        side = 1 - side
    groups = []
    for y in range(across):
        total = parts_ref[y]
        for s in range(y + across, parts_ref.shape[0], across):
            total = total + parts_ref[s]
        groups.append(total)
    total = jnp.concatenate(groups, axis=1)
    rows = total.shape[0]
    high = total.astype(jnp.bfloat16)
    low = (total - high.astype(jnp.float32)).astype(jnp.bfloat16)
    both = jnp.concatenate([high, low], axis=0)
    half = out_ref.shape[1]
    step = math.gcd(half, 512)
    for c in range(half // step):
        start = pl.multiple_of(side * half + c * step, step)
        product, at = None, 0
        for weight_ref in weights:
            depth = weight_ref.shape[0]
            part = jnp.dot(
                both[:, at : at + depth],
                weight_ref[:, pl.ds(start, step)],
                preferred_element_type=jnp.float32,
            )
            product = part if product is None else product + part
            at += depth
        out_ref[:, c * step : (c + 1) * step] = product[:rows] + product[rows:]


def project(across, other, parts, weights):
    return call(
        functools.partial(project_kernel, across, other),
        jax.ShapeDtypeStruct((parts.shape[1], weights[0].shape[1] // 2), jnp.float32),
        in_specs=[in_vmem] * (1 + len(weights)),
    )(parts, *weights)


def on_device(count, queries, key_states, value_states, out_weight, turn_lengths, block_flags):
    across = key_states.shape[1] // HD
    down = count // across
    turns = turn_lengths.shape[0]

    def over(rows, shift):
        pairs = [(i, i - i % across + (i + shift) % across) for i in range(count)]
        return lax.ppermute(rows, "seq", pairs)

    def up(rows, distance, lowest=0):
        step = distance * across
        pairs = [(i, i + step) for i in range(lowest * across, count - step)]
        return lax.ppermute(rows, "seq", pairs)

    _, y = place(across)
    heads = []
    for shift in range(across):
        at = lax.rem(y + shift, across)
        heads.append(pair(pick(key_states, at, across), pick(value_states, at, across)))
    swapped = [over(heads[shift], shift) for shift in range(1, across)]
    rows = join([heads[0]] + swapped)
    first = up(heads[0], 1)
    rest = up(join(swapped), 1)
    rows, queries = lax.optimization_barrier((rows, queries))
    meta = lax.optimization_barrier(jnp.concatenate([turn_lengths, block_flags[0]]))
    padded = -(-count // 16) * 16
    flags = jnp.pad(meta[turns:], (0, padded - count))[:, None]
    groups = [pick(queries, lax.rem(y + shift, across), across) for shift in range(across)]
    sent = []
    for group in groups[1:]:
        under = jnp.broadcast_to(flags, (padded, group.shape[1])).astype(group.dtype)
        sent.append(jnp.concatenate([group, under], axis=0))
    flags = jnp.broadcast_to(flags, (padded, HD)).astype(jnp.float32)
    below = [rows, join_parts([first, rest], 2 * across)] + [None] * (down - 2)
    far, *sent = lax.optimization_barrier((rows, *sent))
    others = [over(group, shift) for shift, group in enumerate(sent, 1)]
    for distance in range(3, down):
        below[distance] = up(far, distance)
    if down > 2:
        below[2] = up(below[1], 1, 1)
    member, inverse = members(across, turns, meta, groups[0])
    inverse, flags = lax.optimization_barrier((inverse, flags))
    depth = out_weight.shape[0]
    pieces = [4 * depth // 8, 2 * depth // 8, 2 * depth // 8]
    turned, flags, weight, *state = attend_first(
        across, flags, [groups[0], *others], rows, out_weight, pieces[0]
    )
    weights = [weight]
    out_piece = (count, turns // count, queries.shape[1] // across)
    stages = [[1]] + [list(range(d, min(d + 2, down))) for d in range(3, down, 2)] + [[2]]
    for number, distances in enumerate(stages):
        last = number == len(stages) - 1
        with_weight = number < 2
        state = attend_next(
            across,
            distances,
            turns,
            turned,
            flags,
            [below[distance] for distance in distances],
            state,
            (member, inverse) if last else None,
            out_piece,
            out_weight,
            sum(pieces[: len(weights)]) if with_weight else None,
            pieces[len(weights)] if with_weight else None,
        )
        if with_weight:
            *state, weight = state
            weights.append(weight)
    parts = lax.all_to_all(state[0], "seq", split_axis=0, concat_axis=0, tiled=True)
    theirs = project(across, True, parts, weights)
    theirs = lax.ppermute(theirs, "head", [(0, 1), (1, 0)])
    return project(across, False, parts, weights) + theirs


def solution(mesh):
    in_specs = (
        P(("conv", "seq"), "head"),
        P(("conv", "seq"), "head"),
        P(("conv", "seq"), "head"),
        P("head", None),
        P("conv"),
        P(("conv", "seq"), None),
    )
    out_specs = P(("conv", "seq"), "head")
    return jax.shard_map(
        functools.partial(on_device, mesh.shape["seq"]),
        mesh=mesh,
        in_specs=in_specs,
        out_specs=out_specs,
        check_vma=False,
    )
```

```python
import functools
import math

import jax
import jax.numpy as jnp
from jax import lax
from jax.experimental import pallas as pl
from jax.experimental.pallas import tpu as pltpu
from jax.sharding import PartitionSpec as P

HD = 128

big_negative = -1e30
log_two_e = 1.4426950408889634

big_limit = 45 * 1024 * 1024
long_flops = 4 * 10**9

in_vmem = pl.BlockSpec(memory_space=pltpu.VMEM)
in_smem = pl.BlockSpec(memory_space=pltpu.SMEM)
anywhere = pl.BlockSpec(memory_space=pl.ANY)


def place(across):
    index = lax.axis_index("seq")
    return index // across, lax.rem(index, across)


def block_at(z, y, e, across):
    return z * across + lax.rem(y - e + across, across)


def call(kernel, out_shape, **settings):
    limit = settings.pop("limit", 16 * 1024 * 1024)
    flops = settings.pop("flops", 0)
    return pl.pallas_call(
        kernel,
        out_shape=out_shape,
        out_specs=jax.tree.map(lambda _: in_vmem, out_shape),
        compiler_params=pltpu.CompilerParams(vmem_limit_bytes=limit),
        cost_estimate=pl.CostEstimate(flops=flops, bytes_accessed=1024, transcendentals=0),
        **settings,
    )


def pick(rows, number, parts):
    width = rows.shape[1] // parts
    picked = rows[:, :width]
    for part in range(1, parts):
        picked = jnp.where(number == part, rows[:, part * width : (part + 1) * width], picked)
    return picked


def pair(keys, values):
    which = lax.broadcasted_iota(jnp.int32, (2,) + keys.shape, 0)
    return jnp.where(which == 0, keys[None], values[None])


def join_kernel(*refs):
    *parts, out_ref = refs
    at = 0
    for part in parts:
        size = min(part.shape[0], out_ref.shape[0] - at)
        out_ref[at : at + size] = part[:size]
        at += size


def join_parts(parts, count):
    return join(parts, count)


def join(parts, count=None):
    count = sum(part.shape[0] for part in parts) if count is None else count
    shape = jax.ShapeDtypeStruct((count,) + parts[0].shape[1:], parts[0].dtype)
    return call(join_kernel, shape, in_specs=[in_vmem] * len(parts))(*parts)


def rows_update(turned_ref, rows_refs, switches, state, first):
    top, total_sum, totals = state
    across, _, columns = turned_ref.shape
    rows = rows_refs[0].shape[1]
    count = across * len(rows_refs)
    factor = log_two_e / math.sqrt(HD)
    keys = [
        jnp.concatenate([kv_ref[2 * e] for e in range(across)], axis=0) for kv_ref in rows_refs
    ]
    values = [
        jnp.concatenate([kv_ref[2 * e + 1] for e in range(across)], axis=0).T for kv_ref in rows_refs
    ]
    span = columns // 2 if columns % 256 == 0 else columns
    pieces = [(e, slice(at, at + span)) for e in range(across) for at in range(0, columns, span)]
    logits = [
        [jnp.dot(part, turned_ref[e, :, cut], preferred_element_type=jnp.float32) for part in keys]
        for e, cut in pieces
    ]
    for number, (e, cut) in enumerate(pieces):
        blocks = [
            logits[number][b // across][b % across * rows : (b % across + 1) * rows]
            for b in range(count)
        ]
        on = [None if switch is None else switch[:, cut] for switch in switches[e]]
        if first:
            key_pos = lax.broadcasted_iota(jnp.int32, (rows, 1), 0)
            column = cut.start + lax.broadcasted_iota(jnp.int32, (1, span), 1)
            blocks[e] = jnp.where(key_pos <= lax.rem(column, rows), blocks[e], big_negative)
        new_top = None if first else top[e, :, cut]
        for b in range(count):
            block_top = jnp.ceil(jnp.max(blocks[b], axis=0, keepdims=True) * factor)
            if on[b] is not None:
                block_top = jnp.where(on[b], block_top, big_negative)
            new_top = block_top if new_top is None else jnp.maximum(new_top, block_top)
        weights, block_sum = [], None
        for b in range(count):
            against = new_top
            if on[b] is not None:
                against = jnp.where(on[b], new_top, -big_negative)
            weights.append(jnp.exp2(blocks[b] * factor - against))
            part = jnp.sum(weights[b], axis=0, keepdims=True)
            block_sum = part if block_sum is None else block_sum + part
        update = None
        for i, part in enumerate(values):
            mine = weights[i * across : (i + 1) * across]
            mine = jnp.concatenate([w.astype(jnp.bfloat16) for w in mine], axis=0)
            part = jnp.dot(part, mine, preferred_element_type=jnp.float32)
            update = part if update is None else update + part
        if not first:
            rescale = jnp.exp2(top[e, :, cut] - new_top)
            block_sum = total_sum[e, :, cut] * rescale + block_sum
            update = totals[e, :, cut] * rescale + update
        top[e, :, cut] = new_top
        total_sum[e, :, cut] = block_sum
        totals[e, :, cut] = update


def switch_of(flags_ref, e, owner, columns, allowed=None):
    flag = flags_ref[e, pl.ds(jnp.maximum(owner, 0), 1), :]
    if allowed is not None:
        flag = flag * jnp.where(allowed, 1.0, 0.0)
    return jnp.concatenate([flag] * (columns // HD), axis=1) > 0.5


def member_kernel(across, turns, meta_ref, after_ref, member_ref, inverse_ref, rows_ref):
    del after_ref
    z, y = place(across)
    columns = rows_ref.shape[1]
    repeat = member_ref.shape[1] // turns
    q_rows = columns // repeat
    owners = [block_at(z, y, e, across) for e in range(across)]
    column = lax.broadcasted_iota(jnp.int32, (1, columns), 1)
    for e in range(across):
        position = lax.rem(column, q_rows) + owners[e] * q_rows
        start = jnp.int32(0)
        for t in range(turns):
            length = meta_ref[t]
            inside = (position >= start) & (position < start + length)
            rows_ref[t : t + 1, :] = jnp.where(inside, 1.0, 0.0)
            if e == 0:
                count = jnp.full((1, HD), length, jnp.int32).astype(jnp.float32)
                inverse_ref[t : t + 1, :] = 1.0 / count
            start = start + length
        for r in range(repeat):
            mine = (column >= r * q_rows) & (column < (r + 1) * q_rows)
            member_ref[e, r * turns : (r + 1) * turns, :] = jnp.where(
                mine, rows_ref[...], 0.0
            ).astype(jnp.bfloat16)


def members(across, turns, meta, group):
    q_rows, width = group.shape
    repeat = width // HD
    columns = repeat * q_rows
    return call(
        functools.partial(member_kernel, across, turns),
        [
            jax.ShapeDtypeStruct((across, repeat * turns, columns), jnp.bfloat16),
            jax.ShapeDtypeStruct((turns, HD), jnp.float32),
        ],
        in_specs=[in_smem, anywhere],
        scratch_shapes=[pltpu.VMEM((turns, columns), jnp.float32)],
        flops=long_flops,
    )(meta, group)


def weight_piece(weight_ref, out_ref, start, sem):
    return pltpu.make_async_copy(weight_ref.at[start : start + out_ref.shape[0]], out_ref, sem)


def early_kernel(across, start, weight_ref, _, out_ref, copied):
    z, _ = place(across)

    @pl.when(z == 0)
    def _():
        copy = weight_piece(weight_ref, out_ref, start, copied)
        copy.start()
        copy.wait()


def early_piece(across, weight, start, piece, after):
    return call(
        functools.partial(early_kernel, across, start),
        jax.ShapeDtypeStruct((piece, weight.shape[1]), weight.dtype),
        in_specs=[anywhere] * 2,
        scratch_shapes=[pltpu.SemaphoreType.DMA(())],
        limit=big_limit,
    )(weight, after)


def first_kernel(across, own_flags_ref, *refs):
    queries, refs = refs[:across], refs[across:]
    kv_ref, weight_ref, turned_ref, flags_ref, weight_out = refs[:5]
    state, copied = refs[5:8], refs[8]
    weight_copy = weight_piece(weight_ref, weight_out, 0, copied)
    weight_copy.start()
    z, y = place(across)
    q_rows = kv_ref.shape[1]
    repeat = queries[0].shape[1] // HD
    columns = repeat * q_rows
    for e in range(across):
        for r in range(repeat):
            turned_ref[e, :, r * q_rows : (r + 1) * q_rows] = queries[e][
                0:q_rows, r * HD : (r + 1) * HD
            ].T
    flags_ref[0] = own_flags_ref[...]
    for e in range(1, across):
        flags_ref[e] = queries[e][q_rows:, 0:HD].astype(jnp.float32)
    owners = [block_at(z, y, e, across) for e in range(across)]
    switches = [
        [
            None if e == b else switch_of(flags_ref, e, owners[b], columns, owners[b] < owners[e])
            for b in range(across)
        ]
        for e in range(across)
    ]
    rows_update(turned_ref, [kv_ref], switches, state, True)

    weight_copy.wait()


def attend_first(across, flags, queries, rows, weight, piece):
    q_rows = rows.shape[1]
    repeat = queries[0].shape[1] // HD
    columns = repeat * q_rows
    f32, b16 = jnp.float32, jnp.bfloat16
    return call(
        functools.partial(first_kernel, across),
        [
            jax.ShapeDtypeStruct((across, HD, columns), b16),
            jax.ShapeDtypeStruct((across,) + flags.shape, f32),
            jax.ShapeDtypeStruct((piece, weight.shape[1]), weight.dtype),
            jax.ShapeDtypeStruct((across, 1, columns), f32),
            jax.ShapeDtypeStruct((across, 1, columns), f32),
            jax.ShapeDtypeStruct((across, HD, columns), f32),
        ],
        in_specs=[in_vmem] * (across + 2) + [anywhere],
        scratch_shapes=[pltpu.SemaphoreType.DMA(())],
        limit=big_limit,
    )(flags, *queries, rows, weight)


def next_kernel(across, distances, turns, last, weight_at, early_at, flags_ref, turned_ref, *refs):
    below_count = len(distances)
    below, state, refs = refs[:below_count], refs[below_count : below_count + 3], refs[below_count + 3 :]
    if weight_at is not None:
        weight_ref, weight_out, copied = refs[0], refs[-2], refs[-1]
        refs = refs[1:-2]
        weight_copy = weight_piece(weight_ref, weight_out, weight_at, copied)
        weight_copy.start()
    z, y = place(across)
    if early_at is not None:
        weight_ref, early_out, copied = refs[1], refs[-2], refs[-1]

        @pl.when(z != 0)
        def _():
            weight_piece(weight_ref, early_out, early_at, copied).start()

    columns = turned_ref.shape[2]

    def update(rows, from_distances):
        switches = [
            [
                switch_of(flags_ref, e, block_at(z - distance, y, b, across), columns)
                for distance in from_distances
                for b in range(across)
            ]
            for e in range(across)
        ]
        rows_update(turned_ref, rows, switches, state, False)

    for number, distance in enumerate(distances, 1):
        here = (z >= distance) if number == len(distances) else (z == distance)
        pl.when(here)(functools.partial(update, below[:number], distances[:number]))

    if weight_at is not None:
        weight_copy.wait()
    if early_at is not None:

        @pl.when(z != 0)
        def _():
            weight_piece(weight_ref, early_out, early_at, copied).wait()

    if last:
        member_ref, inverse_ref, out_ref = refs
        rows = out_ref.shape[1]
        pooled = None
        for e in range(across):
            attended = (state[2][e] / state[1][e]).astype(jnp.bfloat16)
            part = lax.dot_general(
                member_ref[e],
                attended,
                (((1,), (1,)), ((), ())),
                preferred_element_type=jnp.float32,
            )
            pooled = part if pooled is None else pooled + part
        for r in range(pooled.shape[0] // turns):
            mean = pooled[r * turns : (r + 1) * turns] * inverse_ref[...]
            for s in range(out_ref.shape[0]):
                out_ref[s, :, r * HD : (r + 1) * HD] = mean[s * rows : (s + 1) * rows]


def attend_next(across, distances, turns, turned, flags, below, state, pool, out_piece, weight, at, piece, early=None):
    last = pool is not None
    args = [flags, turned, *below, *state]
    in_specs = [in_vmem] * len(args)
    aliases, scratch = {}, []
    if at is not None:
        args.append(weight)
        in_specs.append(anywhere)
        scratch = [pltpu.SemaphoreType.DMA(())]
    if early is not None:
        early_at = weight.shape[0] - early.shape[0]
        early_aliases = {len(args): len(state)}
        args += [early, weight]
        in_specs += [in_vmem, anywhere]
        scratch = [pltpu.SemaphoreType.DMA(())]
    else:
        early_at, early_aliases = None, {}
    if last:
        args += list(pool)
        in_specs += [in_vmem] * len(pool)
        out_shape = [jax.ShapeDtypeStruct(out_piece, jnp.float32)]
    else:
        out_shape = [jax.ShapeDtypeStruct(part.shape, part.dtype) for part in state]
        aliases = {2 + len(below) + i: i for i in range(len(state))}
    if at is not None:
        out_shape.append(jax.ShapeDtypeStruct((piece, weight.shape[1]), weight.dtype))
    if early is not None:
        out_shape.append(jax.ShapeDtypeStruct(early.shape, early.dtype))
        aliases.update(early_aliases)
    return call(
        functools.partial(next_kernel, across, distances, turns, last, at, early_at),
        out_shape,
        in_specs=in_specs,
        scratch_shapes=scratch,
        input_output_aliases=aliases,
        limit=big_limit if scratch else 16 * 1024 * 1024,
    )(*args)


def project_kernel(across, other, parts_ref, *refs):
    weights, out_ref = refs[:-1], refs[-1]
    side = lax.axis_index("head")
    if other:
        side = 1 - side
    groups = []
    for y in range(across):
        total = parts_ref[y]
        for s in range(y + across, parts_ref.shape[0], across):
            total = total + parts_ref[s]
        groups.append(total)
    total = jnp.concatenate(groups, axis=1)
    rows = total.shape[0]
    high = total.astype(jnp.bfloat16)
    low = (total - high.astype(jnp.float32)).astype(jnp.bfloat16)
    both = jnp.concatenate([high, low], axis=0)
    half = out_ref.shape[1]
    step = math.gcd(half, 512)
    for c in range(half // step):
        start = pl.multiple_of(side * half + c * step, step)
        product, at = None, 0
        for weight_ref in weights:
            depth = weight_ref.shape[0]
            part = jnp.dot(
                both[:, at : at + depth],
                weight_ref[:, pl.ds(start, step)],
                preferred_element_type=jnp.float32,
            )
            product = part if product is None else product + part
            at += depth
        out_ref[:, c * step : (c + 1) * step] = product[:rows] + product[rows:]


def project(across, other, parts, weights):
    return call(
        functools.partial(project_kernel, across, other),
        jax.ShapeDtypeStruct((parts.shape[1], weights[0].shape[1] // 2), jnp.float32),
        in_specs=[in_vmem] * (1 + len(weights)),
    )(parts, *weights)


def on_device(count, queries, key_states, value_states, out_weight, turn_lengths, block_flags):
    across = key_states.shape[1] // HD
    down = count // across
    turns = turn_lengths.shape[0]

    def over(rows, shift):
        pairs = [(i, i - i % across + (i + shift) % across) for i in range(count)]
        return lax.ppermute(rows, "seq", pairs)

    def up(rows, distance, lowest=0):
        step = distance * across
        pairs = [(i, i + step) for i in range(lowest * across, count - step)]
        return lax.ppermute(rows, "seq", pairs)

    _, y = place(across)
    heads = []
    for shift in range(across):
        at = lax.rem(y + shift, across)
        heads.append(pair(pick(key_states, at, across), pick(value_states, at, across)))
    swapped = [over(heads[shift], shift) for shift in range(1, across)]
    rows = join([heads[0]] + swapped)
    first = up(heads[0], 1)
    rest = up(join(swapped), 1)
    rows, queries = lax.optimization_barrier((rows, queries))
    meta = lax.optimization_barrier(jnp.concatenate([turn_lengths, block_flags[0]]))
    padded = -(-count // 16) * 16
    flags = jnp.pad(meta[turns:], (0, padded - count))[:, None]
    groups = [pick(queries, lax.rem(y + shift, across), across) for shift in range(across)]
    sent = []
    for group in groups[1:]:
        under = jnp.broadcast_to(flags, (padded, group.shape[1])).astype(group.dtype)
        sent.append(jnp.concatenate([group, under], axis=0))
    flags = jnp.broadcast_to(flags, (padded, HD)).astype(jnp.float32)
    below = [rows, join_parts([first, rest], 2 * across)] + [None] * (down - 2)
    early = early_piece(across, out_weight, out_weight.shape[0] - out_weight.shape[0] // 8, out_weight.shape[0] // 8, groups[0])
    far, early = lax.optimization_barrier((rows, early))
    early, *sent = lax.optimization_barrier((early, *sent))
    others = [over(group, shift) for shift, group in enumerate(sent, 1)]
    for distance in range(3, down):
        below[distance] = up(far, distance)
    if down > 2:
        below[2] = up(below[1], 1, 1)
    member, inverse = members(across, turns, meta, groups[0])
    inverse, flags = lax.optimization_barrier((inverse, flags))
    depth = out_weight.shape[0]
    pieces = [4 * depth // 8, 3 * depth // 8, depth // 8]
    turned, flags, weight, *state = attend_first(
        across, flags, [groups[0], *others], rows, out_weight, pieces[0]
    )
    weights = [weight]
    out_piece = (count, turns // count, queries.shape[1] // across)
    stages = [[1]] + [list(range(d, min(d + 2, down))) for d in range(3, down, 2)] + [[2]]
    for number, distances in enumerate(stages):
        last = number == len(stages) - 1
        with_weight = number == 0
        state = attend_next(
            across,
            distances,
            turns,
            turned,
            flags,
            [below[distance] for distance in distances],
            state,
            (member, inverse) if last else None,
            out_piece,
            out_weight,
            sum(pieces[: len(weights)]) if with_weight else None,
            pieces[len(weights)] if with_weight else None,
            early if number == 1 else None,
        )
        if with_weight or number == 1:
            *state, weight = state
            weights.append(weight)
    parts = lax.all_to_all(state[0], "seq", split_axis=0, concat_axis=0, tiled=True)
    theirs = project(across, True, parts, weights)
    theirs = lax.ppermute(theirs, "head", [(0, 1), (1, 0)])
    return project(across, False, parts, weights) + theirs


def solution(mesh):
    in_specs = (
        P(("conv", "seq"), "head"),
        P(("conv", "seq"), "head"),
        P(("conv", "seq"), "head"),
        P("head", None),
        P("conv"),
        P(("conv", "seq"), None),
    )
    out_specs = P(("conv", "seq"), "head")
    return jax.shard_map(
        functools.partial(on_device, mesh.shape["seq"]),
        mesh=mesh,
        in_specs=in_specs,
        out_specs=out_specs,
        check_vma=False,
    )
```

```python
import functools
import math

import jax
import jax.numpy as jnp
from jax import lax
from jax.experimental import pallas as pl
from jax.experimental.pallas import tpu as pltpu
from jax.sharding import PartitionSpec as P

HD = 128

big_negative = -1e30
log_two_e = 1.4426950408889634

big_limit = 45 * 1024 * 1024
long_flops = 4 * 10**9

in_vmem = pl.BlockSpec(memory_space=pltpu.VMEM)
in_smem = pl.BlockSpec(memory_space=pltpu.SMEM)
anywhere = pl.BlockSpec(memory_space=pl.ANY)


def place(across):
    index = lax.axis_index("seq")
    return index // across, lax.rem(index, across)


def block_at(z, y, e, across):
    return z * across + lax.rem(y - e + across, across)


def call(kernel, out_shape, **settings):
    limit = settings.pop("limit", 16 * 1024 * 1024)
    flops = settings.pop("flops", 0)
    return pl.pallas_call(
        kernel,
        out_shape=out_shape,
        out_specs=jax.tree.map(lambda _: in_vmem, out_shape),
        compiler_params=pltpu.CompilerParams(vmem_limit_bytes=limit),
        cost_estimate=pl.CostEstimate(flops=flops, bytes_accessed=1024, transcendentals=0),
        **settings,
    )


def pick(rows, number, parts):
    width = rows.shape[1] // parts
    picked = rows[:, :width]
    for part in range(1, parts):
        picked = jnp.where(number == part, rows[:, part * width : (part + 1) * width], picked)
    return picked


def pair(keys, values):
    which = lax.broadcasted_iota(jnp.int32, (2,) + keys.shape, 0)
    return jnp.where(which == 0, keys[None], values[None])


def join_kernel(*refs):
    *parts, out_ref = refs
    at = 0
    for part in parts:
        size = min(part.shape[0], out_ref.shape[0] - at)
        out_ref[at : at + size] = part[:size]
        at += size


def join_parts(parts, count):
    return join(parts, count)


def join(parts, count=None):
    count = sum(part.shape[0] for part in parts) if count is None else count
    shape = jax.ShapeDtypeStruct((count,) + parts[0].shape[1:], parts[0].dtype)
    return call(join_kernel, shape, in_specs=[in_vmem] * len(parts))(*parts)


def rows_update(turned_ref, rows_refs, switches, state, first):
    top, total_sum, totals = state
    across, _, columns = turned_ref.shape
    rows = rows_refs[0].shape[1]
    count = across * len(rows_refs)
    factor = log_two_e / math.sqrt(HD)
    keys = [
        jnp.concatenate([kv_ref[2 * e] for e in range(across)], axis=0) for kv_ref in rows_refs
    ]
    values = [
        jnp.concatenate([kv_ref[2 * e + 1] for e in range(across)], axis=0).T for kv_ref in rows_refs
    ]
    span = columns // 2 if columns % 256 == 0 else columns
    pieces = [(e, slice(at, at + span)) for e in range(across) for at in range(0, columns, span)]
    logits = [
        [jnp.dot(part, turned_ref[e, :, cut], preferred_element_type=jnp.float32) for part in keys]
        for e, cut in pieces
    ]
    for number, (e, cut) in enumerate(pieces):
        blocks = [
            logits[number][b // across][b % across * rows : (b % across + 1) * rows]
            for b in range(count)
        ]
        on = [None if switch is None else switch[:, cut] for switch in switches[e]]
        if first:
            key_pos = lax.broadcasted_iota(jnp.int32, (rows, 1), 0)
            column = cut.start + lax.broadcasted_iota(jnp.int32, (1, span), 1)
            blocks[e] = jnp.where(key_pos <= lax.rem(column, rows), blocks[e], big_negative)
        new_top = None if first else top[e, :, cut]
        for b in range(count):
            block_top = jnp.ceil(jnp.max(blocks[b], axis=0, keepdims=True) * factor)
            if on[b] is not None:
                block_top = jnp.where(on[b], block_top, big_negative)
            new_top = block_top if new_top is None else jnp.maximum(new_top, block_top)
        weights, block_sum = [], None
        for b in range(count):
            against = new_top
            if on[b] is not None:
                against = jnp.where(on[b], new_top, -big_negative)
            weights.append(jnp.exp2(blocks[b] * factor - against))
            part = jnp.sum(weights[b], axis=0, keepdims=True)
            block_sum = part if block_sum is None else block_sum + part
        update = None
        for i, part in enumerate(values):
            mine = weights[i * across : (i + 1) * across]
            mine = jnp.concatenate([w.astype(jnp.bfloat16) for w in mine], axis=0)
            part = jnp.dot(part, mine, preferred_element_type=jnp.float32)
            update = part if update is None else update + part
        if not first:
            rescale = jnp.exp2(top[e, :, cut] - new_top)
            block_sum = total_sum[e, :, cut] * rescale + block_sum
            update = totals[e, :, cut] * rescale + update
        top[e, :, cut] = new_top
        total_sum[e, :, cut] = block_sum
        totals[e, :, cut] = update


def switch_of(flags_ref, e, owner, columns, allowed=None):
    flag = flags_ref[e, pl.ds(jnp.maximum(owner, 0), 1), :]
    if allowed is not None:
        flag = flag * jnp.where(allowed, 1.0, 0.0)
    return jnp.concatenate([flag] * (columns // HD), axis=1) > 0.5


def member_kernel(across, turns, meta_ref, after_ref, member_ref, inverse_ref, rows_ref):
    del after_ref
    z, y = place(across)
    columns = rows_ref.shape[1]
    repeat = member_ref.shape[1] // turns
    q_rows = columns // repeat
    owners = [block_at(z, y, e, across) for e in range(across)]
    column = lax.broadcasted_iota(jnp.int32, (1, columns), 1)
    for e in range(across):
        position = lax.rem(column, q_rows) + owners[e] * q_rows
        start = jnp.int32(0)
        for t in range(turns):
            length = meta_ref[t]
            inside = (position >= start) & (position < start + length)
            rows_ref[t : t + 1, :] = jnp.where(inside, 1.0, 0.0)
            if e == 0:
                count = jnp.full((1, HD), length, jnp.int32).astype(jnp.float32)
                inverse_ref[t : t + 1, :] = 1.0 / count
            start = start + length
        for r in range(repeat):
            mine = (column >= r * q_rows) & (column < (r + 1) * q_rows)
            member_ref[e, r * turns : (r + 1) * turns, :] = jnp.where(
                mine, rows_ref[...], 0.0
            ).astype(jnp.bfloat16)


def members(across, turns, meta, group):
    q_rows, width = group.shape
    repeat = width // HD
    columns = repeat * q_rows
    return call(
        functools.partial(member_kernel, across, turns),
        [
            jax.ShapeDtypeStruct((across, repeat * turns, columns), jnp.bfloat16),
            jax.ShapeDtypeStruct((turns, HD), jnp.float32),
        ],
        in_specs=[in_smem, anywhere],
        scratch_shapes=[pltpu.VMEM((turns, columns), jnp.float32)],
        flops=long_flops,
    )(meta, group)


def weight_piece(weight_ref, out_ref, start, sem):
    return pltpu.make_async_copy(weight_ref.at[start : start + out_ref.shape[0]], out_ref, sem)


def early_kernel(across, start, weight_ref, _, out_ref, copied):
    z, _ = place(across)

    @pl.when(z == 0)
    def _():
        copy = weight_piece(weight_ref, out_ref, start, copied)
        copy.start()
        copy.wait()


def early_piece(across, weight, start, piece, after):
    return call(
        functools.partial(early_kernel, across, start),
        jax.ShapeDtypeStruct((piece, weight.shape[1]), weight.dtype),
        in_specs=[anywhere] * 2,
        scratch_shapes=[pltpu.SemaphoreType.DMA(())],
        limit=big_limit,
    )(weight, after)


def first_kernel(across, own_flags_ref, *refs):
    queries, refs = refs[:across], refs[across:]
    kv_ref, weight_ref, turned_ref, flags_ref, weight_out = refs[:5]
    state, copied = refs[5:8], refs[8]
    weight_copy = weight_piece(weight_ref, weight_out, 0, copied)
    weight_copy.start()
    z, y = place(across)
    q_rows = kv_ref.shape[1]
    repeat = queries[0].shape[1] // HD
    columns = repeat * q_rows
    for e in range(across):
        for r in range(repeat):
            turned_ref[e, :, r * q_rows : (r + 1) * q_rows] = queries[e][
                0:q_rows, r * HD : (r + 1) * HD
            ].T
    flags_ref[0] = own_flags_ref[...]
    for e in range(1, across):
        flags_ref[e] = queries[e][q_rows:, 0:HD].astype(jnp.float32)
    owners = [block_at(z, y, e, across) for e in range(across)]
    switches = [
        [
            None if e == b else switch_of(flags_ref, e, owners[b], columns, owners[b] < owners[e])
            for b in range(across)
        ]
        for e in range(across)
    ]
    rows_update(turned_ref, [kv_ref], switches, state, True)

    weight_copy.wait()


def attend_first(across, flags, queries, rows, weight, piece):
    q_rows = rows.shape[1]
    repeat = queries[0].shape[1] // HD
    columns = repeat * q_rows
    f32, b16 = jnp.float32, jnp.bfloat16
    return call(
        functools.partial(first_kernel, across),
        [
            jax.ShapeDtypeStruct((across, HD, columns), b16),
            jax.ShapeDtypeStruct((across,) + flags.shape, f32),
            jax.ShapeDtypeStruct((piece, weight.shape[1]), weight.dtype),
            jax.ShapeDtypeStruct((across, 1, columns), f32),
            jax.ShapeDtypeStruct((across, 1, columns), f32),
            jax.ShapeDtypeStruct((across, HD, columns), f32),
        ],
        in_specs=[in_vmem] * (across + 2) + [anywhere],
        scratch_shapes=[pltpu.SemaphoreType.DMA(())],
        limit=big_limit,
    )(flags, *queries, rows, weight)


def next_kernel(across, distances, turns, last, weight_at, early_at, flags_ref, turned_ref, *refs):
    below_count = len(distances)
    below, state, refs = refs[:below_count], refs[below_count : below_count + 3], refs[below_count + 3 :]
    if weight_at is not None:
        weight_ref, weight_out, copied = refs[0], refs[-2], refs[-1]
        refs = refs[1:-2]
        weight_copy = weight_piece(weight_ref, weight_out, weight_at, copied)
        weight_copy.start()
    z, y = place(across)
    if early_at is not None:
        weight_ref, early_out, copied = refs[1], refs[-2], refs[-1]

        @pl.when(z != 0)
        def _():
            weight_piece(weight_ref, early_out, early_at, copied).start()

    columns = turned_ref.shape[2]

    def update(rows, from_distances):
        switches = [
            [
                switch_of(flags_ref, e, block_at(z - distance, y, b, across), columns)
                for distance in from_distances
                for b in range(across)
            ]
            for e in range(across)
        ]
        rows_update(turned_ref, rows, switches, state, False)

    for number, distance in enumerate(distances, 1):
        here = (z >= distance) if number == len(distances) else (z == distance)
        pl.when(here)(functools.partial(update, below[:number], distances[:number]))

    if weight_at is not None:
        weight_copy.wait()
    if early_at is not None:

        @pl.when(z != 0)
        def _():
            weight_piece(weight_ref, early_out, early_at, copied).wait()

    if last:
        member_ref, inverse_ref, out_ref = refs
        rows = out_ref.shape[1]
        pooled = None
        for e in range(across):
            attended = (state[2][e] / state[1][e]).astype(jnp.bfloat16)
            part = lax.dot_general(
                member_ref[e],
                attended,
                (((1,), (1,)), ((), ())),
                preferred_element_type=jnp.float32,
            )
            pooled = part if pooled is None else pooled + part
        for r in range(pooled.shape[0] // turns):
            mean = pooled[r * turns : (r + 1) * turns] * inverse_ref[...]
            for s in range(out_ref.shape[0]):
                out_ref[s, :, r * HD : (r + 1) * HD] = mean[s * rows : (s + 1) * rows]


def attend_next(across, distances, turns, turned, flags, below, state, pool, out_piece, weight, at, piece, early=None):
    last = pool is not None
    args = [flags, turned, *below, *state]
    in_specs = [in_vmem] * len(args)
    aliases, scratch = {}, []
    if at is not None:
        args.append(weight)
        in_specs.append(anywhere)
        scratch = [pltpu.SemaphoreType.DMA(())]
    if early is not None:
        early_at = weight.shape[0] - early.shape[0]
        early_aliases = {len(args): len(state)}
        args += [early, weight]
        in_specs += [in_vmem, anywhere]
        scratch = [pltpu.SemaphoreType.DMA(())]
    else:
        early_at, early_aliases = None, {}
    if last:
        args += list(pool)
        in_specs += [in_vmem] * len(pool)
        out_shape = [jax.ShapeDtypeStruct(out_piece, jnp.float32)]
    else:
        out_shape = [jax.ShapeDtypeStruct(part.shape, part.dtype) for part in state]
        aliases = {2 + len(below) + i: i for i in range(len(state))}
    if at is not None:
        out_shape.append(jax.ShapeDtypeStruct((piece, weight.shape[1]), weight.dtype))
    if early is not None:
        out_shape.append(jax.ShapeDtypeStruct(early.shape, early.dtype))
        aliases.update(early_aliases)
    return call(
        functools.partial(next_kernel, across, distances, turns, last, at, early_at),
        out_shape,
        in_specs=in_specs,
        scratch_shapes=scratch,
        input_output_aliases=aliases,
        limit=big_limit if scratch else 16 * 1024 * 1024,
    )(*args)


def project_kernel(across, other, parts_ref, *refs):
    weights, out_ref = refs[:-1], refs[-1]
    side = lax.axis_index("head")
    if other:
        side = 1 - side
    groups = []
    for y in range(across):
        total = parts_ref[y]
        for s in range(y + across, parts_ref.shape[0], across):
            total = total + parts_ref[s]
        groups.append(total)
    total = jnp.concatenate(groups, axis=1)
    rows = total.shape[0]
    high = total.astype(jnp.bfloat16)
    low = (total - high.astype(jnp.float32)).astype(jnp.bfloat16)
    both = jnp.concatenate([high, low], axis=0)
    half = out_ref.shape[1]
    step = math.gcd(half, 512)
    for c in range(half // step):
        start = pl.multiple_of(side * half + c * step, step)
        product, at = None, 0
        for weight_ref in weights:
            depth = weight_ref.shape[0]
            part = jnp.dot(
                both[:, at : at + depth],
                weight_ref[:, pl.ds(start, step)],
                preferred_element_type=jnp.float32,
            )
            product = part if product is None else product + part
            at += depth
        out_ref[:, c * step : (c + 1) * step] = product[:rows] + product[rows:]


def project(across, other, parts, weights):
    return call(
        functools.partial(project_kernel, across, other),
        jax.ShapeDtypeStruct((parts.shape[1], weights[0].shape[1] // 2), jnp.float32),
        in_specs=[in_vmem] * (1 + len(weights)),
    )(parts, *weights)


def on_device(count, queries, key_states, value_states, out_weight, turn_lengths, block_flags):
    across = key_states.shape[1] // HD
    down = count // across
    turns = turn_lengths.shape[0]

    def over(rows, shift):
        pairs = [(i, i - i % across + (i + shift) % across) for i in range(count)]
        return lax.ppermute(rows, "seq", pairs)

    def up(rows, distance, lowest=0):
        step = distance * across
        pairs = [(i, i + step) for i in range(lowest * across, count - step)]
        return lax.ppermute(rows, "seq", pairs)

    _, y = place(across)
    heads = []
    for shift in range(across):
        at = lax.rem(y + shift, across)
        heads.append(pair(pick(key_states, at, across), pick(value_states, at, across)))
    swapped = [over(heads[shift], shift) for shift in range(1, across)]
    rows = join([heads[0]] + swapped)
    first = up(heads[0], 1)
    rest = up(join(swapped), 1)
    rows, queries = lax.optimization_barrier((rows, queries))
    meta = lax.optimization_barrier(jnp.concatenate([turn_lengths, block_flags[0]]))
    padded = -(-count // 16) * 16
    flags = jnp.pad(meta[turns:], (0, padded - count))[:, None]
    groups = [pick(queries, lax.rem(y + shift, across), across) for shift in range(across)]
    sent = []
    for group in groups[1:]:
        under = jnp.broadcast_to(flags, (padded, group.shape[1])).astype(group.dtype)
        sent.append(jnp.concatenate([group, under], axis=0))
    flags = jnp.broadcast_to(flags, (padded, HD)).astype(jnp.float32)
    below = [rows, join_parts([first, rest], 2 * across)] + [None] * (down - 2)
    early = early_piece(
        across, out_weight, out_weight.shape[0] * 3 // 4, out_weight.shape[0] // 4, groups[0]
    )
    far, early = lax.optimization_barrier((rows, early))
    early, *sent = lax.optimization_barrier((early, *sent))
    others = [over(group, shift) for shift, group in enumerate(sent, 1)]
    for distance in range(3, down):
        below[distance] = up(far, distance)
    if down > 2:
        below[2] = up(below[1], 1, 1)
    member, inverse = members(across, turns, meta, groups[0])
    inverse, flags = lax.optimization_barrier((inverse, flags))
    depth = out_weight.shape[0]
    pieces = [4 * depth // 8, 2 * depth // 8]
    turned, flags, weight, *state = attend_first(
        across, flags, [groups[0], *others], rows, out_weight, pieces[0]
    )
    weights = [weight]
    out_piece = (count, turns // count, queries.shape[1] // across)
    stages = [[1]] + [list(range(d, min(d + 2, down))) for d in range(3, down, 2)] + [[2]]
    for number, distances in enumerate(stages):
        last = number == len(stages) - 1
        with_weight = number == 0
        state = attend_next(
            across,
            distances,
            turns,
            turned,
            flags,
            [below[distance] for distance in distances],
            state,
            (member, inverse) if last else None,
            out_piece,
            out_weight,
            sum(pieces[: len(weights)]) if with_weight else None,
            pieces[len(weights)] if with_weight else None,
            early if number == 1 else None,
        )
        if with_weight or number == 1:
            *state, weight = state
            weights.append(weight)
    parts = lax.all_to_all(state[0], "seq", split_axis=0, concat_axis=0, tiled=True)
    theirs = project(across, True, parts, weights)
    theirs = lax.ppermute(theirs, "head", [(0, 1), (1, 0)])
    return project(across, False, parts, weights) + theirs


def solution(mesh):
    in_specs = (
        P(("conv", "seq"), "head"),
        P(("conv", "seq"), "head"),
        P(("conv", "seq"), "head"),
        P("head", None),
        P("conv"),
        P(("conv", "seq"), None),
    )
    out_specs = P(("conv", "seq"), "head")
    return jax.shard_map(
        functools.partial(on_device, mesh.shape["seq"]),
        mesh=mesh,
        in_specs=in_specs,
        out_specs=out_specs,
        check_vma=False,
    )
```

```python
import functools
import math

import jax
import jax.numpy as jnp
from jax import lax
from jax.experimental import pallas as pl
from jax.experimental.pallas import tpu as pltpu
from jax.sharding import PartitionSpec as P

HD = 128

big_negative = -1e30
log_two_e = 1.4426950408889634

big_limit = 45 * 1024 * 1024
long_flops = 4 * 10**9

in_vmem = pl.BlockSpec(memory_space=pltpu.VMEM)
in_smem = pl.BlockSpec(memory_space=pltpu.SMEM)
anywhere = pl.BlockSpec(memory_space=pl.ANY)


def place(across):
    index = lax.axis_index("seq")
    return index // across, lax.rem(index, across)


def block_at(z, y, e, across):
    return z * across + lax.rem(y - e + across, across)


def call(kernel, out_shape, **settings):
    limit = settings.pop("limit", 16 * 1024 * 1024)
    flops = settings.pop("flops", 0)
    return pl.pallas_call(
        kernel,
        out_shape=out_shape,
        out_specs=jax.tree.map(lambda _: in_vmem, out_shape),
        compiler_params=pltpu.CompilerParams(vmem_limit_bytes=limit),
        cost_estimate=pl.CostEstimate(flops=flops, bytes_accessed=1024, transcendentals=0),
        **settings,
    )


def pick(rows, number, parts):
    width = rows.shape[1] // parts
    picked = rows[:, :width]
    for part in range(1, parts):
        picked = jnp.where(number == part, rows[:, part * width : (part + 1) * width], picked)
    return picked


def pair(keys, values):
    which = lax.broadcasted_iota(jnp.int32, (2,) + keys.shape, 0)
    return jnp.where(which == 0, keys[None], values[None])


def join_kernel(*refs):
    *parts, out_ref = refs
    at = 0
    for part in parts:
        size = min(part.shape[0], out_ref.shape[0] - at)
        out_ref[at : at + size] = part[:size]
        at += size


def join_parts(parts, count):
    return join(parts, count)


def join(parts, count=None):
    count = sum(part.shape[0] for part in parts) if count is None else count
    shape = jax.ShapeDtypeStruct((count,) + parts[0].shape[1:], parts[0].dtype)
    return call(join_kernel, shape, in_specs=[in_vmem] * len(parts))(*parts)


def rows_update(turned_ref, rows_refs, switches, state, first):
    top, total_sum, totals = state
    across, _, columns = turned_ref.shape
    rows = rows_refs[0].shape[1]
    count = across * len(rows_refs)
    factor = log_two_e / math.sqrt(HD)
    keys = [
        jnp.concatenate([kv_ref[2 * e] for e in range(across)], axis=0) for kv_ref in rows_refs
    ]
    values = [
        jnp.concatenate([kv_ref[2 * e + 1] for e in range(across)], axis=0).T for kv_ref in rows_refs
    ]
    span = columns // 2 if columns % 256 == 0 else columns
    pieces = [(e, slice(at, at + span)) for e in range(across) for at in range(0, columns, span)]
    logits = [
        [jnp.dot(part, turned_ref[e, :, cut], preferred_element_type=jnp.float32) for part in keys]
        for e, cut in pieces
    ]
    for number, (e, cut) in enumerate(pieces):
        blocks = [
            logits[number][b // across][b % across * rows : (b % across + 1) * rows]
            for b in range(count)
        ]
        on = [None if switch is None else switch[:, cut] for switch in switches[e]]
        if first:
            key_pos = lax.broadcasted_iota(jnp.int32, (rows, 1), 0)
            column = cut.start + lax.broadcasted_iota(jnp.int32, (1, span), 1)
            blocks[e] = jnp.where(key_pos <= lax.rem(column, rows), blocks[e], big_negative)
        new_top = None if first else top[e, :, cut]
        for b in range(count):
            block_top = jnp.ceil(jnp.max(blocks[b], axis=0, keepdims=True) * factor)
            if on[b] is not None:
                block_top = jnp.where(on[b], block_top, big_negative)
            new_top = block_top if new_top is None else jnp.maximum(new_top, block_top)
        weights, block_sum = [], None
        for b in range(count):
            against = new_top
            if on[b] is not None:
                against = jnp.where(on[b], new_top, -big_negative)
            weights.append(jnp.exp2(blocks[b] * factor - against))
            part = jnp.sum(weights[b], axis=0, keepdims=True)
            block_sum = part if block_sum is None else block_sum + part
        update = None
        for i, part in enumerate(values):
            mine = weights[i * across : (i + 1) * across]
            mine = jnp.concatenate([w.astype(jnp.bfloat16) for w in mine], axis=0)
            part = jnp.dot(part, mine, preferred_element_type=jnp.float32)
            update = part if update is None else update + part
        if not first:
            rescale = jnp.exp2(top[e, :, cut] - new_top)
            block_sum = total_sum[e, :, cut] * rescale + block_sum
            update = totals[e, :, cut] * rescale + update
        top[e, :, cut] = new_top
        total_sum[e, :, cut] = block_sum
        totals[e, :, cut] = update


def switch_of(flags_ref, e, owner, columns, allowed=None):
    flag = flags_ref[e, pl.ds(jnp.maximum(owner, 0), 1), :]
    if allowed is not None:
        flag = flag * jnp.where(allowed, 1.0, 0.0)
    return jnp.concatenate([flag] * (columns // HD), axis=1) > 0.5


def member_kernel(across, turns, meta_ref, after_ref, member_ref, inverse_ref, rows_ref):
    del after_ref
    z, y = place(across)
    columns = rows_ref.shape[1]
    repeat = member_ref.shape[1] // turns
    q_rows = columns // repeat
    owners = [block_at(z, y, e, across) for e in range(across)]
    column = lax.broadcasted_iota(jnp.int32, (1, columns), 1)
    for e in range(across):
        position = lax.rem(column, q_rows) + owners[e] * q_rows
        start = jnp.int32(0)
        for t in range(turns):
            length = meta_ref[t]
            inside = (position >= start) & (position < start + length)
            rows_ref[t : t + 1, :] = jnp.where(inside, 1.0, 0.0)
            if e == 0:
                count = jnp.full((1, HD), length, jnp.int32).astype(jnp.float32)
                inverse_ref[t : t + 1, :] = 1.0 / count
            start = start + length
        for r in range(repeat):
            mine = (column >= r * q_rows) & (column < (r + 1) * q_rows)
            member_ref[e, r * turns : (r + 1) * turns, :] = jnp.where(
                mine, rows_ref[...], 0.0
            ).astype(jnp.bfloat16)


def members(across, turns, meta, group):
    q_rows, width = group.shape
    repeat = width // HD
    columns = repeat * q_rows
    return call(
        functools.partial(member_kernel, across, turns),
        [
            jax.ShapeDtypeStruct((across, repeat * turns, columns), jnp.bfloat16),
            jax.ShapeDtypeStruct((turns, HD), jnp.float32),
        ],
        in_specs=[in_smem, anywhere],
        scratch_shapes=[pltpu.VMEM((turns, columns), jnp.float32)],
        flops=long_flops,
    )(meta, group)


def weight_piece(weight_ref, out_ref, start, sem):
    return pltpu.make_async_copy(weight_ref.at[start : start + out_ref.shape[0]], out_ref, sem)


def early_kernel(across, start, weight_ref, _, out_ref, copied):
    z, _ = place(across)

    @pl.when(z == 0)
    def _():
        copy = weight_piece(weight_ref, out_ref, start, copied)
        copy.start()
        copy.wait()


def early_piece(across, weight, start, piece, after):
    return call(
        functools.partial(early_kernel, across, start),
        jax.ShapeDtypeStruct((piece, weight.shape[1]), weight.dtype),
        in_specs=[anywhere] * 2,
        scratch_shapes=[pltpu.SemaphoreType.DMA(())],
        limit=big_limit,
    )(weight, after)


def first_kernel(across, own_flags_ref, *refs):
    queries, refs = refs[:across], refs[across:]
    kv_ref, weight_ref, turned_ref, flags_ref, weight_out = refs[:5]
    state, copied = refs[5:8], refs[8]
    weight_copy = weight_piece(weight_ref, weight_out, 0, copied)
    weight_copy.start()
    z, y = place(across)
    q_rows = kv_ref.shape[1]
    repeat = queries[0].shape[1] // HD
    columns = repeat * q_rows
    for e in range(across):
        for r in range(repeat):
            turned_ref[e, :, r * q_rows : (r + 1) * q_rows] = queries[e][
                0:q_rows, r * HD : (r + 1) * HD
            ].T
    flags_ref[0] = own_flags_ref[...]
    for e in range(1, across):
        flags_ref[e] = queries[e][q_rows:, 0:HD].astype(jnp.float32)
    owners = [block_at(z, y, e, across) for e in range(across)]
    switches = [
        [
            None if e == b else switch_of(flags_ref, e, owners[b], columns, owners[b] < owners[e])
            for b in range(across)
        ]
        for e in range(across)
    ]
    rows_update(turned_ref, [kv_ref], switches, state, True)

    weight_copy.wait()


def attend_first(across, flags, queries, rows, weight, piece):
    q_rows = rows.shape[1]
    repeat = queries[0].shape[1] // HD
    columns = repeat * q_rows
    f32, b16 = jnp.float32, jnp.bfloat16
    return call(
        functools.partial(first_kernel, across),
        [
            jax.ShapeDtypeStruct((across, HD, columns), b16),
            jax.ShapeDtypeStruct((across,) + flags.shape, f32),
            jax.ShapeDtypeStruct((piece, weight.shape[1]), weight.dtype),
            jax.ShapeDtypeStruct((across, 1, columns), f32),
            jax.ShapeDtypeStruct((across, 1, columns), f32),
            jax.ShapeDtypeStruct((across, HD, columns), f32),
        ],
        in_specs=[in_vmem] * (across + 2) + [anywhere],
        scratch_shapes=[pltpu.SemaphoreType.DMA(())],
        limit=big_limit,
    )(flags, *queries, rows, weight)


def next_kernel(across, distances, turns, last, weight_at, early_at, flags_ref, turned_ref, *refs):
    below_count = len(distances)
    below, state, refs = refs[:below_count], refs[below_count : below_count + 3], refs[below_count + 3 :]
    if weight_at is not None:
        weight_ref, weight_out, copied = refs[0], refs[-2], refs[-1]
        refs = refs[1:-2]
        weight_copy = weight_piece(weight_ref, weight_out, weight_at, copied)
        weight_copy.start()
    z, y = place(across)
    if early_at is not None:
        weight_ref, early_out, copied = refs[1], refs[-2], refs[-1]

        @pl.when(z != 0)
        def _():
            weight_piece(weight_ref, early_out, early_at, copied).start()

    columns = turned_ref.shape[2]

    def update(rows, from_distances):
        switches = [
            [
                switch_of(flags_ref, e, block_at(z - distance, y, b, across), columns)
                for distance in from_distances
                for b in range(across)
            ]
            for e in range(across)
        ]
        rows_update(turned_ref, rows, switches, state, False)

    for number, distance in enumerate(distances, 1):
        here = (z >= distance) if number == len(distances) else (z == distance)
        pl.when(here)(functools.partial(update, below[:number], distances[:number]))

    if weight_at is not None:
        weight_copy.wait()
    if early_at is not None:

        @pl.when(z != 0)
        def _():
            weight_piece(weight_ref, early_out, early_at, copied).wait()

    if last:
        member_ref, inverse_ref, out_ref = refs
        rows = out_ref.shape[1]
        pooled = None
        for e in range(across):
            attended = (state[2][e] / state[1][e]).astype(jnp.bfloat16)
            part = lax.dot_general(
                member_ref[e],
                attended,
                (((1,), (1,)), ((), ())),
                preferred_element_type=jnp.float32,
            )
            pooled = part if pooled is None else pooled + part
        for r in range(pooled.shape[0] // turns):
            mean = pooled[r * turns : (r + 1) * turns] * inverse_ref[...]
            for s in range(out_ref.shape[0]):
                out_ref[s, :, r * HD : (r + 1) * HD] = mean[s * rows : (s + 1) * rows]


def attend_next(across, distances, turns, turned, flags, below, state, pool, out_piece, weight, at, piece, early=None):
    last = pool is not None
    args = [flags, turned, *below, *state]
    in_specs = [in_vmem] * len(args)
    aliases, scratch = {}, []
    if at is not None:
        args.append(weight)
        in_specs.append(anywhere)
        scratch = [pltpu.SemaphoreType.DMA(())]
    if early is not None:
        early_at = weight.shape[0] - early.shape[0]
        early_aliases = {len(args): len(state)}
        args += [early, weight]
        in_specs += [in_vmem, anywhere]
        scratch = [pltpu.SemaphoreType.DMA(())]
    else:
        early_at, early_aliases = None, {}
    if last:
        args += list(pool)
        in_specs += [in_vmem] * len(pool)
        out_shape = [jax.ShapeDtypeStruct(out_piece, jnp.float32)]
    else:
        out_shape = [jax.ShapeDtypeStruct(part.shape, part.dtype) for part in state]
        aliases = {2 + len(below) + i: i for i in range(len(state))}
    if at is not None:
        out_shape.append(jax.ShapeDtypeStruct((piece, weight.shape[1]), weight.dtype))
    if early is not None:
        out_shape.append(jax.ShapeDtypeStruct(early.shape, early.dtype))
        aliases.update(early_aliases)
    return call(
        functools.partial(next_kernel, across, distances, turns, last, at, early_at),
        out_shape,
        in_specs=in_specs,
        scratch_shapes=scratch,
        input_output_aliases=aliases,
        limit=big_limit if scratch else 16 * 1024 * 1024,
    )(*args)


def project_kernel(across, other, parts_ref, *refs):
    weights, out_ref = refs[:-1], refs[-1]
    side = lax.axis_index("head")
    if other:
        side = 1 - side
    groups = []
    for y in range(across):
        total = parts_ref[y]
        for s in range(y + across, parts_ref.shape[0], across):
            total = total + parts_ref[s]
        groups.append(total)
    total = jnp.concatenate(groups, axis=1)
    rows = total.shape[0]
    high = total.astype(jnp.bfloat16)
    low = (total - high.astype(jnp.float32)).astype(jnp.bfloat16)
    both = jnp.concatenate([high, low], axis=0)
    half = out_ref.shape[1]
    step = math.gcd(half, 512)
    for c in range(half // step):
        start = pl.multiple_of(side * half + c * step, step)
        product, at = None, 0
        for weight_ref in weights:
            depth = weight_ref.shape[0]
            part = jnp.dot(
                both[:, at : at + depth],
                weight_ref[:, pl.ds(start, step)],
                preferred_element_type=jnp.float32,
            )
            product = part if product is None else product + part
            at += depth
        out_ref[:, c * step : (c + 1) * step] = product[:rows] + product[rows:]


def project(across, other, parts, weights):
    return call(
        functools.partial(project_kernel, across, other),
        jax.ShapeDtypeStruct((parts.shape[1], weights[0].shape[1] // 2), jnp.float32),
        in_specs=[in_vmem] * (1 + len(weights)),
    )(parts, *weights)


def on_device(count, queries, key_states, value_states, out_weight, turn_lengths, block_flags):
    across = key_states.shape[1] // HD
    down = count // across
    turns = turn_lengths.shape[0]

    def over(rows, shift):
        pairs = [(i, i - i % across + (i + shift) % across) for i in range(count)]
        return lax.ppermute(rows, "seq", pairs)

    def up(rows, distance, lowest=0):
        step = distance * across
        pairs = [(i, i + step) for i in range(lowest * across, count - step)]
        return lax.ppermute(rows, "seq", pairs)

    _, y = place(across)
    heads = []
    for shift in range(across):
        at = lax.rem(y + shift, across)
        heads.append(pair(pick(key_states, at, across), pick(value_states, at, across)))
    swapped = [over(heads[shift], shift) for shift in range(1, across)]
    rows = join([heads[0]] + swapped)
    first = up(heads[0], 1)
    rest = up(join(swapped), 1)
    rows, queries = lax.optimization_barrier((rows, queries))
    meta = lax.optimization_barrier(jnp.concatenate([turn_lengths, block_flags[0]]))
    padded = -(-count // 16) * 16
    flags = jnp.pad(meta[turns:], (0, padded - count))[:, None]
    groups = [pick(queries, lax.rem(y + shift, across), across) for shift in range(across)]
    sent = []
    for group in groups[1:]:
        under = jnp.broadcast_to(flags, (padded, group.shape[1])).astype(group.dtype)
        sent.append(jnp.concatenate([group, under], axis=0))
    flags = jnp.broadcast_to(flags, (padded, HD)).astype(jnp.float32)
    below = [rows, join_parts([first, rest], 2 * across)] + [None] * (down - 2)
    early = early_piece(across, out_weight, out_weight.shape[0] - out_weight.shape[0] // 8, out_weight.shape[0] // 8, groups[0])
    far, early = lax.optimization_barrier((rows, early))
    early, *sent = lax.optimization_barrier((early, *sent))
    others = [over(group, shift) for shift, group in enumerate(sent, 1)]
    for distance in range(3, down):
        below[distance] = up(far, distance)
    if down > 2:
        below[2] = up(below[1], 1, 1)
    member, inverse = members(across, turns, meta, groups[0])
    inverse, flags = lax.optimization_barrier((inverse, flags))
    depth = out_weight.shape[0]
    pieces = [5 * depth // 8, 2 * depth // 8, depth // 8]
    turned, flags, weight, *state = attend_first(
        across, flags, [groups[0], *others], rows, out_weight, pieces[0]
    )
    weights = [weight]
    out_piece = (count, turns // count, queries.shape[1] // across)
    stages = [[1]] + [list(range(d, min(d + 2, down))) for d in range(3, down, 2)] + [[2]]
    for number, distances in enumerate(stages):
        last = number == len(stages) - 1
        with_weight = number == 0
        state = attend_next(
            across,
            distances,
            turns,
            turned,
            flags,
            [below[distance] for distance in distances],
            state,
            (member, inverse) if last else None,
            out_piece,
            out_weight,
            sum(pieces[: len(weights)]) if with_weight else None,
            pieces[len(weights)] if with_weight else None,
            early if number == 1 else None,
        )
        if with_weight or number == 1:
            *state, weight = state
            weights.append(weight)
    parts = lax.all_to_all(state[0], "seq", split_axis=0, concat_axis=0, tiled=True)
    theirs = project(across, True, parts, weights)
    theirs = lax.ppermute(theirs, "head", [(0, 1), (1, 0)])
    return project(across, False, parts, weights) + theirs


def solution(mesh):
    in_specs = (
        P(("conv", "seq"), "head"),
        P(("conv", "seq"), "head"),
        P(("conv", "seq"), "head"),
        P("head", None),
        P("conv"),
        P(("conv", "seq"), None),
    )
    out_specs = P(("conv", "seq"), "head")
    return jax.shard_map(
        functools.partial(on_device, mesh.shape["seq"]),
        mesh=mesh,
        in_specs=in_specs,
        out_specs=out_specs,
        check_vma=False,
    )
```
